32 devices in a mesh: batch: 4 (over y, x), blk: 8 (over z, core).
Axes of the slice: x: 2, y: 2, z: 4, core: 2. Of those that a mesh axis runs over, the one named last changes fastest.
Arguments:
- tokens: bfloat16 [32, 1024, 1024], P('batch', 'blk'), may hold values from -6 to 6
- lengths: int32 [32], P('batch'), may hold values from 64 to 1024, as said below
- norm_gain: bfloat16 [1024], replicated, may hold values from 0.5 to 1.5
- norm_shift: bfloat16 [1024], replicated, may hold values from -1.25 to 1.25
- joint_weight: bfloat16 [1024, 3072], replicated, may hold values from -0.1875 to 0.1875
- query_bias: bfloat16 [1024], replicated, may hold values from -1.25 to 1.25
- value_bias: bfloat16 [1024], replicated, may hold values from -1.25 to 1.25
- output_weight: bfloat16 [1024, 1024], replicated, may hold values from -0.75 to 0.75
- output_bias: bfloat16 [1024], replicated, may hold values from -1.25 to 1.25
- second_gain: bfloat16 [1024], replicated, may hold values from 0.5 to 1.5
- second_shift: bfloat16 [1024], replicated, may hold values from -1.25 to 1.25
- upward_weight: bfloat16 [1024, 4096], replicated, may hold values from -0.1875 to 0.1875
- upward_bias: bfloat16 [4096], replicated, may hold values from -1.25 to 1.25
- down_weight: bfloat16 [4096, 1024], replicated, may hold values from -0.09375 to 0.09375
- down_bias: bfloat16 [1024], replicated, may hold values from -1.25 to 1.25
- query_down: bfloat16 [1024, 4], replicated, may hold values from -0.1875 to 0.1875
- query_up: bfloat16 [4, 1024], replicated, may hold values from -0.1875 to 0.1875
- value_down: bfloat16 [1024, 4], replicated, may hold values from -0.1875 to 0.1875
- value_up: bfloat16 [4, 1024], replicated, may hold values from -0.1875 to 0.1875
- cotangent: bfloat16 [32, 1024, 1024], P('batch', 'blk'), may hold values from -6 to 6
Outputs:
- block_output: bfloat16 [32, 1024, 1024], P('batch', 'blk')
- token_grads: float32 [32, 1024, 1024], P('batch', 'blk')
- query_down_grad: float32 [1024, 4], replicated
- query_up_grad: float32 [4, 1024], replicated
- value_down_grad: float32 [1024, 4], replicated
- value_up_grad: float32 [4, 1024], replicated
The draws below stay inside these ranges and needn't reach their ends.
Inputs may be any that keep to these rules, and one draw needn't show every extreme that they name: `lengths`: in each group of 8 slots of one index of batch, one slot drawn from the seed has length 1024.
All inputs are finite; a program needn't handle non-finite values.
Results may differ from the reference program's by a relative error of at most 0.015.
Values may be sent and summed in bfloat16 or wider, within the bound.
No kernel may reach another device: no remote copies, remote signals or barrier semaphores. Data moves between devices by JAX's collectives and lax.ppermute only.
A program may use at most 320 MiB of HBM per device.

```python
import jax
import jax.numpy as jnp
from jax import lax

D = 1024
H = 16
HD = 64
FF = 4096
RANK = 4
LEN = 1024
MIN_LEN = 64
SEQS = 8
SEQS_ALL = 32


def draw_lengths(key, part):
    key = jax.random.fold_in(key, 11)
    lead_key, slot_key = jax.random.split(key)
    drawn_lengths = jax.random.randint(lead_key, (SEQS_ALL,), MIN_LEN, LEN + 1)
    groups = SEQS_ALL // SEQS
    chosen = jax.random.randint(slot_key, (groups,), 0, SEQS)
    longest = (jnp.arange(SEQS)[None, :] == chosen[:, None]).reshape(SEQS_ALL)
    return jnp.where(longest, LEN, drawn_lengths).astype(jnp.int32)


def block_levels(stream_key, dims, pieces, low, high):
    loudness, own = 1.0, jax.random.fold_in(stream_key, 6)
    for dim, shards_of in pieces:
        heights = jnp.exp(jax.random.uniform(jax.random.fold_in(own, dim), (shards_of,), jnp.float32, low / len(pieces), high / len(pieces)))
        loudness = loudness * jnp.repeat(heights, dims[dim] // shards_of).reshape([-1 if axis == dim else 1 for axis in range(len(dims))])
    return loudness


def noise(rng, extent, scale, limit, pieces=(), held_as=jnp.bfloat16):
    drawn = jax.random.normal(rng, extent, jnp.float32) * scale
    if len(pieces) > 0:
        drawn = block_levels(rng, extent, pieces, -0.22, 0.18) * drawn
    return jnp.clip(drawn, min=-limit, max=limit).astype(held_as)


def setup_inputs(seed: int = 0) -> dict:
    streams_of = jax.random.split(jax.random.key(seed), 21)
    tokens = noise(streams_of[0], (SEQS_ALL, LEN, D), 1.0, 6.0, ((0, 4), (1, 8)))
    lengths = draw_lengths(jax.random.fold_in(streams_of[20], 71), 0)
    norm_gain = jnp.clip(1.0 + 0.1 * jax.random.normal(streams_of[2], (D,), jnp.float32), 0.5, 1.5).astype(jnp.bfloat16)
    norm_shift = noise(streams_of[3], (D,), 0.2, 1.25)
    joint_weight = noise(streams_of[4], (D, 3 * D), D ** -0.5, 0.1875)
    query_bias = noise(streams_of[5], (D,), 0.2, 1.25)
    value_bias = noise(streams_of[6], (D,), 0.2, 1.25)
    output_weight = noise(streams_of[7], (D, D), (D // 16) ** -0.5, 0.75)
    output_bias = noise(streams_of[8], (D,), 0.2, 1.25)
    second_gain = jnp.clip(1.0 + 0.1 * jax.random.normal(streams_of[9], (D,), jnp.float32), 0.5, 1.5).astype(jnp.bfloat16)
    second_shift = noise(streams_of[10], (D,), 0.2, 1.25)
    upward_weight = noise(streams_of[11], (D, FF), D ** -0.5, 0.1875)
    upward_bias = noise(streams_of[12], (FF,), 0.2, 1.25)
    down_weight = noise(streams_of[13], (FF, D), FF ** -0.5, 0.09375)
    down_bias = noise(streams_of[14], (D,), 0.2, 1.25)
    query_down = noise(streams_of[15], (D, RANK), D ** -0.5, 0.1875)
    query_up = noise(streams_of[16], (RANK, D), 0.03, 0.1875)
    value_down = noise(streams_of[17], (D, RANK), D ** -0.5, 0.1875)
    value_up = noise(streams_of[18], (RANK, D), 0.03, 0.1875)
    cotangent = noise(streams_of[19], (SEQS_ALL, LEN, D), 1.0, 6.0, ((0, 4), (1, 8)))
    return {"tokens": tokens, "lengths": lengths, "norm_gain": norm_gain, "norm_shift": norm_shift, "joint_weight": joint_weight, "query_bias": query_bias, "value_bias": value_bias, "output_weight": output_weight, "output_bias": output_bias, "second_gain": second_gain, "second_shift": second_shift, "upward_weight": upward_weight, "upward_bias": upward_bias, "down_weight": down_weight, "down_bias": down_bias, "query_down": query_down, "query_up": query_up, "value_down": value_down, "value_up": value_up, "cotangent": cotangent}


@jax.custom_vjp
def low(v):
    return lax.optimization_barrier(v.astype(jnp.bfloat16)).astype(jnp.float32)

@jax.custom_vjp
def low_back(v):
    return v

def low_keep(v):
    return (low(v), None)

def low_pass(kept, grad):
    return (grad,)

def back_keep(v):
    return (v, None)

def back_low(kept, grad):
    return (low(grad),)
low.defvjp(low_keep, low_pass)
low_back.defvjp(back_keep, back_low)
epsilon = 1e-05
masked_value = -1e+30

def product(left, right):
    return jnp.dot(left, right, precision=lax.Precision.HIGHEST)

def layer_norm(values, gain, shift):
    centred = values - lax.optimization_barrier(jnp.mean(values, axis=-1, keepdims=True))
    variance = lax.optimization_barrier(jnp.mean(centred * centred, axis=-1, keepdims=True))
    return centred * lax.rsqrt(variance + epsilon) * gain + shift

def sequence_block(seq_input, query_down, query_up, value_down, value_up, length, frozen):
    norm_gain, norm_shift, joint_weight, query_bias, value_bias, output_weight, output_bias, second_gain, second_shift, upward_weight, upward_bias, down_weight, down_bias = frozen
    count, width = seq_input.shape
    adapter = 32.0 / RANK
    normed = low(layer_norm(seq_input, norm_gain, norm_shift))
    joint = product(normed, joint_weight)
    query_low = low_back(low(product(normed, query_down)))
    value_low = low_back(low(product(normed, value_down)))
    queries = low_back(low(joint[:, :width] + query_bias + adapter * product(query_low, query_up)))
    keys_all = low_back(low(joint[:, width:2 * width]))
    values_all = low_back(low(joint[:, 2 * width:] + value_bias + adapter * product(value_low, value_up)))
    query_heads = queries.reshape(count, H, HD)
    key_heads = keys_all.reshape(count, H, HD)
    value_heads = values_all.reshape(count, H, HD)
    scores = jnp.einsum('qhd,khd->hqk', query_heads, key_heads, precision=lax.Precision.HIGHEST) * HD ** (-0.5)
    scores = low_back(scores)
    position = jnp.arange(count, dtype=jnp.int32)
    allowed = (position[None, :] <= position[:, None]) & (position[None, :] < length)
    masked = jnp.where(allowed[None], scores, masked_value)
    highest = lax.optimization_barrier(jnp.max(masked, axis=-1, keepdims=True))
    weights = jnp.where(allowed[None], jnp.exp(masked - highest), 0.0)
    totals = lax.optimization_barrier(jnp.sum(weights, axis=-1))
    mixed = jnp.einsum('hqk,khd->qhd', low(weights), value_heads, precision=lax.Precision.HIGHEST)
    mixed = mixed / jnp.transpose(totals)[:, :, None]
    mixed = low_back(low(mixed.reshape(count, width)))
    branch = low_back(product(mixed, output_weight) + output_bias)
    middle = seq_input + branch
    normed_two = low(layer_norm(middle, second_gain, second_shift))
    hidden = low_back(product(normed_two, upward_weight) + upward_bias)
    active = low(jax.nn.gelu(hidden, approximate=True))
    return middle + product(active, down_weight) + down_bias

def reference(tokens, lengths, norm_gain, norm_shift, joint_weight, query_bias, value_bias, output_weight, output_bias, second_gain, second_shift, upward_weight, upward_bias, down_weight, down_bias, query_down, query_up, value_down, value_up, cotangent):
    frozen = tuple((item.astype(jnp.float32) for item in (norm_gain, norm_shift, joint_weight, query_bias, value_bias, output_weight, output_bias, second_gain, second_shift, upward_weight, upward_bias, down_weight, down_bias)))
    adapters = tuple((item.astype(jnp.float32) for item in (query_down, query_up, value_down, value_up)))

    def one_sequence(running, inputs):
        seq_tokens, length, seq_cotangent = inputs
        runner = jax.checkpoint(lambda seq_input, *factors: sequence_block(seq_input, *factors, length, frozen))
        result, pullback = jax.vjp(runner, seq_tokens.astype(jnp.float32), *adapters)
        gradients = pullback(seq_cotangent.astype(jnp.float32))
        running = tuple((former + latter for former, latter in zip(running, gradients[1:])))
        return (running, (result.astype(jnp.bfloat16), gradients[0]))
    starts = tuple((jnp.zeros_like(item) for item in adapters))
    sums, (outputs, input_grads) = lax.scan(one_sequence, starts, (tokens, lengths, cotangent))
    return (outputs, input_grads, sums[0], sums[1], sums[2], sums[3])
```

```python
from functools import partial

import jax
import jax.numpy as jnp
from jax import lax
from jax.experimental import pallas as pl
from jax.experimental.pallas import tpu as pltpu
from jax.sharding import PartitionSpec as P

HD = 64
RANK = 4
LANES = 128
STEP = 256


epsilon = 1e-05
masked_value = -1e30


def normalize(values, gain, shift):
    centred = values - jnp.mean(values, axis=-1, keepdims=True)
    inverse = lax.rsqrt(jnp.mean(centred * centred, axis=-1, keepdims=True) + epsilon)
    standard = centred * inverse
    return (standard * gain.astype(jnp.float32) + shift.astype(jnp.float32), standard, inverse)


def norm_back(grad, standard, inverse, gain):
    scaled = grad * gain.astype(jnp.float32)
    centred = scaled - jnp.mean(scaled, axis=-1, keepdims=True)
    return inverse * (centred - standard * jnp.mean(scaled * standard, axis=-1, keepdims=True))


def transposed(left, right):
    return lax.dot_general(
        left, right, (((0,), (0,)), ((), ())), preferred_element_type=jnp.float32
    )


def against(left, right):
    return lax.dot_general(
        left, right, (((1,), (1,)), ((), ())), preferred_element_type=jnp.float32
    )

def nt(a, b):
    return lax.dot_general(a, b, (((1,), (1,)), ((), ())), preferred_element_type=jnp.float32)

def tn(a, b):
    return lax.dot_general(a, b, (((0,), (0,)), ((), ())), preferred_element_type=jnp.float32)

def thirds(x):
    first = x.astype(jnp.bfloat16)
    rest = x - first.astype(jnp.float32)
    second = rest.astype(jnp.bfloat16)
    third = (rest - second.astype(jnp.float32)).astype(jnp.bfloat16)
    return first, second, third

def lanes_of(head):
    lane = lax.broadcasted_iota(jnp.int32, (1, LANES), 1)
    own = (lane // HD) == head
    spare = lane - HD * (1 - head)
    return own, spare

def at_spare(spare, start, parts, rest):
    for index, part in enumerate(parts):
        rest = jnp.where(spare == start + index, part, rest)
    return rest

def forward_kernel(lengths, q_ref, k_ref, v_ref, mixed_ref, aux_ref):
    length = lengths[pl.program_id(0)]
    rows = q_ref.shape[0]
    zero, one = jnp.bfloat16(0), jnp.bfloat16(1)
    place = lax.broadcasted_iota(jnp.int32, (rows, LANES), 0)
    bias = jnp.where(place < length, jnp.float32(0), jnp.float32(masked_value)).astype(jnp.bfloat16)
    causal = lax.broadcasted_iota(jnp.int32, (STEP, STEP), 1) <= lax.broadcasted_iota(jnp.int32, (STEP, STEP), 0)
    q, k, v = q_ref[...] * jnp.bfloat16(HD ** -0.5), k_ref[...], v_ref[...]
    own = [lanes_of(h)[0] for h in range(2)]
    spare = [lanes_of(h)[1] for h in range(2)]
    k_aug = [jnp.where(own[h], k, jnp.where(spare[h] == 0, bias, jnp.where((spare[h] > 0) & (spare[h] < 4), one, zero))) for h in range(2)]
    q_aug = [jnp.where(own[h], q, jnp.where(spare[h] == 0, one, zero)) for h in range(2)]
    for start in range(0, rows, STEP):
        stop = start + STEP
        outs, auxs = [], []
        for h in range(2):
            s = nt(q_aug[h][start:stop], k_aug[h][:stop])
            edge = jnp.where(causal, s[:, start:stop], masked_value)
            s = edge if start == 0 else jnp.concatenate([s[:, :start], edge], axis=1)
            top = jnp.max(s, axis=1, keepdims=True)
            w = jnp.exp(s - top)
            total = jnp.sum(w, axis=1, keepdims=True)
            o = jnp.dot(w.astype(jnp.bfloat16), v[:stop], preferred_element_type=jnp.float32)
            outs.append(o / total)
            parts = thirds(-(top + jnp.log(total)))
            auxs.append(at_spare(spare[h], 1, parts, jnp.where(spare[h] == 0, one, zero)))
        mixed_ref[start:stop] = jnp.where(own[0], outs[0], outs[1]).astype(jnp.bfloat16)
        aux_ref[start:stop] = jnp.where(own[0], auxs[1], auxs[0])

def backward_kernel(lengths, q_ref, k_ref, v_ref, mixed_ref, aux_ref, do_ref, dq_ref, dk_ref, dv_ref, acc):
    length = lengths[pl.program_id(0)]
    rows = q_ref.shape[0]
    zero, one = jnp.bfloat16(0), jnp.bfloat16(1)
    place = lax.broadcasted_iota(jnp.int32, (rows, LANES), 0)
    bias = jnp.where(place < length, jnp.float32(0), jnp.float32(masked_value)).astype(jnp.bfloat16)
    causal = lax.broadcasted_iota(jnp.int32, (STEP, STEP), 0) <= lax.broadcasted_iota(jnp.int32, (STEP, STEP), 1)
    q, k, v, do, aux = q_ref[...] * jnp.bfloat16(HD ** -0.5), k_ref[...], v_ref[...], do_ref[...], aux_ref[...]
    product = do.astype(jnp.float32) * mixed_ref[...].astype(jnp.float32)
    own = [lanes_of(h)[0] for h in range(2)]
    spare = [lanes_of(h)[1] for h in range(2)]
    k_aug = [jnp.where(own[h], k, jnp.where(spare[h] == 0, bias, jnp.where((spare[h] > 0) & (spare[h] < 4), one, zero))) for h in range(2)]
    q_aug = [jnp.where(own[h], q, aux) for h in range(2)]
    v_aug = [jnp.where(own[h], v, jnp.where((spare[h] >= 0) & (spare[h] < 3), one, zero)) for h in range(2)]
    do_aug = []
    for h in range(2):
        delta = jnp.sum(jnp.where(own[h], product, 0.0), axis=1, keepdims=True)
        do_aug.append(jnp.where(own[h], do, at_spare(spare[h], 0, thirds(-delta), zero)))
    for start in range(0, rows, STEP):
        stop = start + STEP
        dks, dvs, dqs = [], [], []
        for h in range(2):
            s = nt(k_aug[h][start:stop], q_aug[h][start:])
            edge = jnp.where(causal, s[:, :STEP], masked_value)
            s = edge if stop == rows else jnp.concatenate([edge, s[:, STEP:]], axis=1)
            p = jnp.exp(s)
            dp = nt(v_aug[h][start:stop], do_aug[h][start:])
            ds = (p * dp).astype(jnp.bfloat16)
            dvs.append(jnp.dot(p.astype(jnp.bfloat16), do[start:], preferred_element_type=jnp.float32))
            dks.append(jnp.dot(ds, q[start:], preferred_element_type=jnp.float32))
            dqs.append(tn(ds, k[start:stop]))
        dv_ref[start:stop] = jnp.where(own[0], dvs[0], dvs[1]).astype(jnp.bfloat16)
        dk_ref[start:stop] = jnp.where(own[0], dks[0], dks[1]).astype(jnp.bfloat16)
        dq = jnp.where(own[0], dqs[0], dqs[1])
        if start == 0:
            acc[...] = dq
        else:
            acc[start:] += dq
    dq_ref[...] = (acc[...] * HD ** -0.5).astype(jnp.bfloat16)

def column(offset):
    return lambda slot, pair, lengths: (slot, offset + pair)

def attention_forward(lengths, qkv, width):
    slots = lengths.shape[0]
    rows = qkv.shape[0] // slots
    pairs = width // LANES
    spec = lambda offset: pl.BlockSpec((rows, LANES), column(offset))
    return pl.pallas_call(
        forward_kernel,
        grid_spec=pltpu.PrefetchScalarGridSpec(
            num_scalar_prefetch=1, grid=(slots, pairs),
            in_specs=[spec(0), spec(pairs), spec(2 * pairs)],
            out_specs=[spec(0), spec(0)]),
        out_shape=[jax.ShapeDtypeStruct((slots * rows, width), jnp.bfloat16)] * 2,
        compiler_params=pltpu.CompilerParams(vmem_limit_bytes=48 << 20),
        name="attention_forward",
    )(lengths, qkv, qkv, qkv)

def attention_backward(lengths, qkv, mixed, aux, d_mixed, width):
    slots = lengths.shape[0]
    rows = qkv.shape[0] // slots
    pairs = width // LANES
    spec = lambda offset: pl.BlockSpec((rows, LANES), column(offset))
    return pl.pallas_call(
        backward_kernel,
        grid_spec=pltpu.PrefetchScalarGridSpec(
            num_scalar_prefetch=1, grid=(slots, pairs),
            in_specs=[spec(0), spec(pairs), spec(2 * pairs), spec(0), spec(0), spec(0)],
            out_specs=[spec(0)] * 3,
            scratch_shapes=[pltpu.VMEM((rows, LANES), jnp.float32)]),
        out_shape=[jax.ShapeDtypeStruct((slots * rows, width), jnp.bfloat16)] * 3,
        compiler_params=pltpu.CompilerParams(vmem_limit_bytes=48 << 20),
        name="attention_backward",
    )(lengths, qkv, qkv, qkv, mixed, aux, d_mixed)


def whole_slots(
    tokens,
    lengths,
    norm_gain,
    norm_shift,
    joint_weight,
    query_bias,
    value_bias,
    output_weight,
    output_bias,
    second_gain,
    second_shift,
    upward_weight,
    upward_bias,
    down_weight,
    down_bias,
    query_down,
    query_up,
    value_down,
    value_up,
    cotangent,
):
    seqs_here, rows, width = tokens.shape
    ranks = lax.axis_size("blk")
    slots = seqs_here // ranks
    adapter = 32.0 / RANK
    positions = slots * rows * ranks

    def to_slots(v):
        pieces = lax.all_to_all(
            v.reshape(ranks, slots, rows, width), "blk", 0, 0, tiled=True
        )
        return jnp.swapaxes(pieces, 0, 1).reshape(positions, width)

    def to_rows(v):
        pieces = jnp.swapaxes(v.reshape(slots, ranks, rows, width), 0, 1)
        return lax.all_to_all(pieces, "blk", 0, 0, tiled=True).reshape(seqs_here, rows, width)

    my_lengths = lax.dynamic_slice_in_dim(lengths, lax.axis_index("blk") * slots, slots)
    flat = to_slots(tokens).astype(jnp.float32)
    outer = to_slots(cotangent)
    normed_full, standard, inverse = normalize(flat, norm_gain, norm_shift)
    normed = normed_full.astype(jnp.bfloat16)
    joint = jnp.dot(normed, joint_weight, preferred_element_type=jnp.float32)
    query_low = jnp.dot(normed, query_down, preferred_element_type=jnp.float32).astype(jnp.bfloat16)
    value_low = jnp.dot(normed, value_down, preferred_element_type=jnp.float32).astype(jnp.bfloat16)
    bias = jnp.concatenate((query_bias, jnp.zeros_like(query_bias), value_bias)).astype(jnp.float32)
    lows = jnp.concatenate((query_low, value_low), axis=1)
    nothing = jnp.zeros_like(query_up)
    ups = jnp.concatenate(
        (
            jnp.concatenate((query_up, nothing, nothing), axis=1),
            jnp.concatenate((nothing, nothing, value_up), axis=1),
        ),
        axis=0,
    )
    qkv = (
        joint + bias + adapter * jnp.dot(lows, ups, preferred_element_type=jnp.float32)
    ).astype(jnp.bfloat16)
    mixed, aux = attention_forward(my_lengths, qkv, width)
    middle = (
        flat
        + jnp.dot(mixed, output_weight, preferred_element_type=jnp.float32)
        + output_bias.astype(jnp.float32)
    )
    normed_two_full, standard_two, inverse_two = normalize(middle, second_gain, second_shift)
    normed_two = normed_two_full.astype(jnp.bfloat16)
    hidden = jnp.dot(
        normed_two, upward_weight, preferred_element_type=jnp.float32
    ) + upward_bias.astype(jnp.float32)
    active_full, gelu_pull = jax.vjp(partial(jax.nn.gelu, approximate=True), hidden)
    active = active_full.astype(jnp.bfloat16)
    block_output = (
        middle
        + jnp.dot(active, down_weight, preferred_element_type=jnp.float32)
        + down_bias.astype(jnp.float32)
    ).astype(jnp.bfloat16)
    block_output = to_rows(block_output)
    d_active = against(outer, down_weight)
    d_hidden = gelu_pull(d_active)[0].astype(jnp.bfloat16)
    d_normed_two = against(d_hidden, upward_weight)
    d_middle = outer.astype(jnp.float32) + norm_back(
        d_normed_two, standard_two, inverse_two, second_gain
    )
    d_mixed = against(d_middle.astype(jnp.bfloat16), output_weight).astype(jnp.bfloat16)
    d_query_low, d_key_low, d_value_low = attention_backward(
        my_lengths, qkv, mixed, aux, d_mixed, width
    )
    query_up_grad = adapter * transposed(query_low, d_query_low)
    value_up_grad = adapter * transposed(value_low, d_value_low)
    d_query_small = (adapter * against(d_query_low, query_up)).astype(jnp.bfloat16)
    d_value_small = (adapter * against(d_value_low, value_up)).astype(jnp.bfloat16)
    query_down_grad = transposed(normed, d_query_small)
    value_down_grad = transposed(normed, d_value_small)
    d_joint = jnp.concatenate((d_query_low, d_key_low, d_value_low), axis=1)
    d_normed = (
        against(d_joint, joint_weight)
        + against(d_query_small, query_down)
        + against(d_value_small, value_down)
    )
    token_grads = d_middle + norm_back(d_normed, standard, inverse, norm_gain)
    token_grads = to_rows(token_grads.astype(jnp.bfloat16)).astype(jnp.float32)
    sums = lax.psum(
        (query_down_grad, query_up_grad, value_down_grad, value_up_grad), ("batch", "blk")
    )
    return (block_output, token_grads, sums[0], sums[1], sums[2], sums[3])


def body(
    tokens,
    lengths,
    norm_gain,
    norm_shift,
    joint_weight,
    query_bias,
    value_bias,
    output_weight,
    output_bias,
    second_gain,
    second_shift,
    upward_weight,
    upward_bias,
    down_weight,
    down_bias,
    query_down,
    query_up,
    value_down,
    value_up,
    cotangent,
):
    seqs_here, rows, width = tokens.shape
    heads = width // HD
    positions = seqs_here * rows
    length_all = rows * lax.axis_size("blk")
    scale = HD ** (-0.5)
    adapter = 32.0 / RANK
    flat = tokens.reshape(positions, width).astype(jnp.float32)
    normed_full, standard, inverse = normalize(flat, norm_gain, norm_shift)
    normed = normed_full.astype(jnp.bfloat16)
    joint = jnp.dot(normed, joint_weight, preferred_element_type=jnp.float32)
    query_low = jnp.dot(normed, query_down, preferred_element_type=jnp.float32).astype(jnp.bfloat16)
    value_low = jnp.dot(normed, value_down, preferred_element_type=jnp.float32).astype(jnp.bfloat16)
    queries = (
        joint[:, :width]
        + query_bias.astype(jnp.float32)
        + adapter * jnp.dot(query_low, query_up, preferred_element_type=jnp.float32)
    ).astype(jnp.bfloat16)
    keys_here = joint[:, width : 2 * width].astype(jnp.bfloat16)
    values_here = (
        joint[:, 2 * width :]
        + value_bias.astype(jnp.float32)
        + adapter * jnp.dot(value_low, value_up, preferred_element_type=jnp.float32)
    ).astype(jnp.bfloat16)
    query_heads = queries.reshape(seqs_here, rows, heads, HD)
    key_blocks = keys_here.reshape(seqs_here, rows, width)
    value_blocks = values_here.reshape(seqs_here, rows, width)
    device = lax.axis_index("blk")
    query_place = device * rows + jnp.arange(rows, dtype=jnp.int32)
    limits = lengths[:, None, None, None]

    def visible(query_pos, key_pos):
        return (key_pos[None, None, None, :] <= query_pos[None, None, :, None]) & (
            key_pos[None, None, None, :] < limits
        )

    running = jnp.full((seqs_here, heads, rows), masked_value, jnp.float32)
    key_piece = lax.all_gather(key_blocks, "blk", axis=1, tiled=True)
    value_piece = lax.all_gather(value_blocks, "blk", axis=1, tiled=True)
    count = key_piece.shape[1]
    key_heads = key_piece.reshape(seqs_here, count, heads, HD)
    value_heads = value_piece.reshape(seqs_here, count, heads, HD)
    allowed = visible(query_place, jnp.arange(count, dtype=jnp.int32))
    scores = (
        jnp.einsum("sqhd,skhd->shqk", query_heads, key_heads, preferred_element_type=jnp.float32)
        * scale
    )
    masked = jnp.where(allowed, scores, masked_value)
    highest = jnp.maximum(running, jnp.max(masked, axis=-1))
    weights = jnp.where(allowed, jnp.exp(masked - highest[..., None]), 0.0)
    totals = jnp.sum(weights, axis=-1)
    update = jnp.einsum(
        "shqk,skhd->sqhd",
        weights.astype(jnp.bfloat16),
        value_heads,
        preferred_element_type=jnp.float32,
    )
    summed = update
    running, totals, summed = (highest, totals, summed)
    mixed_full = summed / jnp.transpose(totals, (0, 2, 1))[..., None]
    log_total = running + jnp.log(totals)
    mixed_low = mixed_full.reshape(positions, width).astype(jnp.bfloat16)
    middle = (
        flat
        + jnp.dot(mixed_low, output_weight, preferred_element_type=jnp.float32)
        + output_bias.astype(jnp.float32)
    )
    normed_two_full, standard_two, inverse_two = normalize(middle, second_gain, second_shift)
    normed_two = normed_two_full.astype(jnp.bfloat16)
    hidden = jnp.dot(
        normed_two, upward_weight, preferred_element_type=jnp.float32
    ) + upward_bias.astype(jnp.float32)
    active_full, gelu_pull = jax.vjp(partial(jax.nn.gelu, approximate=True), hidden)
    active = active_full.astype(jnp.bfloat16)
    block_output = (
        (
            middle
            + jnp.dot(active, down_weight, preferred_element_type=jnp.float32)
            + down_bias.astype(jnp.float32)
        )
        .astype(jnp.bfloat16)
        .reshape(seqs_here, rows, width)
    )
    outer = cotangent.reshape(positions, width)
    d_active = against(outer, down_weight)
    d_hidden = gelu_pull(d_active)[0].astype(jnp.bfloat16)
    d_normed_two = against(d_hidden, upward_weight)
    d_middle = outer.astype(jnp.float32) + norm_back(
        d_normed_two, standard_two, inverse_two, second_gain
    )
    d_branch = d_middle.astype(jnp.bfloat16)
    d_mixed = against(d_branch, output_weight).astype(jnp.bfloat16)
    d_mixed_heads = d_mixed.reshape(seqs_here, rows, heads, HD)
    delta = jnp.transpose(
        jnp.sum(d_mixed_heads.astype(jnp.float32) * mixed_full, axis=-1), (0, 2, 1)
    )
    key_all, value_all = (
        lax.all_gather(key_blocks, "blk", axis=1, tiled=True),
        lax.all_gather(value_blocks, "blk", axis=1, tiled=True),
    )
    key_heads_all = key_all.reshape(seqs_here, length_all, heads, HD)
    value_heads_all = value_all.reshape(seqs_here, length_all, heads, HD)
    allowed_all = visible(query_place, jnp.arange(length_all, dtype=jnp.int32))
    scores = (
        jnp.einsum(
            "sqhd,skhd->shqk", query_heads, key_heads_all, preferred_element_type=jnp.float32
        )
        * scale
    )
    probs = jnp.where(allowed_all, jnp.exp(scores - log_total[..., None]), 0.0)
    d_probs = jnp.einsum(
        "sqhd,skhd->shqk", d_mixed_heads, value_heads_all, preferred_element_type=jnp.float32
    )
    d_scores = (probs * (d_probs - delta[..., None])).astype(jnp.bfloat16)
    d_queries = (
        jnp.einsum("shqk,skhd->sqhd", d_scores, key_heads_all, preferred_element_type=jnp.float32)
        * scale
    )
    d_keys_all = (
        jnp.einsum("shqk,sqhd->kshd", d_scores, query_heads, preferred_element_type=jnp.float32)
        * scale
    )
    d_values_all = jnp.einsum(
        "shqk,sqhd->kshd",
        probs.astype(jnp.bfloat16),
        d_mixed_heads,
        preferred_element_type=jnp.float32,
    )
    stacked = jnp.stack(
        (
            d_keys_all.reshape(length_all, seqs_here, width),
            d_values_all.reshape(length_all, seqs_here, width),
        ),
        axis=2,
    )
    owned = lax.psum_scatter(
        stacked.astype(jnp.bfloat16), "blk", scatter_dimension=0, tiled=True
    ).astype(jnp.float32)
    d_keys = jnp.transpose(owned[:, :, 0], (1, 0, 2)).reshape(positions, width)
    d_values = jnp.transpose(owned[:, :, 1], (1, 0, 2)).reshape(positions, width)
    d_query_low = d_queries.reshape(positions, width).astype(jnp.bfloat16)
    d_key_low = d_keys.astype(jnp.bfloat16)
    d_value_low = d_values.astype(jnp.bfloat16)
    query_up_grad = adapter * transposed(query_low, d_query_low)
    value_up_grad = adapter * transposed(value_low, d_value_low)
    d_query_small = (adapter * against(d_query_low, query_up)).astype(jnp.bfloat16)
    d_value_small = (adapter * against(d_value_low, value_up)).astype(jnp.bfloat16)
    query_down_grad = transposed(normed, d_query_small)
    value_down_grad = transposed(normed, d_value_small)
    d_joint = jnp.concatenate((d_query_low, d_key_low, d_value_low), axis=1)
    d_normed = (
        against(d_joint, joint_weight)
        + against(d_query_small, query_down)
        + against(d_value_small, value_down)
    )
    token_grads = (d_middle + norm_back(d_normed, standard, inverse, norm_gain)).reshape(
        seqs_here, rows, width
    )
    sums = lax.psum(
        (query_down_grad, query_up_grad, value_down_grad, value_up_grad), ("batch", "blk")
    )
    return (block_output, token_grads, sums[0], sums[1], sums[2], sums[3])


def choose(tokens, *others):
    fits = tokens.shape[0] % lax.axis_size("blk") == 0
    return (whole_slots if fits else body)(tokens, *others)


def solution(mesh):
    placed = (
        P("batch", "blk", None),
        P("batch"),
        P(),
        P(),
        P(),
        P(),
        P(),
        P(),
        P(),
        P(),
        P(),
        P(),
        P(),
        P(),
        P(),
        P(),
        P(),
        P(),
        P(),
        P("batch", "blk", None),
    )
    return jax.shard_map(
        choose,
        mesh=mesh,
        in_specs=placed,
        out_specs=(P("batch", "blk", None), P("batch", "blk", None), P(), P(), P(), P()),
        check_vma=False,
    )
```

```python
from functools import partial

import jax
import jax.numpy as jnp
from jax import lax
from jax.experimental import pallas as pl
from jax.experimental.pallas import tpu as pltpu
from jax.sharding import PartitionSpec as P

HD = 64
RANK = 4
LANES = 128
STEP = 256
CHUNK = 256
TILE = 512
VMEM = 56 << 20


epsilon = 1e-05
masked_value = -1e30


def normalize(values, gain, shift):
    centred = values - jnp.mean(values, axis=-1, keepdims=True)
    inverse = lax.rsqrt(jnp.mean(centred * centred, axis=-1, keepdims=True) + epsilon)
    standard = centred * inverse
    return (standard * gain.astype(jnp.float32) + shift.astype(jnp.float32), standard, inverse)


def norm_back(grad, standard, inverse, gain):
    scaled = grad * gain.astype(jnp.float32)
    centred = scaled - jnp.mean(scaled, axis=-1, keepdims=True)
    return inverse * (centred - standard * jnp.mean(scaled * standard, axis=-1, keepdims=True))


def transposed(left, right):
    return lax.dot_general(
        left, right, (((0,), (0,)), ((), ())), preferred_element_type=jnp.float32
    )


def against(left, right):
    return lax.dot_general(
        left, right, (((1,), (1,)), ((), ())), preferred_element_type=jnp.float32
    )


def nt(a, b):
    return lax.dot_general(a, b, (((1,), (1,)), ((), ())), preferred_element_type=jnp.float32)


def tn(a, b):
    return lax.dot_general(a, b, (((0,), (0,)), ((), ())), preferred_element_type=jnp.float32)


def nn(a, b):
    return jnp.dot(a, b, preferred_element_type=jnp.float32)


def thirds(x):
    first = x.astype(jnp.bfloat16)
    rest = x - first.astype(jnp.float32)
    second = rest.astype(jnp.bfloat16)
    third = (rest - second.astype(jnp.float32)).astype(jnp.bfloat16)
    return first, second, third


def lanes_of(head):
    lane = lax.broadcasted_iota(jnp.int32, (1, LANES), 1)
    own = (lane // HD) == head
    spare = lane - HD * (1 - head)
    return own, spare


def at_spare(spare, start, parts, rest):
    for index, part in enumerate(parts):
        rest = jnp.where(spare == start + index, part, rest)
    return rest


def forward_kernel(lengths, q_ref, k_ref, v_ref, mixed_ref, aux_ref):
    length = lengths[pl.program_id(0)]
    rows = q_ref.shape[0]
    zero, one = jnp.bfloat16(0), jnp.bfloat16(1)
    place = lax.broadcasted_iota(jnp.int32, (rows, LANES), 0)
    bias = jnp.where(place < length, jnp.float32(0), jnp.float32(masked_value)).astype(jnp.bfloat16)
    causal = lax.broadcasted_iota(jnp.int32, (STEP, STEP), 1) <= lax.broadcasted_iota(jnp.int32, (STEP, STEP), 0)
    q, k, v = q_ref[...] * jnp.bfloat16(HD ** -0.5), k_ref[...], v_ref[...]
    own = [lanes_of(h)[0] for h in range(2)]
    spare = [lanes_of(h)[1] for h in range(2)]
    k_aug = [jnp.where(own[h], k, jnp.where(spare[h] == 0, bias, jnp.where((spare[h] > 0) & (spare[h] < 4), one, zero))) for h in range(2)]
    q_aug = [jnp.where(own[h], q, jnp.where(spare[h] == 0, one, zero)) for h in range(2)]
    for start in range(0, rows, STEP):
        stop = start + STEP
        outs, auxs = [], []
        for h in range(2):
            s = nt(q_aug[h][start:stop], k_aug[h][:stop])
            edge = jnp.where(causal, s[:, start:stop], masked_value)
            s = edge if start == 0 else jnp.concatenate([s[:, :start], edge], axis=1)
            top = jnp.max(s, axis=1, keepdims=True)
            w = jnp.exp(s - top)
            total = jnp.sum(w, axis=1, keepdims=True)
            o = jnp.dot(w.astype(jnp.bfloat16), v[:stop], preferred_element_type=jnp.float32)
            outs.append(o / total)
            parts = thirds(-(top + jnp.log(total)))
            auxs.append(at_spare(spare[h], 1, parts, jnp.where(spare[h] == 0, one, zero)))
        mixed_ref[start:stop] = jnp.where(own[0], outs[0], outs[1]).astype(jnp.bfloat16)
        aux_ref[start:stop] = jnp.where(own[0], auxs[1], auxs[0])


def backward_kernel(lengths, q_ref, k_ref, v_ref, mixed_ref, aux_ref, do_ref, dq_ref, dk_ref, dv_ref, acc):
    length = lengths[pl.program_id(0)]
    rows = q_ref.shape[0]
    zero, one = jnp.bfloat16(0), jnp.bfloat16(1)
    place = lax.broadcasted_iota(jnp.int32, (rows, LANES), 0)
    bias = jnp.where(place < length, jnp.float32(0), jnp.float32(masked_value)).astype(jnp.bfloat16)
    causal = lax.broadcasted_iota(jnp.int32, (STEP, STEP), 0) <= lax.broadcasted_iota(jnp.int32, (STEP, STEP), 1)
    q, k, v, do, aux = q_ref[...] * jnp.bfloat16(HD ** -0.5), k_ref[...], v_ref[...], do_ref[...], aux_ref[...]
    product = do.astype(jnp.float32) * mixed_ref[...].astype(jnp.float32)
    own = [lanes_of(h)[0] for h in range(2)]
    spare = [lanes_of(h)[1] for h in range(2)]
    k_aug = [jnp.where(own[h], k, jnp.where(spare[h] == 0, bias, jnp.where((spare[h] > 0) & (spare[h] < 4), one, zero))) for h in range(2)]
    q_aug = [jnp.where(own[h], q, aux) for h in range(2)]
    v_aug = [jnp.where(own[h], v, jnp.where((spare[h] >= 0) & (spare[h] < 3), one, zero)) for h in range(2)]
    do_aug = []
    for h in range(2):
        delta = jnp.sum(jnp.where(own[h], product, 0.0), axis=1, keepdims=True)
        do_aug.append(jnp.where(own[h], do, at_spare(spare[h], 0, thirds(-delta), zero)))
    for start in range(0, rows, STEP):
        stop = start + STEP
        dks, dvs, dqs = [], [], []
        for h in range(2):
            s = nt(k_aug[h][start:stop], q_aug[h][start:])
            edge = jnp.where(causal, s[:, :STEP], masked_value)
            s = edge if stop == rows else jnp.concatenate([edge, s[:, STEP:]], axis=1)
            p = jnp.exp(s)
            dp = nt(v_aug[h][start:stop], do_aug[h][start:])
            ds = (p * dp).astype(jnp.bfloat16)
            dvs.append(jnp.dot(p.astype(jnp.bfloat16), do[start:], preferred_element_type=jnp.float32))
            dks.append(jnp.dot(ds, q[start:], preferred_element_type=jnp.float32))
            dqs.append(tn(ds, k[start:stop]))
        dv_ref[start:stop] = jnp.where(own[0], dvs[0], dvs[1]).astype(jnp.bfloat16)
        dk_ref[start:stop] = jnp.where(own[0], dks[0], dks[1]).astype(jnp.bfloat16)
        dq = jnp.where(own[0], dqs[0], dqs[1])
        if start == 0:
            acc[...] = dq
        else:
            acc[start:] += dq
    dq_ref[...] = (acc[...] * HD ** -0.5).astype(jnp.bfloat16)


def column(offset):
    return lambda slot, pair, lengths: (slot, offset + pair)


def attention_forward(lengths, qkv, width):
    slots = lengths.shape[0]
    rows = qkv.shape[0] // slots
    pairs = width // LANES
    spec = lambda offset: pl.BlockSpec((rows, LANES), column(offset))
    return pl.pallas_call(
        forward_kernel,
        grid_spec=pltpu.PrefetchScalarGridSpec(
            num_scalar_prefetch=1, grid=(slots, pairs),
            in_specs=[spec(0), spec(pairs), spec(2 * pairs)],
            out_specs=[spec(0), spec(0)]),
        out_shape=[jax.ShapeDtypeStruct((slots * rows, width), jnp.bfloat16)] * 2,
        compiler_params=pltpu.CompilerParams(vmem_limit_bytes=48 << 20),
        name="attention_forward",
    )(lengths, qkv, qkv, qkv)


def attention_backward(lengths, qkv, mixed, aux, d_mixed, width):
    slots = lengths.shape[0]
    rows = qkv.shape[0] // slots
    pairs = width // LANES
    spec = lambda offset: pl.BlockSpec((rows, LANES), column(offset))
    return pl.pallas_call(
        backward_kernel,
        grid_spec=pltpu.PrefetchScalarGridSpec(
            num_scalar_prefetch=1, grid=(slots, pairs),
            in_specs=[spec(0), spec(pairs), spec(2 * pairs), spec(0), spec(0), spec(0)],
            out_specs=[spec(0)] * 3,
            scratch_shapes=[pltpu.VMEM((rows, LANES), jnp.float32)]),
        out_shape=[jax.ShapeDtypeStruct((slots * rows, width), jnp.bfloat16)] * 3,
        compiler_params=pltpu.CompilerParams(vmem_limit_bytes=48 << 20),
        name="attention_backward",
    )(lengths, qkv, qkv, qkv, mixed, aux, d_mixed)


def standardize(values):
    centred = values - jnp.mean(values, axis=-1, keepdims=True)
    inverse = lax.rsqrt(jnp.mean(centred * centred, axis=-1, keepdims=True) + epsilon)
    return centred * inverse, inverse


def pull_norm(grad, standard, inverse, gain):
    scaled = grad * gain
    centred = scaled - jnp.mean(scaled, axis=-1, keepdims=True)
    return inverse * (centred - standard * jnp.mean(scaled * standard, axis=-1, keepdims=True))


def f32(ref):
    return ref[...].astype(jnp.float32)


def chunks_of(rows):
    return [pl.ds(start, CHUNK) for start in range(0, rows, CHUNK)]


def project_kernel(tokens, gain, shift, weight, bias, downs, ups, qkv, lows, normed):
    rows = tokens.shape[0]
    @pl.when(pl.program_id(0) == 0)
    def _():
        for part in chunks_of(rows):
            standard, _ = standardize(tokens[part].astype(jnp.float32))
            normed[part] = (standard * f32(gain) + f32(shift)).astype(jnp.bfloat16)
            lows[part] = nn(normed[part], downs[...]).astype(jnp.bfloat16)
    for part in chunks_of(rows):
        qkv[part] = (nn(normed[part], weight[...]) + bias[...] + nn(lows[part], ups[...])).astype(jnp.bfloat16)


def project(tokens, gain, shift, weight, bias, downs, ups):
    rows, width = tokens.shape
    wide = weight.shape[1]
    small = downs.shape[1]
    fixed = lambda shape: pl.BlockSpec(shape, lambda i: (0, 0))
    sliding = lambda depth: pl.BlockSpec((depth, TILE), lambda i: (0, i))
    return pl.pallas_call(
        project_kernel, grid=(wide // TILE,),
        in_specs=[fixed((rows, width)), fixed((1, width)), fixed((1, width)), sliding(width), sliding(1), fixed((width, small)), sliding(small)],
        out_specs=[sliding(rows), fixed((rows, small))],
        out_shape=[jax.ShapeDtypeStruct((rows, wide), jnp.bfloat16), jax.ShapeDtypeStruct((rows, small), jnp.bfloat16)],
        scratch_shapes=[pltpu.VMEM((rows, width), jnp.bfloat16)],
        compiler_params=pltpu.CompilerParams(vmem_limit_bytes=VMEM),
        name="project",
    )(tokens, gain, shift, weight, bias, downs, ups)


def gelu_and_slope(u):
    c = (2.0 / jnp.pi) ** 0.5
    square = u * u
    share = 0.5 + 0.5 * jnp.tanh(u * (c + (c * 0.044715) * square))
    value = u * share
    slope = share + value * (1.0 - share) * (2 * c + (6 * c * 0.044715) * square)
    return value, slope


def feed_kernel(tokens, mixed, out_weight, out_bias, gain, shift, up, up_bias, down, down_bias, result, middle, slopes, total, normed):
    rows = tokens.shape[0]
    step = pl.program_id(0)
    @pl.when(step == 0)
    def _():
        for part in chunks_of(rows):
            m = tokens[part].astype(jnp.float32) + nn(mixed[part], out_weight[...]) + f32(out_bias)
            middle[part] = m
            standard, _ = standardize(m)
            normed[part] = (standard * f32(gain) + f32(shift)).astype(jnp.bfloat16)
            total[part] = m + f32(down_bias)
    for part in chunks_of(rows):
        value, slope = gelu_and_slope(nn(normed[part], up[...]) + f32(up_bias))
        slopes[part] = slope.astype(jnp.bfloat16)
        total[part] += nn(value.astype(jnp.bfloat16), down[...])
    @pl.when(step == pl.num_programs(0) - 1)
    def _():
        result[...] = total[...].astype(jnp.bfloat16)


def feed(tokens, mixed, out_weight, out_bias, gain, shift, up, up_bias, down, down_bias):
    rows, width = tokens.shape
    wide = up.shape[1]
    fixed = lambda shape: pl.BlockSpec(shape, lambda i: (0, 0))
    sliding = lambda depth: pl.BlockSpec((depth, TILE), lambda i: (0, i))
    return pl.pallas_call(
        feed_kernel, grid=(wide // TILE,),
        in_specs=[fixed((rows, width)), fixed((rows, width)), fixed((width, width)), fixed((1, width)), fixed((1, width)), fixed((1, width)),
                  sliding(width), sliding(1), pl.BlockSpec((TILE, width), lambda i: (i, 0)), fixed((1, width))],
        out_specs=[fixed((rows, width)), fixed((rows, width)), sliding(rows)],
        out_shape=[jax.ShapeDtypeStruct((rows, width), jnp.bfloat16), jax.ShapeDtypeStruct((rows, width), jnp.float32), jax.ShapeDtypeStruct((rows, wide), jnp.bfloat16)],
        scratch_shapes=[pltpu.VMEM((rows, width), jnp.float32), pltpu.VMEM((rows, width), jnp.bfloat16)],
        compiler_params=pltpu.CompilerParams(vmem_limit_bytes=VMEM),
        name="feed",
    )(tokens, mixed, out_weight, out_bias, gain, shift, up, up_bias, down, down_bias)


def feed_back_kernel(outer, slopes, up, down, middle, gain, out_weight, d_middle, d_mixed, total):
    rows = outer.shape[0]
    step = pl.program_id(0)
    for part in chunks_of(rows):
        d_hidden = (nt(outer[part], down[...]) * slopes[part].astype(jnp.float32)).astype(jnp.bfloat16)
        grad = nt(d_hidden, up[...])
        @pl.when(step == 0)
        def _():
            total[part] = grad
        @pl.when(step > 0)
        def _():
            total[part] += grad
    @pl.when(step == pl.num_programs(0) - 1)
    def _():
        for part in chunks_of(rows):
            standard, inverse = standardize(middle[part])
            d = outer[part].astype(jnp.float32) + pull_norm(total[part], standard, inverse, f32(gain))
            d_middle[part] = d
            d_mixed[part] = nt(d.astype(jnp.bfloat16), out_weight[...]).astype(jnp.bfloat16)


def feed_back(outer, slopes, up, down, middle, gain, out_weight):
    rows, width = outer.shape
    wide = up.shape[1]
    fixed = lambda shape: pl.BlockSpec(shape, lambda i: (0, 0))
    sliding = lambda depth: pl.BlockSpec((depth, TILE), lambda i: (0, i))
    return pl.pallas_call(
        feed_back_kernel, grid=(wide // TILE,),
        in_specs=[fixed((rows, width)), sliding(rows), sliding(width), pl.BlockSpec((TILE, width), lambda i: (i, 0)),
                  fixed((rows, width)), fixed((1, width)), fixed((width, width))],
        out_specs=[fixed((rows, width)), fixed((rows, width))],
        out_shape=[jax.ShapeDtypeStruct((rows, width), jnp.float32), jax.ShapeDtypeStruct((rows, width), jnp.bfloat16)],
        scratch_shapes=[pltpu.VMEM((rows, width), jnp.float32)],
        compiler_params=pltpu.CompilerParams(vmem_limit_bytes=VMEM),
        name="feed_back",
    )(outer, slopes, up, down, middle, gain, out_weight)


def finish_kernel(dq, dk, dv, tokens, d_middle, lows, gain, shift, weight, downs, ups, grads, factors):
    width = tokens.shape[1]
    step = pl.program_id(0)
    standard, inverse = standardize(f32(tokens))
    normed = (standard * f32(gain) + f32(shift)).astype(jnp.bfloat16)
    small = (nt(dq[...], ups[:, :width]) + nt(dv[...], ups[:, 2 * width:])).astype(jnp.bfloat16)
    d_normed = nt(dq[...], weight[:, :width]) + nt(dk[...], weight[:, width:2 * width]) + nt(dv[...], weight[:, 2 * width:]) + nt(small, downs[...])
    grads[...] = (f32(d_middle) + pull_norm(d_normed, standard, inverse, f32(gain))).astype(grads.dtype)
    parts = [tn(small, normed), tn(lows[...], dq[...]), tn(lows[...], dv[...])]
    @pl.when(step == 0)
    def _():
        for index, part in enumerate(parts):
            factors[index] = part
    @pl.when(step > 0)
    def _():
        for index, part in enumerate(parts):
            factors[index] += part


def finish(dq, dk, dv, tokens, d_middle, lows, gain, shift, weight, downs, ups):
    rows, width = tokens.shape
    small = downs.shape[1]
    fixed = lambda shape: pl.BlockSpec(shape, lambda i: (0,) * len(shape))
    sliding = lambda across: pl.BlockSpec((CHUNK, across), lambda i: (i, 0))
    return pl.pallas_call(
        finish_kernel, grid=(rows // CHUNK,),
        in_specs=[sliding(width)] * 5 + [sliding(small), fixed((1, width)), fixed((1, width)), fixed(weight.shape), fixed(downs.shape), fixed(ups.shape)],
        out_specs=[sliding(width), fixed((3, small, width))],
        out_shape=[jax.ShapeDtypeStruct((rows, width), jnp.bfloat16), jax.ShapeDtypeStruct((3, small, width), jnp.float32)],
        compiler_params=pltpu.CompilerParams(vmem_limit_bytes=VMEM),
        name="finish",
    )(dq, dk, dv, tokens, d_middle, lows, gain, shift, weight, downs, ups)


def sum_over(v, axis):
    size = lax.axis_size(axis)
    if size & (size - 1):
        return lax.psum(v, axis)
    step = 1
    while step < size:
        v = v + lax.ppermute(v, axis, [(i, i ^ step) for i in range(size)])
        step *= 2
    return v


def whole_slots(
    tokens,
    lengths,
    norm_gain,
    norm_shift,
    joint_weight,
    query_bias,
    value_bias,
    output_weight,
    output_bias,
    second_gain,
    second_shift,
    upward_weight,
    upward_bias,
    down_weight,
    down_bias,
    query_down,
    query_up,
    value_down,
    value_up,
    cotangent,
):
    seqs_here, rows, width = tokens.shape
    ranks = lax.axis_size("blk")
    slots = seqs_here // ranks
    adapter = 32.0 / RANK
    positions = slots * rows * ranks

    def to_slots(v):
        pieces = lax.all_to_all(v.reshape(ranks, slots, rows, width), "blk", 0, 0, tiled=True)
        return jnp.swapaxes(pieces, 0, 1).reshape(positions, width)

    def to_rows(v):
        pieces = jnp.swapaxes(v.reshape(slots, ranks, rows, width), 0, 1)
        return lax.all_to_all(pieces, "blk", 0, 0, tiled=True).reshape(seqs_here, rows, width)

    def line(v):
        return v.reshape(1, -1)

    my_lengths = lax.dynamic_slice_in_dim(lengths, lax.axis_index("blk") * slots, slots)
    bias = line(jnp.concatenate((query_bias, jnp.zeros_like(query_bias), value_bias)))
    downs = jnp.pad(
        jnp.concatenate((query_down, value_down), axis=1), ((0, 0), (0, LANES - 2 * RANK))
    )
    ups = adapter * (
        jnp.pad(query_up, ((0, LANES - RANK), (0, 2 * width)))
        + jnp.pad(value_up, ((RANK, LANES - 2 * RANK), (2 * width, 0)))
    )
    ups = ups.astype(jnp.bfloat16)
    inner = to_slots(tokens)
    outer = to_slots(cotangent)
    qkv, lows = project(
        inner, line(norm_gain), line(norm_shift), joint_weight, bias, downs, ups
    )
    mixed, aux = attention_forward(my_lengths, qkv, width)
    result, middle, slopes = feed(
        inner,
        mixed,
        output_weight,
        line(output_bias),
        line(second_gain),
        line(second_shift),
        upward_weight,
        line(upward_bias),
        down_weight,
        line(down_bias),
    )
    result, middle, slopes, outer = lax.optimization_barrier((result, middle, slopes, outer))
    block_output = to_rows(result)
    d_middle, d_mixed = feed_back(
        outer, slopes, upward_weight, down_weight, middle, line(second_gain), output_weight
    )
    d_queries, d_keys, d_values = attention_backward(
        my_lengths, qkv, mixed, aux, d_mixed, width
    )
    grads, factors = finish(
        d_queries,
        d_keys,
        d_values,
        inner,
        d_middle,
        lows,
        line(norm_gain),
        line(norm_shift),
        joint_weight,
        downs,
        ups,
    )
    token_grads = to_rows(grads).astype(jnp.float32)
    packed = jnp.concatenate(
        (
            factors[0, : 2 * RANK],
            adapter * factors[1, :RANK],
            adapter * factors[2, RANK : 2 * RANK],
        )
    )
    packed = sum_over(sum_over(packed, "batch"), "blk")
    query_down_grad, value_down_grad = packed[:RANK].T, packed[RANK : 2 * RANK].T
    query_up_grad, value_up_grad = packed[2 * RANK : 3 * RANK], packed[3 * RANK :]
    return (
        block_output,
        token_grads,
        query_down_grad,
        query_up_grad,
        value_down_grad,
        value_up_grad,
    )


def body(
    tokens,
    lengths,
    norm_gain,
    norm_shift,
    joint_weight,
    query_bias,
    value_bias,
    output_weight,
    output_bias,
    second_gain,
    second_shift,
    upward_weight,
    upward_bias,
    down_weight,
    down_bias,
    query_down,
    query_up,
    value_down,
    value_up,
    cotangent,
):
    seqs_here, rows, width = tokens.shape
    heads = width // HD
    positions = seqs_here * rows
    length_all = rows * lax.axis_size("blk")
    scale = HD ** (-0.5)
    adapter = 32.0 / RANK
    flat = tokens.reshape(positions, width).astype(jnp.float32)
    normed_full, standard, inverse = normalize(flat, norm_gain, norm_shift)
    normed = normed_full.astype(jnp.bfloat16)
    joint = jnp.dot(normed, joint_weight, preferred_element_type=jnp.float32)
    query_low = jnp.dot(normed, query_down, preferred_element_type=jnp.float32).astype(jnp.bfloat16)
    value_low = jnp.dot(normed, value_down, preferred_element_type=jnp.float32).astype(jnp.bfloat16)
    queries = (
        joint[:, :width]
        + query_bias.astype(jnp.float32)
        + adapter * jnp.dot(query_low, query_up, preferred_element_type=jnp.float32)
    ).astype(jnp.bfloat16)
    keys_here = joint[:, width : 2 * width].astype(jnp.bfloat16)
    values_here = (
        joint[:, 2 * width :]
        + value_bias.astype(jnp.float32)
        + adapter * jnp.dot(value_low, value_up, preferred_element_type=jnp.float32)
    ).astype(jnp.bfloat16)
    query_heads = queries.reshape(seqs_here, rows, heads, HD)
    key_blocks = keys_here.reshape(seqs_here, rows, width)
    value_blocks = values_here.reshape(seqs_here, rows, width)
    device = lax.axis_index("blk")
    query_place = device * rows + jnp.arange(rows, dtype=jnp.int32)
    limits = lengths[:, None, None, None]

    def visible(query_pos, key_pos):
        return (key_pos[None, None, None, :] <= query_pos[None, None, :, None]) & (
            key_pos[None, None, None, :] < limits
        )

    running = jnp.full((seqs_here, heads, rows), masked_value, jnp.float32)
    key_piece = lax.all_gather(key_blocks, "blk", axis=1, tiled=True)
    value_piece = lax.all_gather(value_blocks, "blk", axis=1, tiled=True)
    count = key_piece.shape[1]
    key_heads = key_piece.reshape(seqs_here, count, heads, HD)
    value_heads = value_piece.reshape(seqs_here, count, heads, HD)
    allowed = visible(query_place, jnp.arange(count, dtype=jnp.int32))
    scores = (
        jnp.einsum("sqhd,skhd->shqk", query_heads, key_heads, preferred_element_type=jnp.float32)
        * scale
    )
    masked = jnp.where(allowed, scores, masked_value)
    highest = jnp.maximum(running, jnp.max(masked, axis=-1))
    weights = jnp.where(allowed, jnp.exp(masked - highest[..., None]), 0.0)
    totals = jnp.sum(weights, axis=-1)
    update = jnp.einsum(
        "shqk,skhd->sqhd",
        weights.astype(jnp.bfloat16),
        value_heads,
        preferred_element_type=jnp.float32,
    )
    summed = update
    running, totals, summed = (highest, totals, summed)
    mixed_full = summed / jnp.transpose(totals, (0, 2, 1))[..., None]
    log_total = running + jnp.log(totals)
    mixed_low = mixed_full.reshape(positions, width).astype(jnp.bfloat16)
    middle = (
        flat
        + jnp.dot(mixed_low, output_weight, preferred_element_type=jnp.float32)
        + output_bias.astype(jnp.float32)
    )
    normed_two_full, standard_two, inverse_two = normalize(middle, second_gain, second_shift)
    normed_two = normed_two_full.astype(jnp.bfloat16)
    hidden = jnp.dot(
        normed_two, upward_weight, preferred_element_type=jnp.float32
    ) + upward_bias.astype(jnp.float32)
    active_full, gelu_pull = jax.vjp(partial(jax.nn.gelu, approximate=True), hidden)
    active = active_full.astype(jnp.bfloat16)
    block_output = (
        (
            middle
            + jnp.dot(active, down_weight, preferred_element_type=jnp.float32)
            + down_bias.astype(jnp.float32)
        )
        .astype(jnp.bfloat16)
        .reshape(seqs_here, rows, width)
    )
    outer = cotangent.reshape(positions, width)
    d_active = against(outer, down_weight)
    d_hidden = gelu_pull(d_active)[0].astype(jnp.bfloat16)
    d_normed_two = against(d_hidden, upward_weight)
    d_middle = outer.astype(jnp.float32) + norm_back(
        d_normed_two, standard_two, inverse_two, second_gain
    )
    d_branch = d_middle.astype(jnp.bfloat16)
    d_mixed = against(d_branch, output_weight).astype(jnp.bfloat16)
    d_mixed_heads = d_mixed.reshape(seqs_here, rows, heads, HD)
    delta = jnp.transpose(
        jnp.sum(d_mixed_heads.astype(jnp.float32) * mixed_full, axis=-1), (0, 2, 1)
    )
    key_all, value_all = (
        lax.all_gather(key_blocks, "blk", axis=1, tiled=True),
        lax.all_gather(value_blocks, "blk", axis=1, tiled=True),
    )
    key_heads_all = key_all.reshape(seqs_here, length_all, heads, HD)
    value_heads_all = value_all.reshape(seqs_here, length_all, heads, HD)
    allowed_all = visible(query_place, jnp.arange(length_all, dtype=jnp.int32))
    scores = (
        jnp.einsum(
            "sqhd,skhd->shqk", query_heads, key_heads_all, preferred_element_type=jnp.float32
        )
        * scale
    )
    probs = jnp.where(allowed_all, jnp.exp(scores - log_total[..., None]), 0.0)
    d_probs = jnp.einsum(
        "sqhd,skhd->shqk", d_mixed_heads, value_heads_all, preferred_element_type=jnp.float32
    )
    d_scores = (probs * (d_probs - delta[..., None])).astype(jnp.bfloat16)
    d_queries = (
        jnp.einsum("shqk,skhd->sqhd", d_scores, key_heads_all, preferred_element_type=jnp.float32)
        * scale
    )
    d_keys_all = (
        jnp.einsum("shqk,sqhd->kshd", d_scores, query_heads, preferred_element_type=jnp.float32)
        * scale
    )
    d_values_all = jnp.einsum(
        "shqk,sqhd->kshd",
        probs.astype(jnp.bfloat16),
        d_mixed_heads,
        preferred_element_type=jnp.float32,
    )
    stacked = jnp.stack(
        (
            d_keys_all.reshape(length_all, seqs_here, width),
            d_values_all.reshape(length_all, seqs_here, width),
        ),
        axis=2,
    )
    owned = lax.psum_scatter(
        stacked.astype(jnp.bfloat16), "blk", scatter_dimension=0, tiled=True
    ).astype(jnp.float32)
    d_keys = jnp.transpose(owned[:, :, 0], (1, 0, 2)).reshape(positions, width)
    d_values = jnp.transpose(owned[:, :, 1], (1, 0, 2)).reshape(positions, width)
    d_query_low = d_queries.reshape(positions, width).astype(jnp.bfloat16)
    d_key_low = d_keys.astype(jnp.bfloat16)
    d_value_low = d_values.astype(jnp.bfloat16)
    query_up_grad = adapter * transposed(query_low, d_query_low)
    value_up_grad = adapter * transposed(value_low, d_value_low)
    d_query_small = (adapter * against(d_query_low, query_up)).astype(jnp.bfloat16)
    d_value_small = (adapter * against(d_value_low, value_up)).astype(jnp.bfloat16)
    query_down_grad = transposed(normed, d_query_small)
    value_down_grad = transposed(normed, d_value_small)
    d_joint = jnp.concatenate((d_query_low, d_key_low, d_value_low), axis=1)
    d_normed = (
        against(d_joint, joint_weight)
        + against(d_query_small, query_down)
        + against(d_value_small, value_down)
    )
    token_grads = (d_middle + norm_back(d_normed, standard, inverse, norm_gain)).reshape(
        seqs_here, rows, width
    )
    sums = lax.psum(
        (query_down_grad, query_up_grad, value_down_grad, value_up_grad), ("batch", "blk")
    )
    return (block_output, token_grads, sums[0], sums[1], sums[2], sums[3])


def choose(tokens, *others):
    fits = tokens.shape[0] % lax.axis_size("blk") == 0
    return (whole_slots if fits else body)(tokens, *others)


def solution(mesh):
    placed = (
        P("batch", "blk", None),
        P("batch"),
        P(),
        P(),
        P(),
        P(),
        P(),
        P(),
        P(),
        P(),
        P(),
        P(),
        P(),
        P(),
        P(),
        P(),
        P(),
        P(),
        P(),
        P("batch", "blk", None),
    )
    return jax.shard_map(
        choose,
        mesh=mesh,
        in_specs=placed,
        out_specs=(P("batch", "blk", None), P("batch", "blk", None), P(), P(), P(), P()),
        check_vma=False,
    )
```

```python
from functools import partial

import jax
import jax.numpy as jnp
from jax import lax
from jax.experimental import pallas as pl
from jax.experimental.pallas import tpu as pltpu
from jax.sharding import PartitionSpec as P

HD = 64
RANK = 4
LANES = 128
STEP = 256
SAFE = 80.0
GROUP = 2
CHUNK = 512
TILE = 1024
VMEM = 58 << 20
GAIN = 0
SHIFT = 1
JOINT = 2
OUT = 5
GAIN_TWO = 6
SHIFT_TWO = 7
DOWN = 8
UP = 9


epsilon = 1e-05
masked_value = -1e30


def normalize(values, gain, shift):
    centred = values - jnp.mean(values, axis=-1, keepdims=True)
    inverse = lax.rsqrt(jnp.mean(centred * centred, axis=-1, keepdims=True) + epsilon)
    standard = centred * inverse
    return (standard * gain.astype(jnp.float32) + shift.astype(jnp.float32), standard, inverse)


def norm_back(grad, standard, inverse, gain):
    scaled = grad * gain.astype(jnp.float32)
    centred = scaled - jnp.mean(scaled, axis=-1, keepdims=True)
    return inverse * (centred - standard * jnp.mean(scaled * standard, axis=-1, keepdims=True))


def transposed(left, right):
    return lax.dot_general(
        left, right, (((0,), (0,)), ((), ())), preferred_element_type=jnp.float32
    )


def against(left, right):
    return lax.dot_general(
        left, right, (((1,), (1,)), ((), ())), preferred_element_type=jnp.float32
    )


def nt(a, b):
    return lax.dot_general(a, b, (((1,), (1,)), ((), ())), preferred_element_type=jnp.float32)


def tn(a, b):
    return lax.dot_general(a, b, (((0,), (0,)), ((), ())), preferred_element_type=jnp.float32)


def nn(a, b):
    return jnp.dot(a, b, preferred_element_type=jnp.float32)


def thirds(x):
    first = x.astype(jnp.bfloat16)
    rest = x - first.astype(jnp.float32)
    second = rest.astype(jnp.bfloat16)
    third = (rest - second.astype(jnp.float32)).astype(jnp.bfloat16)
    return first, second, third


def in_first_head():
    return lax.broadcasted_iota(jnp.int32, (1, LANES), 1) < HD


def spare_lane():
    return lax.broadcasted_iota(jnp.int32, (1, LANES), 1) % HD


def key_extras(rows, length):
    place = lax.broadcasted_iota(jnp.int32, (rows, LANES), 0)
    bias = jnp.where(place < length, 0.0, masked_value).astype(jnp.bfloat16)
    spare = spare_lane()
    return jnp.where(spare == 0, bias, jnp.where(spare < 4, jnp.bfloat16(1), jnp.bfloat16(0)))


def forward_kernel(lengths, peaks, q_ref, k_ref, v_ref, mixed_ref, aux_ref, calm):
    group, rows = q_ref.shape[:2]
    one, zero = jnp.bfloat16(1), jnp.bfloat16(0)

    @pl.when(pl.program_id(1) == 0)
    def _():
        bound = jnp.max(peaks[0]) * jnp.max(peaks[1])
        calm[0] = (bound < (SAFE / HD ** -0.5) ** 2).astype(jnp.int32)

    first, spare = in_first_head(), spare_lane()
    extras = key_extras(rows, lengths[pl.program_id(0)])
    lead = jnp.where(spare == 0, one, zero)
    causal = lax.broadcasted_iota(jnp.int32, (STEP, STEP), 1) <= lax.broadcasted_iota(jnp.int32, (STEP, STEP), 0)

    def widen(pair):
        q, k, v = q_ref[pair] * jnp.bfloat16(HD ** -0.5), k_ref[pair], v_ref[pair]
        q_aug = [jnp.where(first, q, lead), jnp.where(first, lead, q)]
        k_aug = [jnp.where(first, k, extras), jnp.where(first, extras, k)]
        v_aug = [jnp.where(first, v, one), jnp.where(first, one, v)]
        return q_aug, k_aug, v_aug

    def write(pair, start, sums, tops):
        total = jnp.where(first, sums[1], sums[0])
        mixed = jnp.where(first, sums[0], sums[1]) * pltpu.roll(1.0 / total, HD, 1)
        mixed_ref[pair, start:start + STEP] = mixed.astype(jnp.bfloat16)
        level = jnp.log(total)
        if tops is not None:
            level = level + jnp.where(first, tops[1], tops[0])
        aux = lead
        for index, part in enumerate(thirds(-level)):
            aux = jnp.where(spare == index + 1, part, aux)
        aux_ref[pair, start:start + STEP] = aux

    @pl.when(calm[0] == 1)
    def _():
        ready = widen(0)
        for pair in range(group):
            q_aug, k_aug, v_aug = ready
            sums = [[None] * (rows // STEP) for _ in range(2)]
            for start in range(0, rows, STEP):
                stop = start + STEP
                for h in range(2):
                    s = nt(q_aug[h][start:], k_aug[h][start:stop])
                    w = jnp.exp(jnp.where(causal, s[:STEP], masked_value)).astype(jnp.bfloat16)
                    if stop < rows:
                        w = jnp.concatenate([w, jnp.exp(s[STEP:]).astype(jnp.bfloat16)], axis=0)
                    o = nn(w, v_aug[h][start:stop])
                    for part in range(start // STEP, rows // STEP):
                        add = o[part * STEP - start:(part + 1) * STEP - start]
                        sums[h][part] = add if start == 0 else sums[h][part] + add
                if start == 0 and pair + 1 < group:
                    ready = widen(pair + 1)
                write(pair, start, [sums[0][start // STEP], sums[1][start // STEP]], None)

    @pl.when(calm[0] == 0)
    def _():
        for pair in range(group):
            q_aug, k_aug, v_aug = widen(pair)
            for start in range(0, rows, STEP):
                stop = start + STEP
                sums, tops = [], []
                for h in range(2):
                    s = nt(q_aug[h][start:stop], k_aug[h][:stop])
                    edge = jnp.where(causal, s[:, start:], masked_value)
                    s = edge if start == 0 else jnp.concatenate([s[:, :start], edge], axis=1)
                    tops.append(jnp.max(s, axis=1, keepdims=True))
                    w = jnp.exp(s - tops[h]).astype(jnp.bfloat16)
                    sums.append(nn(w, v_aug[h][:stop]))
                write(pair, start, sums, tops)


def backward_kernel(lengths, q_ref, k_ref, v_ref, mixed_ref, aux_ref, do_ref, dq_ref, dk_ref, dv_ref, acc):
    group, rows = q_ref.shape[:2]
    one, zero = jnp.bfloat16(1), jnp.bfloat16(0)
    first, spare = in_first_head(), spare_lane()
    extras = key_extras(rows, lengths[pl.program_id(0)])
    three = jnp.where(spare < 3, one, zero)
    causal = lax.broadcasted_iota(jnp.int32, (STEP, STEP), 0) <= lax.broadcasted_iota(jnp.int32, (STEP, STEP), 1)
    row = lax.broadcasted_iota(jnp.int32, (LANES, LANES), 0) // HD
    column = lax.broadcasted_iota(jnp.int32, (LANES, LANES), 1) // HD
    cross = jnp.where(row != column, one, zero)

    def widen(pair):
        q, k, v = q_ref[pair] * jnp.bfloat16(HD ** -0.5), k_ref[pair], v_ref[pair]
        do, aux = do_ref[pair], aux_ref[pair]
        k_aug = [jnp.where(first, k, extras), jnp.where(first, extras, k)]
        q_aug = [jnp.where(first, q, aux), jnp.where(first, aux, q)]
        v_aug = [jnp.where(first, v, three), jnp.where(first, three, v)]
        product = do.astype(jnp.float32) * mixed_ref[pair].astype(jnp.float32)
        high = product.astype(jnp.bfloat16)
        low = (product - high.astype(jnp.float32)).astype(jnp.bfloat16)
        delta = nn(high, cross) + nn(low, cross)
        extra = zero
        for index, part in enumerate(thirds(-delta)):
            extra = jnp.where(spare == index, part, extra)
        do_aug = [jnp.where(first, do, extra), jnp.where(first, extra, do)]
        return q, k, do, q_aug, k_aug, v_aug, do_aug

    ready = widen(0)
    for pair in range(group):
        q, k, do, q_aug, k_aug, v_aug, do_aug = ready
        for start in range(0, rows, STEP):
            stop = start + STEP
            dks, dvs, dqs = [], [], []
            for h in range(2):
                s = nt(k_aug[h][start:stop], q_aug[h][start:])
                edge = jnp.where(causal, s[:, :STEP], masked_value)
                s = edge if stop == rows else jnp.concatenate([edge, s[:, STEP:]], axis=1)
                p = jnp.exp(s)
                dp = nt(v_aug[h][start:stop], do_aug[h][start:])
                ds = (p * dp).astype(jnp.bfloat16)
                dvs.append(nn(p.astype(jnp.bfloat16), do[start:]))
                dks.append(nn(ds, q[start:]))
                dqs.append(tn(ds, k[start:stop]))
            dv_ref[pair, start:stop] = jnp.where(first, dvs[0], dvs[1]).astype(jnp.bfloat16)
            dk_ref[pair, start:stop] = jnp.where(first, dks[0], dks[1]).astype(jnp.bfloat16)
            dq = jnp.where(first, dqs[0], dqs[1])
            if start == 0:
                acc[...] = dq
                if pair + 1 < group:
                    ready = widen(pair + 1)
            else:
                acc[start:] += dq
            dq_ref[pair, start:stop] = (acc[start:stop] * HD ** -0.5).astype(jnp.bfloat16)


def heads(rows, offset):
    return pl.BlockSpec((GROUP, rows, LANES), lambda slot, pair, lengths: (offset // GROUP + pair, slot, 0))


def attention_forward(lengths, peaks, qkv):
    slots = lengths.shape[0]
    pairs, rows = qkv.shape[0] // 3, qkv.shape[1] // slots
    return pl.pallas_call(
        forward_kernel,
        grid_spec=pltpu.PrefetchScalarGridSpec(
            num_scalar_prefetch=1, grid=(slots, pairs // GROUP),
            in_specs=[pl.BlockSpec(peaks.shape, lambda slot, pair, lengths: (0, 0, 0))] + [heads(rows, part * pairs) for part in range(3)],
            out_specs=[heads(rows, 0)] * 2,
            scratch_shapes=[pltpu.SMEM((1,), jnp.int32)]),
        out_shape=[jax.ShapeDtypeStruct((pairs,) + qkv.shape[1:], jnp.bfloat16)] * 2,
        compiler_params=pltpu.CompilerParams(vmem_limit_bytes=VMEM),
        name="attention_forward",
    )(lengths, peaks, qkv, qkv, qkv)


def attention_backward(lengths, qkv, mixed, aux, d_mixed):
    slots = lengths.shape[0]
    pairs, rows = qkv.shape[0] // 3, qkv.shape[1] // slots
    return pl.pallas_call(
        backward_kernel,
        grid_spec=pltpu.PrefetchScalarGridSpec(
            num_scalar_prefetch=1, grid=(slots, pairs // GROUP),
            in_specs=[heads(rows, part * pairs) for part in range(3)] + [heads(rows, 0)] * 3,
            out_specs=[heads(rows, 0)] * 3,
            scratch_shapes=[pltpu.VMEM((rows, LANES), jnp.float32)]),
        out_shape=[jax.ShapeDtypeStruct((pairs,) + qkv.shape[1:], jnp.bfloat16)] * 3,
        compiler_params=pltpu.CompilerParams(vmem_limit_bytes=VMEM),
        name="attention_backward",
    )(lengths, qkv, qkv, qkv, mixed, aux, d_mixed)


def standardize(values):
    centred = values - jnp.mean(values, axis=-1, keepdims=True)
    inverse = lax.rsqrt(jnp.mean(centred * centred, axis=-1, keepdims=True) + epsilon)
    return centred * inverse, inverse


def pull_norm(grad, standard, inverse, gain):
    scaled = grad * gain
    centred = scaled - jnp.mean(scaled, axis=-1, keepdims=True)
    return inverse * (centred - standard * jnp.mean(scaled * standard, axis=-1, keepdims=True))


def f32(ref):
    return ref[...].astype(jnp.float32)


def pieces_of(rows, size):
    return [slice(start, start + size) for start in range(0, rows, size)]


def side_by_side(ref, part):
    return jnp.concatenate([ref[pair, part] for pair in range(ref.shape[0])], axis=1)


def spread(ref, part, values):
    for pair in range(ref.shape[0]):
        ref[pair, part] = values[:, pair * LANES:(pair + 1) * LANES].astype(ref.dtype)


def fixed(shape):
    return pl.BlockSpec(shape, lambda step: (0,) * len(shape), pipeline_mode=pl.Buffered(1))


def sliding(depth):
    return pl.BlockSpec((depth, TILE), lambda step: (0, step))


def project_kernel(tokens, vectors, weight, downs, ups, qkv, lows, peaks, normed):
    step = pl.program_id(0)
    parts = pieces_of(tokens.shape[0], CHUNK)
    lane = lax.broadcasted_iota(jnp.int32, (TILE, LANES), 0) // HD
    each = jnp.where(lane == lax.broadcasted_iota(jnp.int32, (TILE, LANES), 1), 1.0, 0.0).astype(jnp.bfloat16)

    @pl.when(step == 0)
    def _():
        for part in parts:
            standard, _ = standardize(tokens[part].astype(jnp.float32))
            normed[part] = (standard * vectors[GAIN:GAIN + 1] + vectors[SHIFT:SHIFT + 1]).astype(jnp.bfloat16)
            lows[part] = nn(normed[part], downs[...]).astype(jnp.bfloat16)

    for index, part in enumerate(parts):
        values = (nn(normed[part], weight[...]) + vectors[pl.ds(JOINT + step, 1)] + nn(lows[part], ups[...])).astype(jnp.bfloat16)
        spread(qkv, part, values)
        peak = jnp.max(nn(values * values, each).reshape(-1, 8, LANES), axis=0)
        peaks[0] = peak if index == 0 else jnp.maximum(peaks[0], peak)


def project(tokens, vectors, weight, downs, ups):
    rows, width = tokens.shape
    wide, small = weight.shape[1], downs.shape[1]
    return pl.pallas_call(
        project_kernel,
        grid=(wide // TILE,),
        in_specs=[fixed((rows, width)), fixed(vectors.shape), sliding(width), fixed((width, small)), sliding(small)],
        out_specs=[
            pl.BlockSpec((TILE // LANES, rows, LANES), lambda step: (step, 0, 0)),
            fixed((rows, small)),
            pl.BlockSpec((1, 8, LANES), lambda step: (step, 0, 0)),
        ],
        out_shape=[
            jax.ShapeDtypeStruct((wide // LANES, rows, LANES), jnp.bfloat16),
            jax.ShapeDtypeStruct((rows, small), jnp.bfloat16),
            jax.ShapeDtypeStruct((wide // TILE, 8, LANES), jnp.float32),
        ],
        scratch_shapes=[pltpu.VMEM((rows, width), jnp.bfloat16)],
        compiler_params=pltpu.CompilerParams(vmem_limit_bytes=VMEM),
        name="project",
    )(tokens, vectors, weight, downs, ups)


def gelu_and_slope(u):
    c = (2.0 / jnp.pi) ** 0.5
    square = u * u
    share = 0.5 + 0.5 * jnp.tanh(u * (c + (c * 0.044715) * square))
    value = u * share
    slope = share + value * (1.0 - share) * (2 * c + (6 * c * 0.044715) * square)
    return value, slope


def feed_kernel(tokens, mixed, vectors, out_weight, up, down, result, middle, slopes, total, normed):
    step = pl.program_id(0)
    parts = pieces_of(tokens.shape[0], CHUNK)

    @pl.when(step == 0)
    def _():
        for part in parts:
            m = tokens[part].astype(jnp.float32) + nn(side_by_side(mixed, part), out_weight[...]) + vectors[OUT:OUT + 1]
            middle[part] = m
            standard, _ = standardize(m)
            normed[part] = (standard * vectors[GAIN_TWO:GAIN_TWO + 1] + vectors[SHIFT_TWO:SHIFT_TWO + 1]).astype(jnp.bfloat16)
            total[part] = m + vectors[DOWN:DOWN + 1]

    for part in parts:
        value, slope = gelu_and_slope(nn(normed[part], up[...]) + vectors[pl.ds(UP + step, 1)])
        slopes[part] = slope.astype(jnp.bfloat16)
        total[part] += nn(value.astype(jnp.bfloat16), down[...])

    @pl.when(step == pl.num_programs(0) - 1)
    def _():
        result[...] = total[...].astype(jnp.bfloat16)


def feed(tokens, mixed, vectors, out_weight, up, down):
    rows, width = tokens.shape
    wide = up.shape[1]
    return pl.pallas_call(
        feed_kernel,
        grid=(wide // TILE,),
        in_specs=[fixed((rows, width)), fixed(mixed.shape), fixed(vectors.shape), fixed((width, width)),
                  sliding(width), pl.BlockSpec((TILE, width), lambda step: (step, 0))],
        out_specs=[fixed((rows, width)), fixed((rows, width)), sliding(rows)],
        out_shape=[
            jax.ShapeDtypeStruct((rows, width), jnp.bfloat16),
            jax.ShapeDtypeStruct((rows, width), jnp.float32),
            jax.ShapeDtypeStruct((rows, wide), jnp.bfloat16),
        ],
        scratch_shapes=[pltpu.VMEM((rows, width), jnp.float32), pltpu.VMEM((rows, width), jnp.bfloat16)],
        compiler_params=pltpu.CompilerParams(vmem_limit_bytes=VMEM),
        name="feed",
    )(tokens, mixed, vectors, out_weight, up, down)


def feed_back_kernel(outer, slopes, up, down, middle, vectors, out_weight, d_middle, d_mixed, total):
    step = pl.program_id(0)
    parts = pieces_of(outer.shape[0], CHUNK)
    for part in parts:
        d_hidden = (nt(outer[part], down[...]) * slopes[part].astype(jnp.float32)).astype(jnp.bfloat16)
        grad = nt(d_hidden, up[...])
        total[part] = jnp.where(step == 0, grad, total[part] + grad)

    @pl.when(step == pl.num_programs(0) - 1)
    def _():
        for part in parts:
            standard, inverse = standardize(middle[part])
            d = outer[part].astype(jnp.float32) + pull_norm(total[part], standard, inverse, vectors[GAIN_TWO:GAIN_TWO + 1])
            d_middle[part] = d
            spread(d_mixed, part, nt(d.astype(jnp.bfloat16), out_weight[...]))


def feed_back(outer, slopes, up, down, middle, vectors, out_weight):
    rows, width = outer.shape
    wide = up.shape[1]
    return pl.pallas_call(
        feed_back_kernel,
        grid=(wide // TILE,),
        in_specs=[fixed((rows, width)), sliding(rows), sliding(width), pl.BlockSpec((TILE, width), lambda step: (step, 0)),
                  fixed((rows, width)), fixed(vectors.shape), fixed((width, width))],
        out_specs=[fixed((rows, width)), fixed((width // LANES, rows, LANES))],
        out_shape=[jax.ShapeDtypeStruct((rows, width), jnp.float32), jax.ShapeDtypeStruct((width // LANES, rows, LANES), jnp.bfloat16)],
        scratch_shapes=[pltpu.VMEM((rows, width), jnp.float32)],
        compiler_params=pltpu.CompilerParams(vmem_limit_bytes=VMEM),
        name="feed_back",
    )(outer, slopes, up, down, middle, vectors, out_weight)


def finish_kernel(dq, dk, dv, tokens, d_middle, lows, vectors, weight, downs, ups, grads, factors):
    width = tokens.shape[1]
    step = pl.program_id(0)
    everything = slice(None)
    d_queries, d_keys, d_values = (side_by_side(ref, everything) for ref in (dq, dk, dv))
    standard, inverse = standardize(f32(tokens))
    gain = vectors[GAIN:GAIN + 1]
    normed = (standard * gain + vectors[SHIFT:SHIFT + 1]).astype(jnp.bfloat16)
    small = (nt(d_queries, ups[:, :width]) + nt(d_values, ups[:, 2 * width:])).astype(jnp.bfloat16)
    d_normed = nt(d_queries, weight[:, :width]) + nt(d_keys, weight[:, width:2 * width]) + nt(d_values, weight[:, 2 * width:]) + nt(small, downs[...])
    grads[...] = (f32(d_middle) + pull_norm(d_normed, standard, inverse, gain)).astype(grads.dtype)
    for index, part in enumerate((tn(small, normed), tn(lows[...], d_queries), tn(lows[...], d_values))):
        factors[index] = jnp.where(step == 0, part, factors[index] + part)


def finish(dq, dk, dv, tokens, d_middle, lows, vectors, weight, downs, ups):
    rows, width = tokens.shape
    small = downs.shape[1]
    across = lambda span: pl.BlockSpec((CHUNK, span), lambda step: (step, 0))
    paired = pl.BlockSpec((width // LANES, CHUNK, LANES), lambda step: (0, step, 0))
    return pl.pallas_call(
        finish_kernel,
        grid=(rows // CHUNK,),
        in_specs=[paired] * 3 + [across(width)] * 2 + [across(small), fixed(vectors.shape), fixed(weight.shape), fixed(downs.shape), fixed(ups.shape)],
        out_specs=[across(width), fixed((3, small, width))],
        out_shape=[jax.ShapeDtypeStruct((rows, width), jnp.bfloat16), jax.ShapeDtypeStruct((3, small, width), jnp.float32)],
        compiler_params=pltpu.CompilerParams(vmem_limit_bytes=VMEM),
        name="finish",
    )(dq, dk, dv, tokens, d_middle, lows, vectors, weight, downs, ups)


def sum_over(v, axis):
    size = lax.axis_size(axis)
    if size & (size - 1):
        return lax.psum(v, axis)
    step = 1
    while step < size:
        v = v + lax.ppermute(v, axis, [(i, i ^ step) for i in range(size)])
        step *= 2
    return v


def whole_slots(
    tokens,
    lengths,
    norm_gain,
    norm_shift,
    joint_weight,
    query_bias,
    value_bias,
    output_weight,
    output_bias,
    second_gain,
    second_shift,
    upward_weight,
    upward_bias,
    down_weight,
    down_bias,
    query_down,
    query_up,
    value_down,
    value_up,
    cotangent,
):
    seqs_here, rows, width = tokens.shape
    ranks = lax.axis_size("blk")
    slots = seqs_here // ranks
    adapter = 32.0 / RANK
    positions = slots * rows * ranks

    def to_slots(v):
        pieces = lax.all_to_all(v.reshape(ranks, slots, rows, width), "blk", 0, 0, tiled=True)
        return jnp.swapaxes(pieces, 0, 1).reshape(positions, width)

    def to_rows(v):
        pieces = jnp.swapaxes(v.reshape(slots, ranks, rows, width), 0, 1)
        return lax.all_to_all(pieces, "blk", 0, 0, tiled=True).reshape(seqs_here, rows, width)

    my_lengths = lax.dynamic_slice_in_dim(lengths, lax.axis_index("blk") * slots, slots)
    vectors = jnp.concatenate(
        (
            norm_gain,
            norm_shift,
            query_bias,
            jnp.zeros_like(query_bias),
            value_bias,
            output_bias,
            second_gain,
            second_shift,
            down_bias,
            upward_bias,
        )
    )
    vectors = vectors.astype(jnp.float32).reshape(-1, width)
    downs = jnp.pad(
        jnp.concatenate((query_down, value_down), axis=1), ((0, 0), (0, LANES - 2 * RANK))
    )
    ups = adapter * (
        jnp.pad(query_up, ((0, LANES - RANK), (0, 2 * width)))
        + jnp.pad(value_up, ((RANK, LANES - 2 * RANK), (2 * width, 0)))
    )
    ups = ups.astype(jnp.bfloat16)
    inner = to_slots(tokens)
    cotangent, vectors, downs, ups, my_lengths = lax.optimization_barrier(
        (cotangent, vectors, downs, ups, my_lengths)
    )
    outer = to_slots(cotangent)
    qkv, lows, peaks = project(inner, vectors, joint_weight, downs, ups)
    mixed, aux = attention_forward(my_lengths, peaks, qkv)
    result, middle, slopes = feed(
        inner, mixed, vectors, output_weight, upward_weight, down_weight
    )
    result, middle, slopes, outer = lax.optimization_barrier((result, middle, slopes, outer))
    block_output = to_rows(result)
    d_middle, d_mixed = feed_back(
        outer, slopes, upward_weight, down_weight, middle, vectors, output_weight
    )
    d_queries, d_keys, d_values = attention_backward(
        my_lengths, qkv, mixed, aux, d_mixed
    )
    grads, factors = finish(
        d_queries,
        d_keys,
        d_values,
        inner,
        d_middle,
        lows,
        vectors,
        joint_weight,
        downs,
        ups,
    )
    token_grads = to_rows(grads).astype(jnp.float32)
    packed = jnp.concatenate(
        (
            factors[0, : 2 * RANK],
            adapter * factors[1, :RANK],
            adapter * factors[2, RANK : 2 * RANK],
        )
    )
    packed = sum_over(sum_over(packed, "batch"), "blk")
    query_down_grad, value_down_grad = packed[:RANK].T, packed[RANK : 2 * RANK].T
    query_up_grad, value_up_grad = packed[2 * RANK : 3 * RANK], packed[3 * RANK :]
    return (
        block_output,
        token_grads,
        query_down_grad,
        query_up_grad,
        value_down_grad,
        value_up_grad,
    )


def body(
    tokens,
    lengths,
    norm_gain,
    norm_shift,
    joint_weight,
    query_bias,
    value_bias,
    output_weight,
    output_bias,
    second_gain,
    second_shift,
    upward_weight,
    upward_bias,
    down_weight,
    down_bias,
    query_down,
    query_up,
    value_down,
    value_up,
    cotangent,
):
    seqs_here, rows, width = tokens.shape
    heads = width // HD
    positions = seqs_here * rows
    length_all = rows * lax.axis_size("blk")
    scale = HD ** (-0.5)
    adapter = 32.0 / RANK
    flat = tokens.reshape(positions, width).astype(jnp.float32)
    normed_full, standard, inverse = normalize(flat, norm_gain, norm_shift)
    normed = normed_full.astype(jnp.bfloat16)
    joint = jnp.dot(normed, joint_weight, preferred_element_type=jnp.float32)
    query_low = jnp.dot(normed, query_down, preferred_element_type=jnp.float32).astype(jnp.bfloat16)
    value_low = jnp.dot(normed, value_down, preferred_element_type=jnp.float32).astype(jnp.bfloat16)
    queries = (
        joint[:, :width]
        + query_bias.astype(jnp.float32)
        + adapter * jnp.dot(query_low, query_up, preferred_element_type=jnp.float32)
    ).astype(jnp.bfloat16)
    keys_here = joint[:, width : 2 * width].astype(jnp.bfloat16)
    values_here = (
        joint[:, 2 * width :]
        + value_bias.astype(jnp.float32)
        + adapter * jnp.dot(value_low, value_up, preferred_element_type=jnp.float32)
    ).astype(jnp.bfloat16)
    query_heads = queries.reshape(seqs_here, rows, heads, HD)
    key_blocks = keys_here.reshape(seqs_here, rows, width)
    value_blocks = values_here.reshape(seqs_here, rows, width)
    device = lax.axis_index("blk")
    query_place = device * rows + jnp.arange(rows, dtype=jnp.int32)
    limits = lengths[:, None, None, None]

    def visible(query_pos, key_pos):
        return (key_pos[None, None, None, :] <= query_pos[None, None, :, None]) & (
            key_pos[None, None, None, :] < limits
        )

    running = jnp.full((seqs_here, heads, rows), masked_value, jnp.float32)
    key_piece = lax.all_gather(key_blocks, "blk", axis=1, tiled=True)
    value_piece = lax.all_gather(value_blocks, "blk", axis=1, tiled=True)
    count = key_piece.shape[1]
    key_heads = key_piece.reshape(seqs_here, count, heads, HD)
    value_heads = value_piece.reshape(seqs_here, count, heads, HD)
    allowed = visible(query_place, jnp.arange(count, dtype=jnp.int32))
    scores = (
        jnp.einsum("sqhd,skhd->shqk", query_heads, key_heads, preferred_element_type=jnp.float32)
        * scale
    )
    masked = jnp.where(allowed, scores, masked_value)
    highest = jnp.maximum(running, jnp.max(masked, axis=-1))
    weights = jnp.where(allowed, jnp.exp(masked - highest[..., None]), 0.0)
    totals = jnp.sum(weights, axis=-1)
    update = jnp.einsum(
        "shqk,skhd->sqhd",
        weights.astype(jnp.bfloat16),
        value_heads,
        preferred_element_type=jnp.float32,
    )
    summed = update
    running, totals, summed = (highest, totals, summed)
    mixed_full = summed / jnp.transpose(totals, (0, 2, 1))[..., None]
    log_total = running + jnp.log(totals)
    mixed_low = mixed_full.reshape(positions, width).astype(jnp.bfloat16)
    middle = (
        flat
        + jnp.dot(mixed_low, output_weight, preferred_element_type=jnp.float32)
        + output_bias.astype(jnp.float32)
    )
    normed_two_full, standard_two, inverse_two = normalize(middle, second_gain, second_shift)
    normed_two = normed_two_full.astype(jnp.bfloat16)
    hidden = jnp.dot(
        normed_two, upward_weight, preferred_element_type=jnp.float32
    ) + upward_bias.astype(jnp.float32)
    active_full, gelu_pull = jax.vjp(partial(jax.nn.gelu, approximate=True), hidden)
    active = active_full.astype(jnp.bfloat16)
    block_output = (
        (
            middle
            + jnp.dot(active, down_weight, preferred_element_type=jnp.float32)
            + down_bias.astype(jnp.float32)
        )
        .astype(jnp.bfloat16)
        .reshape(seqs_here, rows, width)
    )
    outer = cotangent.reshape(positions, width)
    d_active = against(outer, down_weight)
    d_hidden = gelu_pull(d_active)[0].astype(jnp.bfloat16)
    d_normed_two = against(d_hidden, upward_weight)
    d_middle = outer.astype(jnp.float32) + norm_back(
        d_normed_two, standard_two, inverse_two, second_gain
    )
    d_branch = d_middle.astype(jnp.bfloat16)
    d_mixed = against(d_branch, output_weight).astype(jnp.bfloat16)
    d_mixed_heads = d_mixed.reshape(seqs_here, rows, heads, HD)
    delta = jnp.transpose(
        jnp.sum(d_mixed_heads.astype(jnp.float32) * mixed_full, axis=-1), (0, 2, 1)
    )
    key_all, value_all = (
        lax.all_gather(key_blocks, "blk", axis=1, tiled=True),
        lax.all_gather(value_blocks, "blk", axis=1, tiled=True),
    )
    key_heads_all = key_all.reshape(seqs_here, length_all, heads, HD)
    value_heads_all = value_all.reshape(seqs_here, length_all, heads, HD)
    allowed_all = visible(query_place, jnp.arange(length_all, dtype=jnp.int32))
    scores = (
        jnp.einsum(
            "sqhd,skhd->shqk", query_heads, key_heads_all, preferred_element_type=jnp.float32
        )
        * scale
    )
    probs = jnp.where(allowed_all, jnp.exp(scores - log_total[..., None]), 0.0)
    d_probs = jnp.einsum(
        "sqhd,skhd->shqk", d_mixed_heads, value_heads_all, preferred_element_type=jnp.float32
    )
    d_scores = (probs * (d_probs - delta[..., None])).astype(jnp.bfloat16)
    d_queries = (
        jnp.einsum("shqk,skhd->sqhd", d_scores, key_heads_all, preferred_element_type=jnp.float32)
        * scale
    )
    d_keys_all = (
        jnp.einsum("shqk,sqhd->kshd", d_scores, query_heads, preferred_element_type=jnp.float32)
        * scale
    )
    d_values_all = jnp.einsum(
        "shqk,sqhd->kshd",
        probs.astype(jnp.bfloat16),
        d_mixed_heads,
        preferred_element_type=jnp.float32,
    )
    stacked = jnp.stack(
        (
            d_keys_all.reshape(length_all, seqs_here, width),
            d_values_all.reshape(length_all, seqs_here, width),
        ),
        axis=2,
    )
    owned = lax.psum_scatter(
        stacked.astype(jnp.bfloat16), "blk", scatter_dimension=0, tiled=True
    ).astype(jnp.float32)
    d_keys = jnp.transpose(owned[:, :, 0], (1, 0, 2)).reshape(positions, width)
    d_values = jnp.transpose(owned[:, :, 1], (1, 0, 2)).reshape(positions, width)
    d_query_low = d_queries.reshape(positions, width).astype(jnp.bfloat16)
    d_key_low = d_keys.astype(jnp.bfloat16)
    d_value_low = d_values.astype(jnp.bfloat16)
    query_up_grad = adapter * transposed(query_low, d_query_low)
    value_up_grad = adapter * transposed(value_low, d_value_low)
    d_query_small = (adapter * against(d_query_low, query_up)).astype(jnp.bfloat16)
    d_value_small = (adapter * against(d_value_low, value_up)).astype(jnp.bfloat16)
    query_down_grad = transposed(normed, d_query_small)
    value_down_grad = transposed(normed, d_value_small)
    d_joint = jnp.concatenate((d_query_low, d_key_low, d_value_low), axis=1)
    d_normed = (
        against(d_joint, joint_weight)
        + against(d_query_small, query_down)
        + against(d_value_small, value_down)
    )
    token_grads = (d_middle + norm_back(d_normed, standard, inverse, norm_gain)).reshape(
        seqs_here, rows, width
    )
    sums = lax.psum(
        (query_down_grad, query_up_grad, value_down_grad, value_up_grad), ("batch", "blk")
    )
    return (block_output, token_grads, sums[0], sums[1], sums[2], sums[3])


def choose(tokens, *others):
    fits = tokens.shape[0] % lax.axis_size("blk") == 0
    return (whole_slots if fits else body)(tokens, *others)


def solution(mesh):
    placed = (
        P("batch", "blk", None),
        P("batch"),
        P(),
        P(),
        P(),
        P(),
        P(),
        P(),
        P(),
        P(),
        P(),
        P(),
        P(),
        P(),
        P(),
        P(),
        P(),
        P(),
        P(),
        P("batch", "blk", None),
    )
    return jax.shard_map(
        choose,
        mesh=mesh,
        in_specs=placed,
        out_specs=(P("batch", "blk", None), P("batch", "blk", None), P(), P(), P(), P()),
        check_vma=False,
    )
```

```python
from functools import partial

import jax
import jax.numpy as jnp
from jax import lax
from jax.experimental import pallas as pl
from jax.experimental.pallas import tpu as pltpu
from jax.sharding import PartitionSpec as P

HD = 64
RANK = 4
LANES = 128
STEP = 256
SAFE = 80.0
GROUP = 2
CHUNK = 512
TILE = 1024
VMEM = 58 << 20
GAIN = 0
SHIFT = 1
JOINT = 2
OUT = 5
GAIN_TWO = 6
SHIFT_TWO = 7
DOWN = 8
UP = 9
SMALL = 16


epsilon = 1e-05
masked_value = -1e30


def normalize(values, gain, shift):
    centred = values - jnp.mean(values, axis=-1, keepdims=True)
    inverse = lax.rsqrt(jnp.mean(centred * centred, axis=-1, keepdims=True) + epsilon)
    standard = centred * inverse
    return (standard * gain.astype(jnp.float32) + shift.astype(jnp.float32), standard, inverse)


def norm_back(grad, standard, inverse, gain):
    scaled = grad * gain.astype(jnp.float32)
    centred = scaled - jnp.mean(scaled, axis=-1, keepdims=True)
    return inverse * (centred - standard * jnp.mean(scaled * standard, axis=-1, keepdims=True))


def transposed(left, right):
    return lax.dot_general(
        left, right, (((0,), (0,)), ((), ())), preferred_element_type=jnp.float32
    )


def against(left, right):
    return lax.dot_general(
        left, right, (((1,), (1,)), ((), ())), preferred_element_type=jnp.float32
    )


def nt(a, b):
    return lax.dot_general(a, b, (((1,), (1,)), ((), ())), preferred_element_type=jnp.float32)


def tn(a, b):
    return lax.dot_general(a, b, (((0,), (0,)), ((), ())), preferred_element_type=jnp.float32)


def nn(a, b):
    return jnp.dot(a, b, preferred_element_type=jnp.float32)


def thirds(x):
    first = x.astype(jnp.bfloat16)
    rest = x - first.astype(jnp.float32)
    second = rest.astype(jnp.bfloat16)
    third = (rest - second.astype(jnp.float32)).astype(jnp.bfloat16)
    return first, second, third


def in_first_head():
    return lax.broadcasted_iota(jnp.int32, (1, LANES), 1) < HD


def spare_lane():
    return lax.broadcasted_iota(jnp.int32, (1, LANES), 1) % HD


def key_extras(begin, rows, length):
    place = begin + lax.broadcasted_iota(jnp.int32, (rows, LANES), 0)
    bias = jnp.where(place < length, 0.0, masked_value).astype(jnp.bfloat16)
    spare = spare_lane()
    return jnp.where(spare == 0, bias, jnp.where(spare < 4, jnp.bfloat16(1), jnp.bfloat16(0)))


def forward_kernel(place, peaks, others, qkv_ref, mixed_ref, aux_ref, calm):
    q_ref, k_ref, v_ref = (qkv_ref.at[part] for part in range(3))
    group, rows = q_ref.shape[:2]
    one, zero = jnp.bfloat16(1), jnp.bfloat16(0)

    @pl.when(pl.program_id(0) == 0)
    def _():
        bound = jnp.max(jnp.maximum(peaks[0], others[0])) * jnp.max(jnp.maximum(peaks[1], others[1]))
        calm[0] = (bound < (SAFE / HD ** -0.5) ** 2).astype(jnp.int32)

    first, spare = in_first_head(), spare_lane()
    extras = key_extras(0, rows, place[3])
    lead = jnp.where(spare == 0, one, zero)
    causal = lax.broadcasted_iota(jnp.int32, (STEP, STEP), 1) <= lax.broadcasted_iota(jnp.int32, (STEP, STEP), 0)

    def widen(pair):
        q, k, v = q_ref[pair] * jnp.bfloat16(HD ** -0.5), k_ref[pair], v_ref[pair]
        q_aug = [jnp.where(first, q, lead), jnp.where(first, lead, q)]
        k_aug = [jnp.where(first, k, extras), jnp.where(first, extras, k)]
        v_aug = [jnp.where(first, v, one), jnp.where(first, one, v)]
        return q_aug, k_aug, v_aug

    def write(pair, start, sums, tops):
        total = jnp.where(first, sums[1], sums[0])
        mixed = jnp.where(first, sums[0], sums[1]) * pltpu.roll(1.0 / total, HD, 1)
        mixed_ref[pair, start:start + STEP] = mixed.astype(jnp.bfloat16)
        level = jnp.log(total)
        if tops is not None:
            level = level + jnp.where(first, tops[1], tops[0])
        aux = lead
        for index, part in enumerate(thirds(-level)):
            aux = jnp.where(spare == index + 1, part, aux)
        aux_ref[pair, start:start + STEP] = aux

    @pl.when(calm[0] == 1)
    def _():
        ready = widen(0)
        for pair in range(group):
            q_aug, k_aug, v_aug = ready
            sums = [[None] * (rows // STEP) for _ in range(2)]
            for start in range(0, rows, STEP):
                stop = start + STEP
                for h in range(2):
                    s = nt(q_aug[h][start:], k_aug[h][start:stop])
                    w = jnp.exp(jnp.where(causal, s[:STEP], masked_value)).astype(jnp.bfloat16)
                    if stop < rows:
                        w = jnp.concatenate([w, jnp.exp(s[STEP:]).astype(jnp.bfloat16)], axis=0)
                    o = nn(w, v_aug[h][start:stop])
                    for part in range(start // STEP, rows // STEP):
                        add = o[part * STEP - start:(part + 1) * STEP - start]
                        sums[h][part] = add if start == 0 else sums[h][part] + add
                if start == 0 and pair + 1 < group:
                    ready = widen(pair + 1)
                write(pair, start, [sums[0][start // STEP], sums[1][start // STEP]], None)

    @pl.when(calm[0] == 0)
    def _():
        for pair in range(group):
            q_aug, k_aug, v_aug = widen(pair)
            for start in range(0, rows, STEP):
                stop = start + STEP
                sums, tops = [], []
                for h in range(2):
                    s = nt(q_aug[h][start:stop], k_aug[h][:stop])
                    edge = jnp.where(causal, s[:, start:], masked_value)
                    s = edge if start == 0 else jnp.concatenate([s[:, :start], edge], axis=1)
                    tops.append(jnp.max(s, axis=1, keepdims=True))
                    w = jnp.exp(s - tops[h]).astype(jnp.bfloat16)
                    sums.append(nn(w, v_aug[h][:stop]))
                write(pair, start, sums, tops)


def widen_backward(pair, extras, q_ref, k_ref, v_ref, mixed_ref, aux_ref, do_ref):
    one, zero = jnp.bfloat16(1), jnp.bfloat16(0)
    first, spare = in_first_head(), spare_lane()
    three = jnp.where(spare < 3, one, zero)
    row = lax.broadcasted_iota(jnp.int32, (LANES, LANES), 0) // HD
    column = lax.broadcasted_iota(jnp.int32, (LANES, LANES), 1) // HD
    cross = jnp.where(row != column, one, zero)
    q, k, v = q_ref[pair] * jnp.bfloat16(HD ** -0.5), k_ref[pair], v_ref[pair]
    do, aux = do_ref[pair], aux_ref[pair]
    k_aug = [jnp.where(first, k, extras), jnp.where(first, extras, k)]
    q_aug = [jnp.where(first, q, aux), jnp.where(first, aux, q)]
    v_aug = [jnp.where(first, v, three), jnp.where(first, three, v)]
    product = do.astype(jnp.float32) * mixed_ref[pair].astype(jnp.float32)
    high = product.astype(jnp.bfloat16)
    low = (product - high.astype(jnp.float32)).astype(jnp.bfloat16)
    delta = nn(high, cross) + nn(low, cross)
    extra = zero
    for index, part in enumerate(thirds(-delta)):
        extra = jnp.where(spare == index, part, extra)
    do_aug = [jnp.where(first, do, extra), jnp.where(first, extra, do)]
    return (q, do, *q_aug, *do_aug), (k, *k_aug, *v_aug)


def square_back(asking, asked, causal):
    q, do = asking[:2]
    k = asked[0]
    rows = q.shape[0]
    first = in_first_head()
    allowed = lax.broadcasted_iota(jnp.int32, (STEP, STEP), 0) <= lax.broadcasted_iota(jnp.int32, (STEP, STEP), 1)
    d_queries, d_keys, d_values = [None] * (rows // STEP), [], []
    for start in range(0, rows, STEP):
        stop = start + STEP
        begin = start if causal else 0
        dks, dvs, dqs = [], [], []
        for h in range(2):
            s = nt(asked[1 + h][start:stop], asking[2 + h][begin:])
            if causal:
                edge = jnp.where(allowed, s[:, :STEP], masked_value)
                s = edge if stop == rows else jnp.concatenate([edge, s[:, STEP:]], axis=1)
            p = jnp.exp(s)
            dp = nt(asked[3 + h][start:stop], asking[4 + h][begin:])
            ds = (p * dp).astype(jnp.bfloat16)
            dvs.append(nn(p.astype(jnp.bfloat16), do[begin:]))
            dks.append(nn(ds, q[begin:]))
            dqs.append(tn(ds, k[start:stop]))
        d_values.append(jnp.where(first, dvs[0], dvs[1]))
        d_keys.append(jnp.where(first, dks[0], dks[1]))
        dq = jnp.where(first, dqs[0], dqs[1])
        for part in range(begin // STEP, rows // STEP):
            add = dq[part * STEP - begin:(part + 1) * STEP - begin]
            d_queries[part] = add if d_queries[part] is None else d_queries[part] + add
    return [jnp.concatenate(parts, axis=0) for parts in (d_queries, d_keys, d_values)]


def far_back_kernel(place, qkv_ref, mixed_ref, aux_ref, do_ref, d_ref, kept_ref, other_ref):
    q_ref, k_ref, v_ref = (qkv_ref.at[part] for part in range(3))
    group, rows = q_ref.shape[:2]
    span = rows // 2
    low_far = place[1] == 0
    extras = key_extras(0, rows, place[3])
    ready = widen_backward(0, extras, q_ref, k_ref, v_ref, mixed_ref, aux_ref, do_ref)
    for pair in range(group):
        asking, asked = ready
        late = [x[span:] for x in asking]
        early = [x[:span] for x in asked]
        cross_q, cross_k, cross_v = square_back(late, early, False)
        if pair + 1 < group:
            ready = widen_backward(pair + 1, extras, q_ref, k_ref, v_ref, mixed_ref, aux_ref, do_ref)
        far_asking = [jnp.where(low_far, x[:span], x[span:]) for x in asking]
        far_asked = [jnp.where(low_far, x[:span], x[span:]) for x in asked]
        d_q, d_k, d_v = square_back(far_asking, far_asked, True)
        d_ref[0, pair] = ((d_q + jnp.where(low_far, 0.0, cross_q)) * HD ** -0.5).astype(jnp.bfloat16)
        d_ref[1, pair] = (d_k + jnp.where(low_far, cross_k, 0.0)).astype(jnp.bfloat16)
        d_ref[2, pair] = (d_v + jnp.where(low_far, cross_v, 0.0)).astype(jnp.bfloat16)
        kept_ref[pair] = jnp.where(low_far, cross_q, cross_k)
        other_ref[pair] = cross_v


def near_back_kernel(place, qkv_ref, mixed_ref, aux_ref, do_ref, kept_ref, other_ref, d_ref):
    q_ref, k_ref, v_ref = (qkv_ref.at[part] for part in range(3))
    group, span = q_ref.shape[:2]
    low_far = place[1] == 0
    extras = key_extras(place[2] * span, span, place[3])
    ready = widen_backward(0, extras, q_ref, k_ref, v_ref, mixed_ref, aux_ref, do_ref)
    for pair in range(group):
        asking, asked = ready
        d_q, d_k, d_v = square_back(asking, asked, True)
        if pair + 1 < group:
            ready = widen_backward(pair + 1, extras, q_ref, k_ref, v_ref, mixed_ref, aux_ref, do_ref)
        kept = kept_ref[pair]
        d_ref[0, pair] = ((d_q + jnp.where(low_far, kept, 0.0)) * HD ** -0.5).astype(jnp.bfloat16)
        d_ref[1, pair] = (d_k + jnp.where(low_far, 0.0, kept)).astype(jnp.bfloat16)
        d_ref[2, pair] = (d_v + jnp.where(low_far, 0.0, other_ref[pair])).astype(jnp.bfloat16)


def heads(rows, half=None):
    return pl.BlockSpec((GROUP, rows, LANES), lambda step, place: (step, 0 if half is None else place[half], 0))


def triple(rows, half=None):
    return pl.BlockSpec((3, GROUP, rows, LANES), lambda step, place: (0, step, 0 if half is None else place[half], 0))


def attention_forward(place, peaks, others, qkv):
    pairs, rows = qkv.shape[1:3]
    return pl.pallas_call(
        forward_kernel,
        grid_spec=pltpu.PrefetchScalarGridSpec(
            num_scalar_prefetch=1, grid=(pairs // GROUP,),
            in_specs=[held(peaks.shape)] * 2 + [triple(rows)],
            out_specs=[heads(rows)] * 2,
            scratch_shapes=[pltpu.SMEM((1,), jnp.int32)]),
        out_shape=[jax.ShapeDtypeStruct(qkv.shape[1:], jnp.bfloat16)] * 2,
        compiler_params=pltpu.CompilerParams(vmem_limit_bytes=VMEM),
        cost_estimate=pl.CostEstimate(flops=20 << 30, bytes_accessed=10 << 20, transcendentals=0),
        name="attention_forward",
    )(place, peaks, others, qkv)


def attention_backward_far(place, qkv, mixed, aux, d_mixed):
    pairs, rows = qkv.shape[1:3]
    span = rows // 2
    return pl.pallas_call(
        far_back_kernel,
        grid_spec=pltpu.PrefetchScalarGridSpec(
            num_scalar_prefetch=1, grid=(pairs // GROUP,),
            in_specs=[triple(rows)] + [heads(rows)] * 3,
            out_specs=[triple(span)] + [heads(span)] * 2),
        out_shape=[jax.ShapeDtypeStruct((3, pairs, span, LANES), jnp.bfloat16)] + [jax.ShapeDtypeStruct((pairs, span, LANES), jnp.float32)] * 2,
        compiler_params=pltpu.CompilerParams(vmem_limit_bytes=VMEM),
        cost_estimate=pl.CostEstimate(flops=30 << 30, bytes_accessed=20 << 20, transcendentals=0),
        name="attention_backward_far",
    )(place, qkv, mixed, aux, d_mixed)


def attention_backward_near(place, qkv, mixed, aux, d_mixed, kept, other):
    pairs, rows = qkv.shape[1:3]
    span = rows // 2
    return pl.pallas_call(
        near_back_kernel,
        grid_spec=pltpu.PrefetchScalarGridSpec(
            num_scalar_prefetch=1, grid=(pairs // GROUP,),
            in_specs=[triple(span, 2)] + [heads(span, 2)] * 3 + [heads(span)] * 2,
            out_specs=triple(span)),
        out_shape=jax.ShapeDtypeStruct((3, pairs, span, LANES), jnp.bfloat16),
        compiler_params=pltpu.CompilerParams(vmem_limit_bytes=VMEM),
        cost_estimate=pl.CostEstimate(flops=15 << 30, bytes_accessed=20 << 20, transcendentals=0),
        name="attention_backward_near",
    )(place, qkv, mixed, aux, d_mixed, kept, other)


def standardize(values):
    centred = values - jnp.mean(values, axis=-1, keepdims=True)
    inverse = lax.rsqrt(jnp.mean(centred * centred, axis=-1, keepdims=True) + epsilon)
    return centred * inverse, inverse


def pull_norm(grad, standard, inverse, gain):
    scaled = grad * gain
    centred = scaled - jnp.mean(scaled, axis=-1, keepdims=True)
    return inverse * (centred - standard * jnp.mean(scaled * standard, axis=-1, keepdims=True))


def side_by_side(ref, part):
    return jnp.concatenate([ref[pair, part] for pair in range(ref.shape[0])], axis=1)


def spread(ref, part, values):
    for pair in range(ref.shape[0]):
        ref[pair, part] = values[:, pair * LANES:(pair + 1) * LANES].astype(ref.dtype)


def held(shape):
    return pl.BlockSpec(shape, lambda step, place: (0,) * len(shape), pipeline_mode=pl.Buffered(1))


def deal_kernel(tokens, *refs):
    count = tokens.shape[0]
    blocks, held, semaphores = refs[:count], refs[count], refs[count + 1]
    me = lax.axis_index("blk")
    order = list(range(count // 2, count)) + list(range(count // 2))
    pulled = [pltpu.make_async_copy(tokens.at[me ^ index], held.at[index], semaphores.at[index]) for index in order]
    pushed = [pltpu.make_async_copy(held.at[index], blocks[index], semaphores.at[count + index]) for index in order]
    for move in pulled:
        move.start()
    for pull, push in zip(pulled, pushed):
        pull.wait()
        push.start()
    for move in pushed:
        move.wait()


def deal(tokens):
    count = tokens.shape[0]
    return pl.pallas_call(
        deal_kernel,
        in_specs=anywhere(1),
        out_specs=anywhere(count),
        out_shape=[jax.ShapeDtypeStruct(tokens.shape[1:], tokens.dtype)] * count,
        scratch_shapes=[pltpu.VMEM(tokens.shape, tokens.dtype), pltpu.SemaphoreType.DMA((2 * count,))],
        compiler_params=pltpu.CompilerParams(vmem_limit_bytes=VMEM),
        name="deal",
    )(tokens)


def gather_kernel(place, far, *refs):
    count = len(refs) - 4
    near, out, arrived, made, semaphores = refs[:count], refs[count], *refs[count + 1:]
    copy = copier(semaphores)
    slots, moves, sent = [], [], []
    for index in range(count):
        slots.append(place[1] * count + index)
        moves.append(copy(far.at[slots[-1]], arrived.at[index]))
    for index, block in enumerate(near):
        slots.append(place[0] ^ index)
        moves.append(copy(block, arrived.at[count + index]))
    for index, slot in enumerate(slots):
        moves[index].wait()
        made[index] = arrived[index].astype(made.dtype)
        sent.append(copy(made.at[index], out.at[slot]))
    for move in sent:
        move.wait()


def gather(place, far, near, dtype):
    return pl.pallas_call(
        gather_kernel,
        in_specs=[pl.BlockSpec(memory_space=pltpu.SMEM)] + anywhere(1 + len(near)),
        out_specs=anywhere(1)[0],
        out_shape=jax.ShapeDtypeStruct(far.shape, dtype),
        scratch_shapes=[pltpu.VMEM(far.shape, far.dtype), pltpu.VMEM(far.shape, dtype), pltpu.SemaphoreType.DMA((2 * far.shape[0],))],
        compiler_params=pltpu.CompilerParams(vmem_limit_bytes=VMEM),
        cost_estimate=pl.CostEstimate(flops=0, bytes_accessed=8 << 20, transcendentals=0),
        name="gather",
    )(place, far, *near)


def copier(semaphores):
    started = []

    def copy(source, target):
        move = pltpu.make_async_copy(source, target, semaphores.at[len(started)])
        started.append(move)
        move.start()
        return move

    return copy


def pieces_of(rows, size):
    return [slice(start, start + size) for start in range(0, rows, size)]


def anywhere(count):
    return [pl.BlockSpec(memory_space=pl.ANY)] * count


def project_kernel(half, count, place, vectors, factors, weight, *refs):
    blocks = refs[:count]
    qkv, lows, inner, peaks, token_buf, weight_buf, normed, qkv_buf, low_buf, semaphores = refs[-10:]
    copy = copier(semaphores)
    rows, width = blocks[0].shape
    span = rows * count
    mine = pl.ds(pl.multiple_of(place[half] * span, span), span)
    arrivals = []
    for index, block in enumerate(blocks):
        part = pl.ds(pl.multiple_of((place[0] % count ^ index) * rows, rows), rows)
        arrivals.append(copy(block, token_buf.at[part]))
    weights = [copy(weight.at[:, part], weight_buf.at[t]) for t, part in enumerate(pieces_of(weight.shape[1], width))]
    for arrival in arrivals:
        arrival.wait()
    sent = [copy(token_buf, inner.at[mine])]
    lane = lax.broadcasted_iota(jnp.int32, (width, LANES), 0) // HD
    each = jnp.where(lane == lax.broadcasted_iota(jnp.int32, (width, LANES), 1), 1.0, 0.0).astype(jnp.bfloat16)
    parts = pieces_of(span, STEP)
    for t, ready in enumerate(weights):
        ready.wait()
        for index, part in enumerate(parts):
            if t == 0:
                standard, _ = standardize(token_buf[part].astype(jnp.float32))
                normed[part] = (standard * vectors[GAIN:GAIN + 1] + vectors[SHIFT:SHIFT + 1]).astype(jnp.bfloat16)
                low_buf[part] = nt(normed[part], factors[:SMALL]).astype(jnp.bfloat16)
            values = nn(normed[part], weight_buf[t]) + vectors[JOINT + t:JOINT + t + 1]
            if t != 1:
                start = SMALL if t == 0 else 2 * SMALL
                values = values + nn(low_buf[part], factors[start:start + SMALL])
            values = values.astype(jnp.bfloat16)
            spread(qkv_buf.at[t], part, values)
            if t < 2:
                peak = jnp.max(nn(values * values, each).reshape(-1, 8, LANES), axis=0)
                peaks[t] = peak if index == 0 else jnp.maximum(peaks[t], peak)
        if t == 0:
            sent.append(copy(low_buf, lows.at[mine]))
        sent.append(copy(qkv_buf.at[t], qkv.at[t, :, mine]))
    for move in sent:
        move.wait()


def project(place, half, blocks, vectors, factors, weight, former):
    count = len(blocks)
    rows, width = blocks[0].shape
    parts, small = weight.shape[1] // width, SMALL
    span, pairs = count * rows, width // LANES
    return pl.pallas_call(
        partial(project_kernel, half, count),
        in_specs=[pl.BlockSpec(memory_space=pltpu.SMEM)] + [pl.BlockSpec(memory_space=pltpu.VMEM)] * 2 + anywhere(1 + count + len(former)),
        out_specs=anywhere(3) + [pl.BlockSpec(memory_space=pltpu.VMEM)],
        out_shape=[
            jax.ShapeDtypeStruct((parts, pairs, 2 * span, LANES), jnp.bfloat16),
            jax.ShapeDtypeStruct((2 * span, small), jnp.bfloat16),
            jax.ShapeDtypeStruct((2 * span, width), jnp.bfloat16),
            jax.ShapeDtypeStruct((2, 8, LANES), jnp.float32),
        ],
        scratch_shapes=[
            pltpu.VMEM((span, width), jnp.bfloat16),
            pltpu.VMEM((parts, width, width), jnp.bfloat16),
            pltpu.VMEM((span, width), jnp.bfloat16),
            pltpu.VMEM((parts, pairs, span, LANES), jnp.bfloat16),
            pltpu.VMEM((span, small), jnp.bfloat16),
            pltpu.SemaphoreType.DMA((count + 2 * parts + 2,)),
        ],
        input_output_aliases={count + 4 + index: index for index in range(len(former))},
        compiler_params=pltpu.CompilerParams(vmem_limit_bytes=VMEM),
        cost_estimate=pl.CostEstimate(flops=2 * span * width * width * parts, bytes_accessed=6 * width * width * 2, transcendentals=0),
        name="project",
    )(place, vectors, factors, weight, *blocks, *former)


def gelu_and_slope(u):
    c = (2.0 / jnp.pi) ** 0.5
    square = u * u
    share = 0.5 + 0.5 * jnp.tanh(u * (c + (c * 0.044715) * square))
    value = u * share
    slope = share + value * (1.0 - share) * (2 * c + (6 * c * 0.044715) * square)
    return value, slope


def feed_kernel(vectors, tokens, mixed, out_weight, up, down, result, middle, slopes, token_buf, mixed_buf, out_buf, up_buf, down_buf, middle_buf, slope_buf, active, result_buf, semaphores):
    copy = copier(semaphores)
    width = out_weight.shape[0]
    parts = pieces_of(tokens.shape[0], CHUNK)
    columns = pieces_of(up.shape[1], width)
    fetched = [copy(out_weight, out_buf), copy(mixed, mixed_buf), copy(tokens, token_buf)]
    ups = [copy(up.at[:, column], up_buf.at[t]) for t, column in enumerate(columns)]
    downs = copy(down, down_buf)
    for ready in fetched:
        ready.wait()
    sent = []
    for index, part in enumerate(parts):
        m = token_buf[part].astype(jnp.float32) + nn(side_by_side(mixed_buf, part), out_buf[...]) + vectors[OUT:OUT + 1]
        middle_buf[part] = m
        sent.append(copy(middle_buf.at[part], middle.at[part]))
        standard, _ = standardize(m)
        normed = (standard * vectors[GAIN_TWO:GAIN_TWO + 1] + vectors[SHIFT_TWO:SHIFT_TWO + 1]).astype(jnp.bfloat16)
        for t, column in enumerate(columns):
            if index == 0:
                ups[t].wait()
            value, slope = gelu_and_slope(nn(normed, up_buf[t]) + vectors[UP + t:UP + t + 1])
            slope_buf[part, column] = slope.astype(jnp.bfloat16)
            active[:, column] = value.astype(jnp.bfloat16)
        sent.append(copy(slope_buf.at[part], slopes.at[part]))
        if index == 0:
            downs.wait()
        result_buf[part] = (middle_buf[part] + vectors[DOWN:DOWN + 1] + nn(active[...], down_buf[...])).astype(jnp.bfloat16)
        sent.append(copy(result_buf.at[part], result.at[part]))
    for move in sent:
        move.wait()


def feed(tokens, mixed, vectors, out_weight, up, down):
    rows, width = tokens.shape
    wide = up.shape[1]
    return pl.pallas_call(
        feed_kernel,
        in_specs=[pl.BlockSpec(memory_space=pltpu.VMEM)] + anywhere(5),
        out_specs=anywhere(3),
        out_shape=[
            jax.ShapeDtypeStruct((rows, width), jnp.bfloat16),
            jax.ShapeDtypeStruct((rows, width), jnp.float32),
            jax.ShapeDtypeStruct((rows, wide), jnp.bfloat16),
        ],
        scratch_shapes=[
            pltpu.VMEM((rows, width), jnp.bfloat16),
            pltpu.VMEM(mixed.shape, jnp.bfloat16),
            pltpu.VMEM((width, width), jnp.bfloat16),
            pltpu.VMEM((wide // width, width, width), jnp.bfloat16),
            pltpu.VMEM((wide, width), jnp.bfloat16),
            pltpu.VMEM((rows, width), jnp.float32),
            pltpu.VMEM((rows, wide), jnp.bfloat16),
            pltpu.VMEM((CHUNK, wide), jnp.bfloat16),
            pltpu.VMEM((rows, width), jnp.bfloat16),
            pltpu.SemaphoreType.DMA((4 + wide // width + 3 * (rows // CHUNK),)),
        ],
        compiler_params=pltpu.CompilerParams(vmem_limit_bytes=VMEM),
        cost_estimate=pl.CostEstimate(flops=2 * rows * width * (width + 2 * wide), bytes_accessed=40 << 20, transcendentals=rows * wide),
        name="feed",
    )(vectors, tokens, mixed, out_weight, up, down)


def feed_back_kernel(vectors, outer, slopes, up, down, middle, out_weight, d_middle, d_mixed, outer_buf, slope_buf, up_buf, down_buf, middle_buf, out_buf, hidden, mixed_buf, semaphores):
    copy = copier(semaphores)
    width = out_weight.shape[0]
    parts = pieces_of(outer.shape[0], CHUNK)
    columns = pieces_of(up.shape[1], width)
    outer_ready = copy(outer, outer_buf)
    downs, slants = [], []
    for t, column in enumerate(columns):
        downs.append(copy(down.at[column], down_buf.at[column]))
        slants.append(copy(slopes.at[:, column], slope_buf.at[:, column]))
    late = [copy(up, up_buf), copy(middle, middle_buf), copy(out_weight, out_buf)]
    outer_ready.wait()
    sent = []
    for index, part in enumerate(parts):
        for t, column in enumerate(columns):
            if index == 0:
                downs[t].wait()
                slants[t].wait()
            d_active = nt(outer_buf[part], down_buf[column])
            hidden[:, column] = (d_active * slope_buf[part, column].astype(jnp.float32)).astype(jnp.bfloat16)
        if index == 0:
            for ready in late:
                ready.wait()
        grad = nt(hidden[...], up_buf[...])
        standard, inverse = standardize(middle_buf[part])
        d = outer_buf[part].astype(jnp.float32) + pull_norm(grad, standard, inverse, vectors[GAIN_TWO:GAIN_TWO + 1])
        middle_buf[part] = d
        sent.append(copy(middle_buf.at[part], d_middle.at[part]))
        spread(mixed_buf, part, nt(d.astype(jnp.bfloat16), out_buf[...]))
        sent.append(copy(mixed_buf.at[:, part], d_mixed.at[:, part]))
    for move in sent:
        move.wait()


def feed_back(outer, slopes, up, down, middle, vectors, out_weight):
    rows, width = outer.shape
    wide = up.shape[1]
    pairs = width // LANES
    return pl.pallas_call(
        feed_back_kernel,
        in_specs=[pl.BlockSpec(memory_space=pltpu.VMEM)] + anywhere(6),
        out_specs=anywhere(2),
        out_shape=[jax.ShapeDtypeStruct((rows, width), jnp.float32), jax.ShapeDtypeStruct((pairs, rows, LANES), jnp.bfloat16)],
        scratch_shapes=[
            pltpu.VMEM((rows, width), jnp.bfloat16),
            pltpu.VMEM((rows, wide), jnp.bfloat16),
            pltpu.VMEM((width, wide), jnp.bfloat16),
            pltpu.VMEM((wide, width), jnp.bfloat16),
            pltpu.VMEM((rows, width), jnp.float32),
            pltpu.VMEM((width, width), jnp.bfloat16),
            pltpu.VMEM((CHUNK, wide), jnp.bfloat16),
            pltpu.VMEM((pairs, rows, LANES), jnp.bfloat16),
            pltpu.SemaphoreType.DMA((4 + 2 * (wide // width) + 2 * (rows // CHUNK),)),
        ],
        compiler_params=pltpu.CompilerParams(vmem_limit_bytes=VMEM),
        cost_estimate=pl.CostEstimate(flops=2 * rows * width * (width + 2 * wide), bytes_accessed=40 << 20, transcendentals=0),
        name="feed_back",
    )(vectors, outer, slopes, up, down, middle, out_weight)


def finish_kernel(half, count, place, vectors, factors, former, d_qkv, inner, d_middle, lows, weight, *refs):
    carried, refs = (refs[:1], refs[1:]) if half == 2 else ((), refs)
    summed, refs = refs[0], refs[1:]
    landed, refs = (refs[:1], refs[1:]) if half == 2 else ((), refs)
    blocks, refs = refs[:count if half == 2 else 1], refs[count if half == 2 else 1:]
    d_buf, weight_buf, token_buf, middle_buf, low_buf, normed, grad_buf, semaphores, *held = refs
    copy = copier(semaphores)
    span, width = token_buf.shape
    rows = span // count
    mine = pl.ds(pl.multiple_of(place[half] * span, span), span)
    pulls, weights = [], []
    for t, columns in enumerate(pieces_of(weight.shape[1], width)):
        pulls.append(copy(d_qkv.at[t], d_buf.at[t]))
        weights.append(copy(weight.at[:, columns], weight_buf.at[t]))
        if t == 0:
            late = [copy(inner.at[mine], token_buf), copy(lows.at[mine], low_buf)]
    late.append(copy(d_middle.at[mine], middle_buf))
    late.extend(copy(source, target) for source, target in zip(carried, held))
    gain = vectors[GAIN:GAIN + 1]
    parts = pieces_of(span, STEP)
    totals, smalls = [None] * len(parts), [None] * len(parts)
    for t in range(len(weights)):
        pulls[t].wait()
        weights[t].wait()
        for index, part in enumerate(parts):
            d_here = side_by_side(d_buf.at[t], part)
            grad = nt(d_here, weight_buf[t])
            totals[index] = grad if t == 0 else totals[index] + grad
            if t != 1:
                low = nt(d_here, factors[SMALL:2 * SMALL] if t == 0 else factors[2 * SMALL:])
                smalls[index] = low if t == 0 else smalls[index] + low
    for ready in late:
        ready.wait()
    sent = [copy(source, target) for source, target in zip(held, landed)]
    for index, part in enumerate(parts):
        small = smalls[index].astype(jnp.bfloat16)
        standard, inverse = standardize(token_buf[part].astype(jnp.float32))
        normed[part] = (standard * gain + vectors[SHIFT:SHIFT + 1]).astype(jnp.bfloat16)
        d_normed = totals[index] + nn(small, factors[:SMALL])
        grad_buf[part] = (middle_buf[part] + pull_norm(d_normed, standard, inverse, gain)).astype(grad_buf.dtype)
        smalls[index] = small
    if len(blocks) == 1:
        sent.append(copy(grad_buf, blocks[0].at[mine]))
    else:
        for index, block in enumerate(blocks):
            part = pl.ds(pl.multiple_of((place[0] % count ^ index) * rows, rows), rows)
            sent.append(copy(grad_buf.at[part], block))
    everything = slice(None)
    scale = 32.0 / RANK
    summed[:2 * RANK] = former[:2 * RANK] + tn(jnp.concatenate(smalls, axis=0), normed[...])[:2 * RANK]
    summed[2 * RANK:] = former[2 * RANK:] + scale * jnp.concatenate(
        (tn(low_buf[...], side_by_side(d_buf.at[0], everything))[:RANK], tn(low_buf[...], side_by_side(d_buf.at[2], everything))[RANK:2 * RANK])
    )
    for move in sent:
        move.wait()


def finish(place, half, count, d_qkv, inner, d_middle, lows, vectors, factors, weight, former, carried=()):
    parts, pairs, span = d_qkv.shape[:3]
    small, width = SMALL, inner.shape[1]
    rows = span // count
    outs = [(2 * span, width)] if half == 1 else [(rows, width)] * count
    return pl.pallas_call(
        partial(finish_kernel, half, count),
        in_specs=[pl.BlockSpec(memory_space=pltpu.SMEM)] + [pl.BlockSpec(memory_space=pltpu.VMEM)] * 3 + anywhere(5 + len(carried)),
        out_specs=[pl.BlockSpec(memory_space=pltpu.VMEM)] + anywhere(len(carried) + len(outs)),
        out_shape=[jax.ShapeDtypeStruct((4 * RANK, width), jnp.float32)] + [jax.ShapeDtypeStruct(x.shape, x.dtype) for x in carried] + [jax.ShapeDtypeStruct(out, jnp.bfloat16) for out in outs],
        scratch_shapes=[
            pltpu.VMEM((parts, pairs, span, LANES), jnp.bfloat16),
            pltpu.VMEM((parts, width, width), jnp.bfloat16),
            pltpu.VMEM((span, width), jnp.bfloat16),
            pltpu.VMEM((span, width), jnp.float32),
            pltpu.VMEM((span, small), jnp.bfloat16),
            pltpu.VMEM((span, width), jnp.bfloat16),
            pltpu.VMEM((span, width), jnp.bfloat16),
            pltpu.SemaphoreType.DMA((2 * parts + 5 + count,)),
        ] + [pltpu.VMEM(x.shape, x.dtype) for x in carried],
        compiler_params=pltpu.CompilerParams(vmem_limit_bytes=VMEM),
        cost_estimate=pl.CostEstimate(flops=2 * span * width * width * parts, bytes_accessed=12 << 20, transcendentals=0),
        name="finish",
    )(place, vectors, factors, former, d_qkv, inner, d_middle, lows, weight, *carried)


def sum_over(v, axis):
    size = lax.axis_size(axis)
    if size & (size - 1):
        return lax.psum(v, axis)
    step = 1
    while step < size:
        v = v + lax.ppermute(v, axis, [(i, i ^ step) for i in range(size)])
        step *= 2
    return v


def whole_slots(
    tokens,
    lengths,
    norm_gain,
    norm_shift,
    joint_weight,
    query_bias,
    value_bias,
    output_weight,
    output_bias,
    second_gain,
    second_shift,
    upward_weight,
    upward_bias,
    down_weight,
    down_bias,
    query_down,
    query_up,
    value_down,
    value_up,
    cotangent,
):
    seqs_here, rows, width = tokens.shape
    ranks = lax.axis_size("blk")
    half = ranks // 2
    adapter = 32.0 / RANK

    def partner(index):
        return [(i, i ^ index) for i in range(ranks)]

    me = lax.axis_index("blk")
    side = me // half
    place = jnp.stack((me, 1 - side, side, lengths[me])).astype(jnp.int32)
    vectors = jnp.concatenate(
        (
            norm_gain,
            norm_shift,
            query_bias,
            jnp.zeros_like(query_bias),
            value_bias,
            output_bias,
            second_gain,
            second_shift,
            down_bias,
            upward_bias,
        )
    )
    vectors = vectors.astype(jnp.float32).reshape(-1, width)
    factors = jnp.concatenate(
        (
            jnp.pad(jnp.concatenate((query_down, value_down), axis=1).T, ((0, 2 * RANK), (0, 0))),
            jnp.pad(adapter * query_up, ((0, 3 * RANK), (0, 0))).astype(jnp.bfloat16),
            jnp.pad(adapter * value_up, ((RANK, 2 * RANK), (0, 0))).astype(jnp.bfloat16),
        )
    )
    own, *others = deal(tokens)
    far = [lax.ppermute(others[k - 1], "blk", partner(k)) for k in range(half, ranks)]
    near = [own] + [lax.ppermute(others[k - 1], "blk", partner(k)) for k in range(1, half)]
    *former, near_peaks = project(place, 2, near, vectors, factors, joint_weight, ())
    cotangent, far, *_ = lax.optimization_barrier((cotangent, far, near_peaks))
    outer = lax.all_to_all(cotangent, "blk", 0, 0, tiled=True).reshape(-1, width)
    qkv, lows, inner, far_peaks = project(
        place, 1, far, vectors, factors, joint_weight, former
    )
    mixed, aux = attention_forward(place, near_peaks, far_peaks, qkv)
    result, middle, slopes = feed(
        inner, mixed, vectors, output_weight, upward_weight, down_weight
    )
    result, middle, slopes, outer = lax.optimization_barrier((result, middle, slopes, outer))
    block_output = lax.all_to_all(
        result.reshape(ranks, rows, width), "blk", 0, 0, tiled=True
    )
    d_middle, d_mixed = feed_back(
        outer, slopes, upward_weight, down_weight, middle, vectors, output_weight
    )
    d_far, kept, other = attention_backward_far(place, qkv, mixed, aux, d_mixed)
    shared = (inner, d_middle, lows, vectors, factors, joint_weight)
    nothing = jnp.zeros((4 * RANK, width), jnp.float32)
    far_factors, far_grads = finish(place, 1, half, d_far, *shared, nothing)
    far_grads = lax.all_to_all(far_grads.reshape(ranks, rows, width), "blk", 0, 0, tiled=True)
    d_near = attention_backward_near(place, qkv, mixed, aux, d_mixed, kept, other)
    packed, block_output, *near_grads = finish(
        place, 2, half, d_near, *shared, far_factors, (block_output,)
    )
    near_grads = near_grads[:1] + [
        lax.ppermute(near_grads[k], "blk", partner(k)) for k in range(1, half)
    ]
    packed, near_grads = lax.optimization_barrier((sum_over(packed, "batch"), near_grads))
    packed = sum_over(packed, "blk")
    token_grads = gather(place, far_grads, near_grads, jnp.float32)
    query_down_grad, value_down_grad = packed[:RANK].T, packed[RANK : 2 * RANK].T
    query_up_grad, value_up_grad = packed[2 * RANK : 3 * RANK], packed[3 * RANK :]
    return (
        block_output,
        token_grads,
        query_down_grad,
        query_up_grad,
        value_down_grad,
        value_up_grad,
    )


def body(
    tokens,
    lengths,
    norm_gain,
    norm_shift,
    joint_weight,
    query_bias,
    value_bias,
    output_weight,
    output_bias,
    second_gain,
    second_shift,
    upward_weight,
    upward_bias,
    down_weight,
    down_bias,
    query_down,
    query_up,
    value_down,
    value_up,
    cotangent,
):
    seqs_here, rows, width = tokens.shape
    heads = width // HD
    positions = seqs_here * rows
    length_all = rows * lax.axis_size("blk")
    scale = HD ** (-0.5)
    adapter = 32.0 / RANK
    flat = tokens.reshape(positions, width).astype(jnp.float32)
    normed_full, standard, inverse = normalize(flat, norm_gain, norm_shift)
    normed = normed_full.astype(jnp.bfloat16)
    joint = jnp.dot(normed, joint_weight, preferred_element_type=jnp.float32)
    query_low = jnp.dot(normed, query_down, preferred_element_type=jnp.float32).astype(jnp.bfloat16)
    value_low = jnp.dot(normed, value_down, preferred_element_type=jnp.float32).astype(jnp.bfloat16)
    queries = (
        joint[:, :width]
        + query_bias.astype(jnp.float32)
        + adapter * jnp.dot(query_low, query_up, preferred_element_type=jnp.float32)
    ).astype(jnp.bfloat16)
    keys_here = joint[:, width : 2 * width].astype(jnp.bfloat16)
    values_here = (
        joint[:, 2 * width :]
        + value_bias.astype(jnp.float32)
        + adapter * jnp.dot(value_low, value_up, preferred_element_type=jnp.float32)
    ).astype(jnp.bfloat16)
    query_heads = queries.reshape(seqs_here, rows, heads, HD)
    key_blocks = keys_here.reshape(seqs_here, rows, width)
    value_blocks = values_here.reshape(seqs_here, rows, width)
    device = lax.axis_index("blk")
    query_place = device * rows + jnp.arange(rows, dtype=jnp.int32)
    limits = lengths[:, None, None, None]

    def visible(query_pos, key_pos):
        return (key_pos[None, None, None, :] <= query_pos[None, None, :, None]) & (
            key_pos[None, None, None, :] < limits
        )

    running = jnp.full((seqs_here, heads, rows), masked_value, jnp.float32)
    key_piece = lax.all_gather(key_blocks, "blk", axis=1, tiled=True)
    value_piece = lax.all_gather(value_blocks, "blk", axis=1, tiled=True)
    count = key_piece.shape[1]
    key_heads = key_piece.reshape(seqs_here, count, heads, HD)
    value_heads = value_piece.reshape(seqs_here, count, heads, HD)
    allowed = visible(query_place, jnp.arange(count, dtype=jnp.int32))
    scores = (
        jnp.einsum("sqhd,skhd->shqk", query_heads, key_heads, preferred_element_type=jnp.float32)
        * scale
    )
    masked = jnp.where(allowed, scores, masked_value)
    highest = jnp.maximum(running, jnp.max(masked, axis=-1))
    weights = jnp.where(allowed, jnp.exp(masked - highest[..., None]), 0.0)
    totals = jnp.sum(weights, axis=-1)
    update = jnp.einsum(
        "shqk,skhd->sqhd",
        weights.astype(jnp.bfloat16),
        value_heads,
        preferred_element_type=jnp.float32,
    )
    summed = update
    running, totals, summed = (highest, totals, summed)
    mixed_full = summed / jnp.transpose(totals, (0, 2, 1))[..., None]
    log_total = running + jnp.log(totals)
    mixed_low = mixed_full.reshape(positions, width).astype(jnp.bfloat16)
    middle = (
        flat
        + jnp.dot(mixed_low, output_weight, preferred_element_type=jnp.float32)
        + output_bias.astype(jnp.float32)
    )
    normed_two_full, standard_two, inverse_two = normalize(middle, second_gain, second_shift)
    normed_two = normed_two_full.astype(jnp.bfloat16)
    hidden = jnp.dot(
        normed_two, upward_weight, preferred_element_type=jnp.float32
    ) + upward_bias.astype(jnp.float32)
    active_full, gelu_pull = jax.vjp(partial(jax.nn.gelu, approximate=True), hidden)
    active = active_full.astype(jnp.bfloat16)
    block_output = (
        (
            middle
            + jnp.dot(active, down_weight, preferred_element_type=jnp.float32)
            + down_bias.astype(jnp.float32)
        )
        .astype(jnp.bfloat16)
        .reshape(seqs_here, rows, width)
    )
    outer = cotangent.reshape(positions, width)
    d_active = against(outer, down_weight)
    d_hidden = gelu_pull(d_active)[0].astype(jnp.bfloat16)
    d_normed_two = against(d_hidden, upward_weight)
    d_middle = outer.astype(jnp.float32) + norm_back(
        d_normed_two, standard_two, inverse_two, second_gain
    )
    d_branch = d_middle.astype(jnp.bfloat16)
    d_mixed = against(d_branch, output_weight).astype(jnp.bfloat16)
    d_mixed_heads = d_mixed.reshape(seqs_here, rows, heads, HD)
    delta = jnp.transpose(
        jnp.sum(d_mixed_heads.astype(jnp.float32) * mixed_full, axis=-1), (0, 2, 1)
    )
    key_all, value_all = (
        lax.all_gather(key_blocks, "blk", axis=1, tiled=True),
        lax.all_gather(value_blocks, "blk", axis=1, tiled=True),
    )
    key_heads_all = key_all.reshape(seqs_here, length_all, heads, HD)
    value_heads_all = value_all.reshape(seqs_here, length_all, heads, HD)
    allowed_all = visible(query_place, jnp.arange(length_all, dtype=jnp.int32))
    scores = (
        jnp.einsum(
            "sqhd,skhd->shqk", query_heads, key_heads_all, preferred_element_type=jnp.float32
        )
        * scale
    )
    probs = jnp.where(allowed_all, jnp.exp(scores - log_total[..., None]), 0.0)
    d_probs = jnp.einsum(
        "sqhd,skhd->shqk", d_mixed_heads, value_heads_all, preferred_element_type=jnp.float32
    )
    d_scores = (probs * (d_probs - delta[..., None])).astype(jnp.bfloat16)
    d_queries = (
        jnp.einsum("shqk,skhd->sqhd", d_scores, key_heads_all, preferred_element_type=jnp.float32)
        * scale
    )
    d_keys_all = (
        jnp.einsum("shqk,sqhd->kshd", d_scores, query_heads, preferred_element_type=jnp.float32)
        * scale
    )
    d_values_all = jnp.einsum(
        "shqk,sqhd->kshd",
        probs.astype(jnp.bfloat16),
        d_mixed_heads,
        preferred_element_type=jnp.float32,
    )
    stacked = jnp.stack(
        (
            d_keys_all.reshape(length_all, seqs_here, width),
            d_values_all.reshape(length_all, seqs_here, width),
        ),
        axis=2,
    )
    owned = lax.psum_scatter(
        stacked.astype(jnp.bfloat16), "blk", scatter_dimension=0, tiled=True
    ).astype(jnp.float32)
    d_keys = jnp.transpose(owned[:, :, 0], (1, 0, 2)).reshape(positions, width)
    d_values = jnp.transpose(owned[:, :, 1], (1, 0, 2)).reshape(positions, width)
    d_query_low = d_queries.reshape(positions, width).astype(jnp.bfloat16)
    d_key_low = d_keys.astype(jnp.bfloat16)
    d_value_low = d_values.astype(jnp.bfloat16)
    query_up_grad = adapter * transposed(query_low, d_query_low)
    value_up_grad = adapter * transposed(value_low, d_value_low)
    d_query_small = (adapter * against(d_query_low, query_up)).astype(jnp.bfloat16)
    d_value_small = (adapter * against(d_value_low, value_up)).astype(jnp.bfloat16)
    query_down_grad = transposed(normed, d_query_small)
    value_down_grad = transposed(normed, d_value_small)
    d_joint = jnp.concatenate((d_query_low, d_key_low, d_value_low), axis=1)
    d_normed = (
        against(d_joint, joint_weight)
        + against(d_query_small, query_down)
        + against(d_value_small, value_down)
    )
    token_grads = (d_middle + norm_back(d_normed, standard, inverse, norm_gain)).reshape(
        seqs_here, rows, width
    )
    sums = lax.psum(
        (query_down_grad, query_up_grad, value_down_grad, value_up_grad), ("batch", "blk")
    )
    return (block_output, token_grads, sums[0], sums[1], sums[2], sums[3])


def choose(tokens, *others):
    seqs, rows = tokens.shape[:2]
    ranks = lax.axis_size("blk")
    fits = seqs == ranks and ranks > 1 and not ranks & (ranks - 1)
    fits = fits and rows % LANES == 0 and (ranks // 2 * rows) % CHUNK == 0
    return (whole_slots if fits else body)(tokens, *others)


def solution(mesh):
    placed = (
        P("batch", "blk", None),
        P("batch"),
        P(),
        P(),
        P(),
        P(),
        P(),
        P(),
        P(),
        P(),
        P(),
        P(),
        P(),
        P(),
        P(),
        P(),
        P(),
        P(),
        P(),
        P("batch", "blk", None),
    )
    return jax.shard_map(
        choose,
        mesh=mesh,
        in_specs=placed,
        out_specs=(P("batch", "blk", None), P("batch", "blk", None), P(), P(), P(), P()),
        check_vma=False,
    )
```

```python
from functools import partial

import jax
import jax.numpy as jnp
from jax import lax
from jax.experimental import pallas as pl
from jax.experimental.pallas import tpu as pltpu
from jax.sharding import PartitionSpec as P

HD = 64
RANK = 4
LANES = 128
STEP = 256
SAFE = 80.0
GROUP = 2
CHUNK = 512
TILE = 1024
VMEM = 62 << 20
GAIN = 0
SHIFT = 1
JOINT = 2
OUT = 5
GAIN_TWO = 6
SHIFT_TWO = 7
DOWN = 8
UP = 9
SMALL = 16


epsilon = 1e-05
masked_value = -1e30


def normalize(values, gain, shift):
    centred = values - jnp.mean(values, axis=-1, keepdims=True)
    inverse = lax.rsqrt(jnp.mean(centred * centred, axis=-1, keepdims=True) + epsilon)
    standard = centred * inverse
    return (standard * gain.astype(jnp.float32) + shift.astype(jnp.float32), standard, inverse)


def norm_back(grad, standard, inverse, gain):
    scaled = grad * gain.astype(jnp.float32)
    centred = scaled - jnp.mean(scaled, axis=-1, keepdims=True)
    return inverse * (centred - standard * jnp.mean(scaled * standard, axis=-1, keepdims=True))


def transposed(left, right):
    return lax.dot_general(
        left, right, (((0,), (0,)), ((), ())), preferred_element_type=jnp.float32
    )


def against(left, right):
    return lax.dot_general(
        left, right, (((1,), (1,)), ((), ())), preferred_element_type=jnp.float32
    )


def nt(a, b):
    return lax.dot_general(a, b, (((1,), (1,)), ((), ())), preferred_element_type=jnp.float32)


def tn(a, b):
    return lax.dot_general(a, b, (((0,), (0,)), ((), ())), preferred_element_type=jnp.float32)


def nn(a, b):
    return jnp.dot(a, b, preferred_element_type=jnp.float32)


def thirds(x):
    first = x.astype(jnp.bfloat16)
    rest = x - first.astype(jnp.float32)
    second = rest.astype(jnp.bfloat16)
    third = (rest - second.astype(jnp.float32)).astype(jnp.bfloat16)
    return first, second, third


def in_first_head():
    return lax.broadcasted_iota(jnp.int32, (1, LANES), 1) < HD


def spare_lane():
    return lax.broadcasted_iota(jnp.int32, (1, LANES), 1) % HD


def key_extras(begin, rows, length):
    place = begin + lax.broadcasted_iota(jnp.int32, (rows, LANES), 0)
    bias = jnp.where(place < length, 0.0, masked_value).astype(jnp.bfloat16)
    spare = spare_lane()
    return jnp.where(spare == 0, bias, jnp.where(spare < 4, jnp.bfloat16(1), jnp.bfloat16(0)))


def attend_forward(base, group, calm, length, qkv, mixed_ref, aux_ref):
    q_ref, k_ref, v_ref = (qkv.at[part] for part in range(3))
    rows = q_ref.shape[1]
    one, zero = jnp.bfloat16(1), jnp.bfloat16(0)
    first, spare = in_first_head(), spare_lane()
    extras = key_extras(0, rows, length)
    lead = jnp.where(spare == 0, one, zero)
    causal = lax.broadcasted_iota(jnp.int32, (STEP, STEP), 1) <= lax.broadcasted_iota(jnp.int32, (STEP, STEP), 0)

    def widen(pair):
        q, k, v = q_ref[base + pair] * jnp.bfloat16(HD ** -0.5), k_ref[base + pair], v_ref[base + pair]
        q_aug = [jnp.where(first, q, lead), jnp.where(first, lead, q)]
        k_aug = [jnp.where(first, k, extras), jnp.where(first, extras, k)]
        v_aug = [jnp.where(first, v, one), jnp.where(first, one, v)]
        return q_aug, k_aug, v_aug

    def write(pair, start, sums, tops):
        total = jnp.where(first, sums[1], sums[0])
        mixed = jnp.where(first, sums[0], sums[1]) * pltpu.roll(1.0 / total, HD, 1)
        mixed_ref[base + pair, start:start + STEP] = mixed.astype(jnp.bfloat16)
        level = jnp.log(total)
        if tops is not None:
            level = level + jnp.where(first, tops[1], tops[0])
        aux = lead
        for index, part in enumerate(thirds(-level)):
            aux = jnp.where(spare == index + 1, part, aux)
        aux_ref[base + pair, start:start + STEP] = aux

    @pl.when(calm)
    def _():
        ready = widen(0)
        for pair in range(group):
            q_aug, k_aug, v_aug = ready
            sums = [[None] * (rows // STEP) for _ in range(2)]
            for start in range(0, rows, STEP):
                stop = start + STEP
                for h in range(2):
                    s = nt(q_aug[h][start:], k_aug[h][start:stop])
                    w = jnp.exp(jnp.where(causal, s[:STEP], masked_value)).astype(jnp.bfloat16)
                    if stop < rows:
                        w = jnp.concatenate([w, jnp.exp(s[STEP:]).astype(jnp.bfloat16)], axis=0)
                    o = nn(w, v_aug[h][start:stop])
                    for part in range(start // STEP, rows // STEP):
                        add = o[part * STEP - start:(part + 1) * STEP - start]
                        sums[h][part] = add if start == 0 else sums[h][part] + add
                if start == 0 and pair + 1 < group:
                    ready = widen(pair + 1)
                write(pair, start, [sums[0][start // STEP], sums[1][start // STEP]], None)

    @pl.when(jnp.logical_not(calm))
    def _():
        for pair in range(group):
            q_aug, k_aug, v_aug = widen(pair)
            for start in range(0, rows, STEP):
                stop = start + STEP
                sums, tops = [], []
                for h in range(2):
                    s = nt(q_aug[h][start:stop], k_aug[h][:stop])
                    edge = jnp.where(causal, s[:, start:], masked_value)
                    s = edge if start == 0 else jnp.concatenate([s[:, :start], edge], axis=1)
                    tops.append(jnp.max(s, axis=1, keepdims=True))
                    w = jnp.exp(s - tops[h]).astype(jnp.bfloat16)
                    sums.append(nn(w, v_aug[h][:stop]))
                write(pair, start, sums, tops)


def widen_backward(pair, extras, q_ref, k_ref, v_ref, mixed_ref, aux_ref, do_ref):
    one, zero = jnp.bfloat16(1), jnp.bfloat16(0)
    first, spare = in_first_head(), spare_lane()
    three = jnp.where(spare < 3, one, zero)
    row = lax.broadcasted_iota(jnp.int32, (LANES, LANES), 0) // HD
    column = lax.broadcasted_iota(jnp.int32, (LANES, LANES), 1) // HD
    cross = jnp.where(row != column, one, zero)
    q, k, v = q_ref[pair] * jnp.bfloat16(HD ** -0.5), k_ref[pair], v_ref[pair]
    do, aux = do_ref[pair], aux_ref[pair]
    k_aug = [jnp.where(first, k, extras), jnp.where(first, extras, k)]
    q_aug = [jnp.where(first, q, aux), jnp.where(first, aux, q)]
    v_aug = [jnp.where(first, v, three), jnp.where(first, three, v)]
    product = do.astype(jnp.float32) * mixed_ref[pair].astype(jnp.float32)
    high = product.astype(jnp.bfloat16)
    low = (product - high.astype(jnp.float32)).astype(jnp.bfloat16)
    delta = nn(high, cross) + nn(low, cross)
    extra = zero
    for index, part in enumerate(thirds(-delta)):
        extra = jnp.where(spare == index, part, extra)
    do_aug = [jnp.where(first, do, extra), jnp.where(first, extra, do)]
    return (q, do, *q_aug, *do_aug), (k, *k_aug, *v_aug)


def square_back(asking, asked, causal):
    q, do = asking[:2]
    k = asked[0]
    rows = q.shape[0]
    first = in_first_head()
    allowed = lax.broadcasted_iota(jnp.int32, (STEP, STEP), 0) <= lax.broadcasted_iota(jnp.int32, (STEP, STEP), 1)
    d_queries, d_keys, d_values = [None] * (rows // STEP), [], []
    for start in range(0, rows, STEP):
        stop = start + STEP
        begin = start if causal else 0
        dks, dvs, dqs = [], [], []
        for h in range(2):
            s = nt(asked[1 + h][start:stop], asking[2 + h][begin:])
            if causal:
                edge = jnp.where(allowed, s[:, :STEP], masked_value)
                s = edge if stop == rows else jnp.concatenate([edge, s[:, STEP:]], axis=1)
            p = jnp.exp(s)
            dp = nt(asked[3 + h][start:stop], asking[4 + h][begin:])
            ds = (p * dp).astype(jnp.bfloat16)
            dvs.append(nn(p.astype(jnp.bfloat16), do[begin:]))
            dks.append(nn(ds, q[begin:]))
            dqs.append(tn(ds, k[start:stop]))
        d_values.append(jnp.where(first, dvs[0], dvs[1]))
        d_keys.append(jnp.where(first, dks[0], dks[1]))
        dq = jnp.where(first, dqs[0], dqs[1])
        for part in range(begin // STEP, rows // STEP):
            add = dq[part * STEP - begin:(part + 1) * STEP - begin]
            d_queries[part] = add if d_queries[part] is None else d_queries[part] + add
    return [jnp.concatenate(parts, axis=0) for parts in (d_queries, d_keys, d_values)]


def attend_back_far(place, base, group, qkv, mixed, aux, d_mixed, d_buf, store):
    views = (qkv.at[0], qkv.at[1], qkv.at[2], mixed, aux, d_mixed)
    rows = mixed.shape[1]
    span = rows // 2
    low_far = place[1] == 0
    extras = key_extras(0, rows, place[3])
    ready = widen_backward(base, extras, *views)
    for pair in range(group):
        asking, asked = ready
        late = [x[span:] for x in asking]
        early = [x[:span] for x in asked]
        cross_q, cross_k, cross_v = square_back(late, early, False)
        if pair + 1 < group:
            ready = widen_backward(base + pair + 1, extras, *views)
        far_asking = [jnp.where(low_far, x[:span], x[span:]) for x in asking]
        far_asked = [jnp.where(low_far, x[:span], x[span:]) for x in asked]
        d_q, d_k, d_v = square_back(far_asking, far_asked, True)
        at = base + pair
        d_buf[0, at] = ((d_q + jnp.where(low_far, 0.0, cross_q)) * HD ** -0.5).astype(jnp.bfloat16)
        d_buf[1, at] = (d_k + jnp.where(low_far, cross_k, 0.0)).astype(jnp.bfloat16)
        d_buf[2, at] = (d_v + jnp.where(low_far, cross_v, 0.0)).astype(jnp.bfloat16)
        store(at, jnp.where(low_far, cross_q, cross_k), cross_v)


def attend_back_near(place, step, qkv_ref, mixed_ref, aux_ref, do_ref, d_buf, kept_ref, other_ref):
    q_ref, k_ref, v_ref = (qkv_ref.at[part] for part in range(3))
    group, span = q_ref.shape[:2]
    low_far = place[1] == 0
    extras = key_extras(place[2] * span, span, place[3])
    ready = widen_backward(0, extras, q_ref, k_ref, v_ref, mixed_ref, aux_ref, do_ref)
    for pair in range(group):
        asking, asked = ready
        d_q, d_k, d_v = square_back(asking, asked, True)
        if pair + 1 < group:
            ready = widen_backward(pair + 1, extras, q_ref, k_ref, v_ref, mixed_ref, aux_ref, do_ref)
        kept, other = (ref[:, pair * LANES:(pair + 1) * LANES] for ref in (kept_ref, other_ref))
        at = step * group + pair
        d_buf[0, at] = ((d_q + jnp.where(low_far, kept, 0.0)) * HD ** -0.5).astype(jnp.bfloat16)
        d_buf[1, at] = (d_k + jnp.where(low_far, 0.0, kept)).astype(jnp.bfloat16)
        d_buf[2, at] = (d_v + jnp.where(low_far, 0.0, other)).astype(jnp.bfloat16)


def finish_grads(vectors, factors, d_buf, weight_buf, token_buf, middle_buf, normed, grad_buf):
    gain = vectors[GAIN:GAIN + 1]
    smalls = []
    for part in pieces_of(grad_buf.shape[0], STEP):
        d_parts = [side_by_side(d_buf.at[t], part) for t in range(d_buf.shape[0])]
        small = nt(d_parts[0], factors[SMALL:2 * SMALL]) + nt(d_parts[2], factors[2 * SMALL:])
        small = small.astype(jnp.bfloat16)
        d_normed = nt(jnp.concatenate(d_parts, axis=1), weight_buf[...]) + nn(small, factors[:SMALL])
        standard, inverse = standardize(token_buf[part].astype(jnp.float32))
        normed[part] = (standard * gain + vectors[SHIFT:SHIFT + 1]).astype(jnp.bfloat16)
        grad_buf[part] = (middle_buf[part] + pull_norm(d_normed, standard, inverse, gain)).astype(grad_buf.dtype)
        smalls.append(small)
    return jnp.concatenate(smalls, axis=0)


def sum_factors(small, normed, low_buf, d_buf, former, summed):
    everything = slice(None)
    scale = 32.0 / RANK
    downs = tn(small, normed[...])[:2 * RANK]
    ups = scale * jnp.concatenate(
        (
            tn(low_buf[...], side_by_side(d_buf.at[0], everything))[:RANK],
            tn(low_buf[...], side_by_side(d_buf.at[2], everything))[RANK:2 * RANK],
        )
    )
    if former is not None:
        downs, ups = former[:2 * RANK] + downs, former[2 * RANK:] + ups
    summed[:2 * RANK] = downs
    summed[2 * RANK:] = ups


def near_kernel(count, place, vectors, factors, former, qkv, mixed, aux, d_mixed, kept, other, inner, d_middle, lows, weight, carried, summed, landed, *refs):
    blocks, refs = refs[:count], refs[count:]
    d_buf, weight_buf, token_buf, middle_buf, low_buf, normed, grad_buf, held_buf, semaphores = refs
    step = pl.program_id(0)
    span = grad_buf.shape[0]
    rows = span // count
    mine = pl.ds(pl.multiple_of(place[2] * span, span), span)
    sources = [weight, inner.at[mine], d_middle.at[mine], lows.at[mine], carried]
    targets = [weight_buf, token_buf, middle_buf, low_buf, held_buf]
    fetched = [pltpu.make_async_copy(a, b, semaphores.at[i]) for i, (a, b) in enumerate(zip(sources, targets))]
    used = len(fetched)

    @pl.when(step == 0)
    def _():
        for move in fetched:
            move.start()

    attend_back_near(place, step, qkv, mixed, aux, d_mixed, d_buf, kept, other)

    @pl.when(step == pl.num_programs(0) - 1)
    def _():
        for move in fetched:
            move.wait()
        sent = [pltpu.make_async_copy(held_buf, landed, semaphores.at[used])]
        sent[0].start()
        small = finish_grads(vectors, factors, d_buf, weight_buf, token_buf, middle_buf, normed, grad_buf)
        for index, block in enumerate(blocks):
            part = block_part(place, index, count, rows, 0)
            sent.append(pltpu.make_async_copy(grad_buf.at[part], block, semaphores.at[used + 1 + index]))
            sent[-1].start()
        sum_factors(small, normed, low_buf, d_buf, former, summed)
        for move in sent:
            move.wait()


def heads(rows, half=None):
    return pl.BlockSpec((GROUP, rows, LANES), lambda step, place: (step, 0 if half is None else place[half], 0))


def triple(rows, half=None):
    return pl.BlockSpec((3, GROUP, rows, LANES), lambda step, place: (0, step, 0 if half is None else place[half], 0))


def backward_near(place, count, qkv, mixed, aux, d_mixed, kept, other, inner, d_middle, lows, vectors, factors, weight, former, carried):
    pairs, rows = qkv.shape[1:3]
    span, width = rows // 2, inner.shape[1]
    summed = jax.ShapeDtypeStruct((4 * RANK, width), jnp.float32)
    partial_sums = pl.BlockSpec((span, GROUP * LANES), lambda step, place: (0, step))
    return pl.pallas_call(
        partial(near_kernel, count),
        grid_spec=pltpu.PrefetchScalarGridSpec(
            num_scalar_prefetch=1, grid=(pairs // GROUP,),
            in_specs=[held(vectors.shape), held(factors.shape), held(former.shape), triple(span, 2)] + [heads(span, 2)] * 3
            + [partial_sums] * 2 + anywhere(5),
            out_specs=[held(summed.shape)] + anywhere(1 + count),
            scratch_shapes=[
                pltpu.VMEM((3, pairs, span, LANES), jnp.bfloat16),
                pltpu.VMEM(weight.shape, jnp.bfloat16),
                pltpu.VMEM((span, width), jnp.bfloat16),
                pltpu.VMEM((span, width), jnp.float32),
                pltpu.VMEM((span, SMALL), jnp.bfloat16),
                pltpu.VMEM((span, width), jnp.bfloat16),
                pltpu.VMEM((span, width), jnp.bfloat16),
                pltpu.VMEM(carried.shape, carried.dtype),
                pltpu.SemaphoreType.DMA((6 + count,)),
            ]),
        out_shape=[summed, jax.ShapeDtypeStruct(carried.shape, carried.dtype)] + [jax.ShapeDtypeStruct((span // count, width), jnp.bfloat16)] * count,
        compiler_params=pltpu.CompilerParams(vmem_limit_bytes=VMEM),
        cost_estimate=pl.CostEstimate(flops=20 << 30, bytes_accessed=20 << 20, transcendentals=0),
        name="backward_near",
    )(place, vectors, factors, former, qkv, mixed, aux, d_mixed, kept, other, inner, d_middle, lows, weight, carried)


def standardize(values):
    centred = values - jnp.mean(values, axis=-1, keepdims=True)
    inverse = lax.rsqrt(jnp.mean(centred * centred, axis=-1, keepdims=True) + epsilon)
    return centred * inverse, inverse


def pull_norm(grad, standard, inverse, gain):
    scaled = grad * gain
    centred = scaled - jnp.mean(scaled, axis=-1, keepdims=True)
    return inverse * (centred - standard * jnp.mean(scaled * standard, axis=-1, keepdims=True))


def side_by_side(ref, part):
    return jnp.concatenate([ref[pair, part] for pair in range(ref.shape[0])], axis=1)


def spread(ref, part, values):
    for pair in range(ref.shape[0]):
        ref[pair, part] = values[:, pair * LANES:(pair + 1) * LANES].astype(ref.dtype)


def held(shape):
    return pl.BlockSpec(shape, lambda step, place: (0,) * len(shape), pipeline_mode=pl.Buffered(1))


def deal_kernel(tokens, *refs):
    count = tokens.shape[0]
    blocks, held, semaphores = refs[:count], refs[count], refs[count + 1]
    me = lax.axis_index("blk")
    order = list(range(count // 2, count)) + list(range(count // 2))
    pulled = [pltpu.make_async_copy(tokens.at[me ^ index], held.at[index], semaphores.at[index]) for index in order]
    pushed = [pltpu.make_async_copy(held.at[index], blocks[index], semaphores.at[count + index]) for index in order]
    for move in pulled:
        move.start()
    for pull, push in zip(pulled, pushed):
        pull.wait()
        push.start()
    for move in pushed:
        move.wait()


def deal(tokens):
    count = tokens.shape[0]
    return pl.pallas_call(
        deal_kernel,
        in_specs=anywhere(1),
        out_specs=anywhere(count),
        out_shape=[jax.ShapeDtypeStruct(tokens.shape[1:], tokens.dtype)] * count,
        scratch_shapes=[pltpu.VMEM(tokens.shape, tokens.dtype), pltpu.SemaphoreType.DMA((2 * count,))],
        compiler_params=pltpu.CompilerParams(vmem_limit_bytes=VMEM),
        name="deal",
    )(tokens)


def gather_kernel(place, far, *refs):
    count = len(refs) - 4
    near, out, arrived, made, semaphores = refs[:count], refs[count], *refs[count + 1:]
    copy = copier(semaphores)
    slots, moves, sent = [], [], []
    for index in range(count):
        slots.append(place[1] * count + index)
        moves.append(copy(far.at[slots[-1]], arrived.at[index]))
    for index, block in enumerate(near):
        slots.append(place[0] ^ index)
        moves.append(copy(block, arrived.at[count + index]))
    for index, slot in enumerate(slots):
        moves[index].wait()
        made[index] = arrived[index].astype(made.dtype)
        sent.append(copy(made.at[index], out.at[slot]))
    for move in sent:
        move.wait()


def gather(place, far, near, dtype):
    return pl.pallas_call(
        gather_kernel,
        in_specs=[pl.BlockSpec(memory_space=pltpu.SMEM)] + anywhere(1 + len(near)),
        out_specs=anywhere(1)[0],
        out_shape=jax.ShapeDtypeStruct(far.shape, dtype),
        scratch_shapes=[pltpu.VMEM(far.shape, far.dtype), pltpu.VMEM(far.shape, dtype), pltpu.SemaphoreType.DMA((2 * far.shape[0],))],
        compiler_params=pltpu.CompilerParams(vmem_limit_bytes=VMEM),
        cost_estimate=pl.CostEstimate(flops=0, bytes_accessed=8 << 20, transcendentals=0),
        name="gather",
    )(place, far, *near)


def copier(semaphores):
    started = []

    def copy(source, target):
        move = pltpu.make_async_copy(source, target, semaphores.at[len(started)])
        started.append(move)
        move.start()
        return move

    return copy


def pieces_of(rows, size):
    return [slice(start, start + size) for start in range(0, rows, size)]


def anywhere(count):
    return [pl.BlockSpec(memory_space=pl.ANY)] * count


def project_rows(parts, vectors, factors, token_buf, normed, low_buf, weight_of, qkv_buf, finished):
    width = token_buf.shape[1]
    lane = lax.broadcasted_iota(jnp.int32, (width, LANES), 0) // HD
    each = jnp.where(lane == lax.broadcasted_iota(jnp.int32, (width, LANES), 1), 1.0, 0.0).astype(jnp.bfloat16)
    peaks = []
    for t in range(3):
        weight = weight_of(t)
        peak = None
        for index, part in enumerate(parts):
            own = slice(index * STEP, (index + 1) * STEP)
            if t == 0:
                standard, _ = standardize(token_buf[part].astype(jnp.float32))
                normed[own] = (standard * vectors[GAIN:GAIN + 1] + vectors[SHIFT:SHIFT + 1]).astype(jnp.bfloat16)
                low_buf[own] = nt(normed[own], factors[:SMALL]).astype(jnp.bfloat16)
            values = nn(normed[own], weight) + vectors[JOINT + t:JOINT + t + 1]
            if t != 1:
                start = SMALL if t == 0 else 2 * SMALL
                values = values + nn(low_buf[own], factors[start:start + SMALL])
            values = values.astype(jnp.bfloat16)
            spread(qkv_buf.at[t], part, values)
            if t < 2:
                new = jnp.max(nn(values * values, each).reshape(-1, 8, LANES), axis=0)
                peak = new if index == 0 else jnp.maximum(peak, new)
        peaks.append(peak)
        finished(t)
    return peaks[:2]


def block_part(place, index, count, rows, base):
    return pl.ds(pl.multiple_of(base + (place[0] % count ^ index) * rows, rows), rows)


def project_kernel(count, place, vectors, factors, weight, *refs):
    blocks = refs[:count]
    qkv, lows, inner, peaks, token_buf, weight_buf, normed, qkv_buf, low_buf, semaphores = refs[-10:]
    copy = copier(semaphores)
    rows, width = blocks[0].shape
    span = rows * count
    mine = pl.ds(pl.multiple_of(place[2] * span, span), span)
    arrivals = [copy(block, token_buf.at[block_part(place, index, count, rows, 0)]) for index, block in enumerate(blocks)]
    weights = [copy(weight.at[:, part], weight_buf.at[t]) for t, part in enumerate(pieces_of(weight.shape[1], width))]
    for arrival in arrivals:
        arrival.wait()
    sent = [copy(token_buf, inner.at[mine])]

    def weight_of(t):
        weights[t].wait()
        return weight_buf[t]

    def finished(t):
        if t == 0:
            sent.append(copy(low_buf, lows.at[mine]))
        sent.append(copy(qkv_buf.at[t], qkv.at[t, :, mine]))

    found = project_rows(pieces_of(span, STEP), vectors, factors, token_buf, normed, low_buf, weight_of, qkv_buf, finished)
    for index, peak in enumerate(found):
        peaks[index] = peak
    for move in sent:
        move.wait()


def project(place, blocks, vectors, factors, weight):
    count = len(blocks)
    rows, width = blocks[0].shape
    parts = weight.shape[1] // width
    span, pairs = count * rows, width // LANES
    return pl.pallas_call(
        partial(project_kernel, count),
        in_specs=[pl.BlockSpec(memory_space=pltpu.SMEM)] + [pl.BlockSpec(memory_space=pltpu.VMEM)] * 2 + anywhere(1 + count),
        out_specs=anywhere(3) + [pl.BlockSpec(memory_space=pltpu.VMEM)],
        out_shape=[
            jax.ShapeDtypeStruct((parts, pairs, 2 * span, LANES), jnp.bfloat16),
            jax.ShapeDtypeStruct((2 * span, SMALL), jnp.bfloat16),
            jax.ShapeDtypeStruct((2 * span, width), jnp.bfloat16),
            jax.ShapeDtypeStruct((2, 8, LANES), jnp.float32),
        ],
        scratch_shapes=[
            pltpu.VMEM((span, width), jnp.bfloat16),
            pltpu.VMEM((parts, width, width), jnp.bfloat16),
            pltpu.VMEM((span, width), jnp.bfloat16),
            pltpu.VMEM((parts, pairs, span, LANES), jnp.bfloat16),
            pltpu.VMEM((span, SMALL), jnp.bfloat16),
            pltpu.SemaphoreType.DMA((count + 2 * parts + 2,)),
        ],
        compiler_params=pltpu.CompilerParams(vmem_limit_bytes=VMEM),
        cost_estimate=pl.CostEstimate(flops=2 * span * width * width * parts, bytes_accessed=6 * width * width * 2, transcendentals=0),
        name="project",
    )(place, vectors, factors, weight, *blocks)


def gelu_and_slope(u):
    c = (2.0 / jnp.pi) ** 0.5
    square = u * u
    share = 0.5 + 0.5 * jnp.tanh(u * (c + (c * 0.044715) * square))
    value = u * share
    slope = share + value * (1.0 - share) * (2 * c + (6 * c * 0.044715) * square)
    return value, slope


def forward_kernel(count, place, vectors, factors, peaks, weight, out_weight, up, down, *refs):
    blocks, refs = refs[:count], refs[count:]
    former_qkv, _, former_inner = refs[:3]
    qkv, lows, inner, mixed, aux, result, middle, slopes = refs[3:11]
    token_buf, normed, low_buf, qkv_buf, mixed_buf, aux_buf, out_buf, up_buf, down_buf, middle_buf, slope_buf, active, semaphores = refs[11:]
    copy = copier(semaphores)
    rows, width = blocks[0].shape
    span = rows * count
    far_base = pl.multiple_of(place[1] * span, span)
    far, near = pl.ds(far_base, span), pl.ds(pl.multiple_of(place[2] * span, span), span)
    joint = pieces_of(weight.shape[1], width)
    columns = pieces_of(up.shape[1], width)
    arrivals = [copy(block, token_buf.at[block_part(place, index, count, rows, far_base)]) for index, block in enumerate(blocks)]
    weights = [copy(weight.at[:, part], slope_buf.at[:, part]) for part in joint]
    near_qkv = copy(former_qkv.at[:, :, near], qkv_buf.at[:, :, near])
    fetched = [copy(former_inner.at[near], token_buf.at[near]), copy(out_weight, out_buf)]
    ups = [copy(up.at[:, column], up_buf.at[t]) for t, column in enumerate(columns)]
    downs = copy(down, down_buf)
    for arrival in arrivals:
        arrival.wait()
    early = [copy(token_buf.at[far], inner.at[far])]

    def weight_of(t):
        weights[t].wait()
        return slope_buf[:, joint[t]]

    def finished(t):
        if t == 0:
            early.append(copy(low_buf, lows.at[far]))
        early.append(copy(qkv_buf.at[t, :, far], qkv.at[t, :, far]))

    parts = [pl.ds(pl.multiple_of(far_base + start, STEP), STEP) for start in range(0, span, STEP)]
    found = project_rows(parts, vectors, factors, token_buf, normed, low_buf, weight_of, qkv_buf, finished)
    bound = jnp.max(jnp.maximum(peaks[0], found[0])) * jnp.max(jnp.maximum(peaks[1], found[1]))
    calm = bound < (SAFE / HD ** -0.5) ** 2
    near_qkv.wait()

    @pl.loop(0, qkv_buf.shape[1] // GROUP)
    def _(step):
        attend_forward(step * GROUP, GROUP, calm, place[3], qkv_buf, mixed_buf, aux_buf)

    for move in early + fetched:
        move.wait()
    sent = [copy(mixed_buf, mixed), copy(aux_buf, aux)]
    for index, part in enumerate(pieces_of(2 * span, CHUNK)):
        m = token_buf[part].astype(jnp.float32) + nn(side_by_side(mixed_buf, part), out_buf[...]) + vectors[OUT:OUT + 1]
        middle_buf[part] = m
        sent.append(copy(middle_buf.at[part], middle.at[part]))
        standard, _ = standardize(m)
        normed_two = (standard * vectors[GAIN_TWO:GAIN_TWO + 1] + vectors[SHIFT_TWO:SHIFT_TWO + 1]).astype(jnp.bfloat16)
        for t, column in enumerate(columns):
            if index == 0:
                ups[t].wait()
            value, slope = gelu_and_slope(nn(normed_two, up_buf[t]) + vectors[UP + t:UP + t + 1])
            slope_buf[part, column] = slope.astype(jnp.bfloat16)
            active[:, column] = value.astype(jnp.bfloat16)
        sent.append(copy(slope_buf.at[part], slopes.at[part]))
        if index == 0:
            downs.wait()
        token_buf[part] = (middle_buf[part] + vectors[DOWN:DOWN + 1] + nn(active[...], down_buf[...])).astype(jnp.bfloat16)
        sent.append(copy(token_buf.at[part], result.at[part]))
    for move in sent:
        move.wait()


def forward(place, blocks, former, peaks, vectors, factors, weight, out_weight, up, down):
    count = len(blocks)
    rows, width = blocks[0].shape
    span, wide = count * rows, up.shape[1]
    qkv, lows, inner = former
    length = 2 * span
    pairs = qkv.shape[1]
    moves = count + 3 + 3 + wide // width + 1 + 5 + 2 + 3 * (length // CHUNK)
    shape = jax.ShapeDtypeStruct
    return pl.pallas_call(
        partial(forward_kernel, count),
        in_specs=[pl.BlockSpec(memory_space=pltpu.SMEM)] + [pl.BlockSpec(memory_space=pltpu.VMEM)] * 3 + anywhere(4 + count + 3),
        out_specs=anywhere(8),
        out_shape=[
            shape(qkv.shape, qkv.dtype),
            shape(lows.shape, lows.dtype),
            shape(inner.shape, inner.dtype),
            shape(qkv.shape[1:], jnp.bfloat16),
            shape(qkv.shape[1:], jnp.bfloat16),
            shape((length, width), jnp.bfloat16),
            shape((length, width), jnp.float32),
            shape((length, wide), jnp.bfloat16),
        ],
        scratch_shapes=[
            pltpu.VMEM((length, width), jnp.bfloat16),
            pltpu.VMEM((span, width), jnp.bfloat16),
            pltpu.VMEM((span, SMALL), jnp.bfloat16),
            pltpu.VMEM(qkv.shape, jnp.bfloat16),
            pltpu.VMEM((pairs, length, LANES), jnp.bfloat16),
            pltpu.VMEM((pairs, length, LANES), jnp.bfloat16),
            pltpu.VMEM((width, width), jnp.bfloat16),
            pltpu.VMEM((wide // width, width, width), jnp.bfloat16),
            pltpu.VMEM((wide, width), jnp.bfloat16),
            pltpu.VMEM((length, width), jnp.float32),
            pltpu.VMEM((length, wide), jnp.bfloat16),
            pltpu.VMEM((CHUNK, wide), jnp.bfloat16),
            pltpu.SemaphoreType.DMA((moves,)),
        ],
        input_output_aliases={8 + count + index: index for index in range(3)},
        compiler_params=pltpu.CompilerParams(vmem_limit_bytes=VMEM),
        cost_estimate=pl.CostEstimate(flops=60 << 30, bytes_accessed=60 << 20, transcendentals=0),
        name="forward",
    )(place, vectors, factors, peaks, weight, out_weight, up, down, *blocks, *former)


def far_kernel(place, vectors, factors, outer, slopes, up, down, middle, out_weight, qkv, mixed, aux, inner, lows, weight, *refs):
    summed, d_middle, d_mixed, kept, other, grads = refs[:6]
    outer_buf, slope_buf, up_buf, down_buf, middle_buf, out_buf, d_mixed_buf, qkv_buf, mixed_buf, aux_buf, d_buf, other_buf, low_buf, semaphores = refs[6:]
    copy = copier(semaphores)
    length, width = outer.shape
    span = length // 2
    far = pl.ds(pl.multiple_of(place[1] * span, span), span)
    near_base = pl.multiple_of(place[2] * span, span)
    near = pl.ds(near_base, span)
    parts = pieces_of(length, CHUNK)
    columns = pieces_of(up.shape[1], width)
    outers = [copy(outer.at[part], outer_buf.at[part]) for part in parts]
    downs, slants = [], []
    for column in columns:
        downs.append(copy(down.at[column], down_buf.at[column]))
        slants.append(copy(slopes.at[:, column], slope_buf.at[:, column]))
    late = [copy(up, up_buf), copy(middle, middle_buf), copy(out_weight, out_buf)]
    attended = [copy(qkv, qkv_buf), copy(mixed, mixed_buf), copy(aux, aux_buf)]
    for index, part in enumerate(parts):
        outers[index].wait()
        for t, column in enumerate(columns):
            if index == 0:
                downs[t].wait()
                slants[t].wait()
            d_active = nt(outer_buf[part], down_buf[column])
            slope_buf[part, column] = (d_active * slope_buf[part, column].astype(jnp.float32)).astype(jnp.bfloat16)
        if index == 0:
            for ready in late:
                ready.wait()
        for start in range(0, CHUNK, STEP):
            rows = slice(part.start + start, part.start + start + STEP)
            grad = nt(slope_buf[rows], up_buf[...])
            standard, inverse = standardize(middle_buf[rows])
            d = outer_buf[rows].astype(jnp.float32) + pull_norm(grad, standard, inverse, vectors[GAIN_TWO:GAIN_TWO + 1])
            middle_buf[rows] = d
            spread(d_mixed_buf, rows, nt(d.astype(jnp.bfloat16), out_buf[...]))
    sent = [copy(d_mixed_buf, d_mixed)]
    passed = copy(middle_buf.at[near], d_middle.at[near])
    weight_buf = slope_buf.at[:, :weight.shape[1]]
    ready = [copy(weight, weight_buf), copy(inner.at[far], outer_buf.at[:span]), copy(lows.at[far], low_buf)]
    passed.wait()
    for move in attended:
        move.wait()

    def store(at, first, second):
        lanes = pl.ds(pl.multiple_of(at * LANES, LANES), LANES)
        middle_buf[near, lanes] = first
        other_buf[:, lanes] = second

    @pl.loop(0, qkv_buf.shape[1] // GROUP)
    def _(step):
        attend_back_far(place, step * GROUP, GROUP, qkv_buf, mixed_buf, aux_buf, d_mixed_buf, d_buf, store)

    sent.append(copy(middle_buf.at[near], kept))
    sent.append(copy(other_buf, other))
    for move in ready:
        move.wait()
    normed, grad_buf = outer_buf.at[span:], slope_buf.at[:span, weight.shape[1]:]
    small = finish_grads(vectors, factors, d_buf, weight_buf, outer_buf.at[:span], middle_buf.at[far], normed, grad_buf)
    sent.append(copy(grad_buf, grads.at[far]))
    sum_factors(small, normed, low_buf, d_buf, None, summed)
    for move in sent:
        move.wait()


def backward_far(place, outer, slopes, up, down, middle, out_weight, qkv, mixed, aux, inner, lows, vectors, factors, weight):
    length, width = outer.shape
    span, wide, pairs = length // 2, up.shape[1], qkv.shape[1]
    shape = jax.ShapeDtypeStruct
    moves = length // CHUNK + 2 * (wide // width) + 3 + 3 + 2 + 3 + 2 + 1
    return pl.pallas_call(
        far_kernel,
        in_specs=[pl.BlockSpec(memory_space=pltpu.SMEM)] + [pl.BlockSpec(memory_space=pltpu.VMEM)] * 2 + anywhere(12),
        out_specs=[pl.BlockSpec(memory_space=pltpu.VMEM)] + anywhere(5),
        out_shape=[
            shape((4 * RANK, width), jnp.float32),
            shape((length, width), jnp.float32),
            shape(mixed.shape, jnp.bfloat16),
            shape((span, width), jnp.float32),
            shape((span, width), jnp.float32),
            shape((length, width), jnp.bfloat16),
        ],
        scratch_shapes=[
            pltpu.VMEM((length, width), jnp.bfloat16),
            pltpu.VMEM((length, wide), jnp.bfloat16),
            pltpu.VMEM((width, wide), jnp.bfloat16),
            pltpu.VMEM((wide, width), jnp.bfloat16),
            pltpu.VMEM((length, width), jnp.float32),
            pltpu.VMEM((width, width), jnp.bfloat16),
            pltpu.VMEM(mixed.shape, jnp.bfloat16),
            pltpu.VMEM(qkv.shape, jnp.bfloat16),
            pltpu.VMEM(mixed.shape, jnp.bfloat16),
            pltpu.VMEM(mixed.shape, jnp.bfloat16),
            pltpu.VMEM((3, pairs, span, LANES), jnp.bfloat16),
            pltpu.VMEM((span, width), jnp.float32),
            pltpu.VMEM((span, SMALL), jnp.bfloat16),
            pltpu.SemaphoreType.DMA((moves,)),
        ],
        compiler_params=pltpu.CompilerParams(vmem_limit_bytes=VMEM),
        cost_estimate=pl.CostEstimate(flops=80 << 30, bytes_accessed=60 << 20, transcendentals=0),
        name="backward_far",
    )(place, vectors, factors, outer, slopes, up, down, middle, out_weight, qkv, mixed, aux, inner, lows, weight)


def forward_kernel(count, place, vectors, factors, peaks, weight, out_weight, up, down, *refs):
    blocks, refs = refs[:count], refs[count:]
    former_qkv, _, former_inner = refs[:3]
    qkv, lows, inner, mixed, aux, result, middle, slopes = refs[3:11]
    token_buf, normed, low_buf, qkv_buf, mixed_buf, aux_buf, out_buf, up_buf, down_buf, middle_buf, slope_buf, active, semaphores = refs[11:]
    copy = copier(semaphores)
    rows, width = blocks[0].shape
    span = rows * count
    far_base = pl.multiple_of(place[1] * span, span)
    far, near = pl.ds(far_base, span), pl.ds(pl.multiple_of(place[2] * span, span), span)
    joint = pieces_of(weight.shape[1], width)
    columns = pieces_of(up.shape[1], width)
    arrivals = [copy(block, token_buf.at[block_part(place, index, count, rows, far_base)]) for index, block in enumerate(blocks)]
    weights = [copy(weight.at[:, part], slope_buf.at[:, part]) for part in joint]
    near_qkv = copy(former_qkv.at[:, :, near], qkv_buf.at[:, :, near])
    fetched = [copy(former_inner.at[near], token_buf.at[near]), copy(out_weight, out_buf)]
    ups = [copy(up.at[:, column], up_buf.at[t]) for t, column in enumerate(columns)]
    downs = copy(down, down_buf)
    for arrival in arrivals:
        arrival.wait()
    early = [copy(token_buf.at[far], inner.at[far])]

    def weight_of(t):
        weights[t].wait()
        return slope_buf[:, joint[t]]

    def finished(t):
        if t == 0:
            early.append(copy(low_buf, lows.at[far]))
        early.append(copy(qkv_buf.at[t, :, far], qkv.at[t, :, far]))

    parts = [pl.ds(pl.multiple_of(far_base + start, STEP), STEP) for start in range(0, span, STEP)]
    found = project_rows(parts, vectors, factors, token_buf, normed, low_buf, weight_of, qkv_buf, finished)
    bound = jnp.max(jnp.maximum(peaks[0], found[0])) * jnp.max(jnp.maximum(peaks[1], found[1]))
    calm = bound < (SAFE / HD ** -0.5) ** 2
    near_qkv.wait()

    @pl.loop(0, qkv_buf.shape[1] // GROUP)
    def _(step):
        attend_forward(step * GROUP, GROUP, calm, place[3], qkv_buf, mixed_buf, aux_buf)

    for move in early + fetched:
        move.wait()
    sent = [copy(mixed_buf, mixed), copy(aux_buf, aux)]
    for index, part in enumerate(pieces_of(2 * span, CHUNK)):
        m = token_buf[part].astype(jnp.float32) + nn(side_by_side(mixed_buf, part), out_buf[...]) + vectors[OUT:OUT + 1]
        middle_buf[part] = m
        sent.append(copy(middle_buf.at[part], middle.at[part]))
        standard, _ = standardize(m)
        normed_two = (standard * vectors[GAIN_TWO:GAIN_TWO + 1] + vectors[SHIFT_TWO:SHIFT_TWO + 1]).astype(jnp.bfloat16)
        for t, column in enumerate(columns):
            if index == 0:
                ups[t].wait()
            value, slope = gelu_and_slope(nn(normed_two, up_buf[t]) + vectors[UP + t:UP + t + 1])
            slope_buf[part, column] = slope.astype(jnp.bfloat16)
            active[:, column] = value.astype(jnp.bfloat16)
        sent.append(copy(slope_buf.at[part], slopes.at[part]))
        if index == 0:
            downs.wait()
        token_buf[part] = (middle_buf[part] + vectors[DOWN:DOWN + 1] + nn(active[...], down_buf[...])).astype(jnp.bfloat16)
        sent.append(copy(token_buf.at[part], result.at[part]))
    for move in sent:
        move.wait()


def forward(place, blocks, former, peaks, vectors, factors, weight, out_weight, up, down):
    count = len(blocks)
    rows, width = blocks[0].shape
    span, wide = count * rows, up.shape[1]
    qkv, lows, inner = former
    length = 2 * span
    pairs = qkv.shape[1]
    moves = count + 3 + 3 + wide // width + 1 + 5 + 2 + 3 * (length // CHUNK)
    shape = jax.ShapeDtypeStruct
    return pl.pallas_call(
        partial(forward_kernel, count),
        in_specs=[pl.BlockSpec(memory_space=pltpu.SMEM)] + [pl.BlockSpec(memory_space=pltpu.VMEM)] * 3 + anywhere(4 + count + 3),
        out_specs=anywhere(8),
        out_shape=[
            shape(qkv.shape, qkv.dtype),
            shape(lows.shape, lows.dtype),
            shape(inner.shape, inner.dtype),
            shape(qkv.shape[1:], jnp.bfloat16),
            shape(qkv.shape[1:], jnp.bfloat16),
            shape((length, width), jnp.bfloat16),
            shape((length, width), jnp.float32),
            shape((length, wide), jnp.bfloat16),
        ],
        scratch_shapes=[
            pltpu.VMEM((length, width), jnp.bfloat16),
            pltpu.VMEM((span, width), jnp.bfloat16),
            pltpu.VMEM((span, SMALL), jnp.bfloat16),
            pltpu.VMEM(qkv.shape, jnp.bfloat16),
            pltpu.VMEM((pairs, length, LANES), jnp.bfloat16),
            pltpu.VMEM((pairs, length, LANES), jnp.bfloat16),
            pltpu.VMEM((width, width), jnp.bfloat16),
            pltpu.VMEM((wide // width, width, width), jnp.bfloat16),
            pltpu.VMEM((wide, width), jnp.bfloat16),
            pltpu.VMEM((length, width), jnp.float32),
            pltpu.VMEM((length, wide), jnp.bfloat16),
            pltpu.VMEM((CHUNK, wide), jnp.bfloat16),
            pltpu.SemaphoreType.DMA((moves,)),
        ],
        input_output_aliases={8 + count + index: index for index in range(3)},
        compiler_params=pltpu.CompilerParams(vmem_limit_bytes=VMEM),
        cost_estimate=pl.CostEstimate(flops=60 << 30, bytes_accessed=60 << 20, transcendentals=0),
        name="forward",
    )(place, vectors, factors, peaks, weight, out_weight, up, down, *blocks, *former)


def feed_back_kernel(vectors, outer, slopes, up, down, middle, out_weight, d_middle, d_mixed, outer_buf, slope_buf, up_buf, down_buf, middle_buf, out_buf, hidden, mixed_buf, semaphores):
    copy = copier(semaphores)
    width = out_weight.shape[0]
    parts = pieces_of(outer.shape[0], CHUNK)
    columns = pieces_of(up.shape[1], width)
    outer_ready = copy(outer, outer_buf)
    downs, slants = [], []
    for t, column in enumerate(columns):
        downs.append(copy(down.at[column], down_buf.at[column]))
        slants.append(copy(slopes.at[:, column], slope_buf.at[:, column]))
    late = [copy(up, up_buf), copy(middle, middle_buf), copy(out_weight, out_buf)]
    outer_ready.wait()
    sent = []
    for index, part in enumerate(parts):
        for t, column in enumerate(columns):
            if index == 0:
                downs[t].wait()
                slants[t].wait()
            d_active = nt(outer_buf[part], down_buf[column])
            slope_buf[part, column] = (d_active * slope_buf[part, column].astype(jnp.float32)).astype(jnp.bfloat16)
        if index == 0:
            for ready in late:
                ready.wait()
        grad = nt(hidden[...], up_buf[...])
        standard, inverse = standardize(middle_buf[part])
        d = outer_buf[part].astype(jnp.float32) + pull_norm(grad, standard, inverse, vectors[GAIN_TWO:GAIN_TWO + 1])
        middle_buf[part] = d
        sent.append(copy(middle_buf.at[part], d_middle.at[part]))
        spread(mixed_buf, part, nt(d.astype(jnp.bfloat16), out_buf[...]))
        sent.append(copy(mixed_buf.at[:, part], d_mixed.at[:, part]))
    for move in sent:
        move.wait()


def feed_back(outer, slopes, up, down, middle, vectors, out_weight):
    rows, width = outer.shape
    wide = up.shape[1]
    pairs = width // LANES
    return pl.pallas_call(
        feed_back_kernel,
        in_specs=[pl.BlockSpec(memory_space=pltpu.VMEM)] + anywhere(6),
        out_specs=anywhere(2),
        out_shape=[jax.ShapeDtypeStruct((rows, width), jnp.float32), jax.ShapeDtypeStruct((pairs, rows, LANES), jnp.bfloat16)],
        scratch_shapes=[
            pltpu.VMEM((rows, width), jnp.bfloat16),
            pltpu.VMEM((rows, wide), jnp.bfloat16),
            pltpu.VMEM((width, wide), jnp.bfloat16),
            pltpu.VMEM((wide, width), jnp.bfloat16),
            pltpu.VMEM((rows, width), jnp.float32),
            pltpu.VMEM((width, width), jnp.bfloat16),
            pltpu.VMEM((CHUNK, wide), jnp.bfloat16),
            pltpu.VMEM((pairs, rows, LANES), jnp.bfloat16),
            pltpu.SemaphoreType.DMA((4 + 2 * (wide // width) + 2 * (rows // CHUNK),)),
        ],
        compiler_params=pltpu.CompilerParams(vmem_limit_bytes=VMEM),
        cost_estimate=pl.CostEstimate(flops=2 * rows * width * (width + 2 * wide), bytes_accessed=40 << 20, transcendentals=0),
        name="feed_back",
    )(vectors, outer, slopes, up, down, middle, out_weight)


def sum_over(v, axis):
    size = lax.axis_size(axis)
    if size & (size - 1):
        return lax.psum(v, axis)
    step = 1
    while step < size:
        v = v + lax.ppermute(v, axis, [(i, i ^ step) for i in range(size)])
        step *= 2
    return v


def whole_slots(
    tokens,
    lengths,
    norm_gain,
    norm_shift,
    joint_weight,
    query_bias,
    value_bias,
    output_weight,
    output_bias,
    second_gain,
    second_shift,
    upward_weight,
    upward_bias,
    down_weight,
    down_bias,
    query_down,
    query_up,
    value_down,
    value_up,
    cotangent,
):
    seqs_here, rows, width = tokens.shape
    ranks = lax.axis_size("blk")
    half = ranks // 2
    adapter = 32.0 / RANK

    def partner(index):
        return [(i, i ^ index) for i in range(ranks)]

    me = lax.axis_index("blk")
    side = me // half
    place = jnp.stack((me, 1 - side, side, lengths[me])).astype(jnp.int32)
    vectors = jnp.concatenate(
        (
            norm_gain,
            norm_shift,
            query_bias,
            jnp.zeros_like(query_bias),
            value_bias,
            output_bias,
            second_gain,
            second_shift,
            down_bias,
            upward_bias,
        )
    )
    vectors = vectors.astype(jnp.float32).reshape(-1, width)
    factors = jnp.concatenate(
        (
            jnp.pad(jnp.concatenate((query_down, value_down), axis=1).T, ((0, 2 * RANK), (0, 0))),
            jnp.pad(adapter * query_up, ((0, 3 * RANK), (0, 0))).astype(jnp.bfloat16),
            jnp.pad(adapter * value_up, ((RANK, 2 * RANK), (0, 0))).astype(jnp.bfloat16),
        )
    )
    own, *others = deal(tokens)
    far = [lax.ppermute(others[k - 1], "blk", partner(k)) for k in range(half, ranks)]
    near = [own] + [lax.ppermute(others[k - 1], "blk", partner(k)) for k in range(1, half)]
    *former, near_peaks = project(place, near, vectors, factors, joint_weight)
    cotangent, far, *_ = lax.optimization_barrier((cotangent, far, near_peaks))
    outer = lax.all_to_all(cotangent, "blk", 0, 0, tiled=True).reshape(-1, width)
    qkv, lows, inner, mixed, aux, result, middle, slopes = forward(
        place,
        far,
        former,
        near_peaks,
        vectors,
        factors,
        joint_weight,
        output_weight,
        upward_weight,
        down_weight,
    )
    result, middle, slopes, outer = lax.optimization_barrier((result, middle, slopes, outer))
    block_output = lax.all_to_all(
        result.reshape(ranks, rows, width), "blk", 0, 0, tiled=True
    )
    shared = (vectors, factors, joint_weight)
    far_factors, d_middle, d_mixed, kept, other, far_grads = backward_far(
        place,
        outer,
        slopes,
        upward_weight,
        down_weight,
        middle,
        output_weight,
        qkv,
        mixed,
        aux,
        inner,
        lows,
        *shared,
    )
    far_grads = lax.all_to_all(far_grads.reshape(ranks, rows, width), "blk", 0, 0, tiled=True)
    packed, block_output, *near_grads = backward_near(
        place,
        half,
        qkv,
        mixed,
        aux,
        d_mixed,
        kept,
        other,
        inner,
        d_middle,
        lows,
        *shared,
        far_factors,
        block_output,
    )
    near_grads = near_grads[:1] + [
        lax.ppermute(near_grads[k], "blk", partner(k)) for k in range(1, half)
    ]
    packed, near_grads = lax.optimization_barrier((sum_over(packed, "batch"), near_grads))
    packed = sum_over(packed, "blk")
    token_grads = gather(place, far_grads, near_grads, jnp.float32)
    query_down_grad, value_down_grad = packed[:RANK].T, packed[RANK : 2 * RANK].T
    query_up_grad, value_up_grad = packed[2 * RANK : 3 * RANK], packed[3 * RANK :]
    return (
        block_output,
        token_grads,
        query_down_grad,
        query_up_grad,
        value_down_grad,
        value_up_grad,
    )


def body(
    tokens,
    lengths,
    norm_gain,
    norm_shift,
    joint_weight,
    query_bias,
    value_bias,
    output_weight,
    output_bias,
    second_gain,
    second_shift,
    upward_weight,
    upward_bias,
    down_weight,
    down_bias,
    query_down,
    query_up,
    value_down,
    value_up,
    cotangent,
):
    seqs_here, rows, width = tokens.shape
    heads = width // HD
    positions = seqs_here * rows
    length_all = rows * lax.axis_size("blk")
    scale = HD ** (-0.5)
    adapter = 32.0 / RANK
    flat = tokens.reshape(positions, width).astype(jnp.float32)
    normed_full, standard, inverse = normalize(flat, norm_gain, norm_shift)
    normed = normed_full.astype(jnp.bfloat16)
    joint = jnp.dot(normed, joint_weight, preferred_element_type=jnp.float32)
    query_low = jnp.dot(normed, query_down, preferred_element_type=jnp.float32).astype(jnp.bfloat16)
    value_low = jnp.dot(normed, value_down, preferred_element_type=jnp.float32).astype(jnp.bfloat16)
    queries = (
        joint[:, :width]
        + query_bias.astype(jnp.float32)
        + adapter * jnp.dot(query_low, query_up, preferred_element_type=jnp.float32)
    ).astype(jnp.bfloat16)
    keys_here = joint[:, width : 2 * width].astype(jnp.bfloat16)
    values_here = (
        joint[:, 2 * width :]
        + value_bias.astype(jnp.float32)
        + adapter * jnp.dot(value_low, value_up, preferred_element_type=jnp.float32)
    ).astype(jnp.bfloat16)
    query_heads = queries.reshape(seqs_here, rows, heads, HD)
    key_blocks = keys_here.reshape(seqs_here, rows, width)
    value_blocks = values_here.reshape(seqs_here, rows, width)
    device = lax.axis_index("blk")
    query_place = device * rows + jnp.arange(rows, dtype=jnp.int32)
    limits = lengths[:, None, None, None]

    def visible(query_pos, key_pos):
        return (key_pos[None, None, None, :] <= query_pos[None, None, :, None]) & (
            key_pos[None, None, None, :] < limits
        )

    running = jnp.full((seqs_here, heads, rows), masked_value, jnp.float32)
    key_piece = lax.all_gather(key_blocks, "blk", axis=1, tiled=True)
    value_piece = lax.all_gather(value_blocks, "blk", axis=1, tiled=True)
    count = key_piece.shape[1]
    key_heads = key_piece.reshape(seqs_here, count, heads, HD)
    value_heads = value_piece.reshape(seqs_here, count, heads, HD)
    allowed = visible(query_place, jnp.arange(count, dtype=jnp.int32))
    scores = (
        jnp.einsum("sqhd,skhd->shqk", query_heads, key_heads, preferred_element_type=jnp.float32)
        * scale
    )
    masked = jnp.where(allowed, scores, masked_value)
    highest = jnp.maximum(running, jnp.max(masked, axis=-1))
    weights = jnp.where(allowed, jnp.exp(masked - highest[..., None]), 0.0)
    totals = jnp.sum(weights, axis=-1)
    update = jnp.einsum(
        "shqk,skhd->sqhd",
        weights.astype(jnp.bfloat16),
        value_heads,
        preferred_element_type=jnp.float32,
    )
    summed = update
    running, totals, summed = (highest, totals, summed)
    mixed_full = summed / jnp.transpose(totals, (0, 2, 1))[..., None]
    log_total = running + jnp.log(totals)
    mixed_low = mixed_full.reshape(positions, width).astype(jnp.bfloat16)
    middle = (
        flat
        + jnp.dot(mixed_low, output_weight, preferred_element_type=jnp.float32)
        + output_bias.astype(jnp.float32)
    )
    normed_two_full, standard_two, inverse_two = normalize(middle, second_gain, second_shift)
    normed_two = normed_two_full.astype(jnp.bfloat16)
    hidden = jnp.dot(
        normed_two, upward_weight, preferred_element_type=jnp.float32
    ) + upward_bias.astype(jnp.float32)
    active_full, gelu_pull = jax.vjp(partial(jax.nn.gelu, approximate=True), hidden)
    active = active_full.astype(jnp.bfloat16)
    block_output = (
        (
            middle
            + jnp.dot(active, down_weight, preferred_element_type=jnp.float32)
            + down_bias.astype(jnp.float32)
        )
        .astype(jnp.bfloat16)
        .reshape(seqs_here, rows, width)
    )
    outer = cotangent.reshape(positions, width)
    d_active = against(outer, down_weight)
    d_hidden = gelu_pull(d_active)[0].astype(jnp.bfloat16)
    d_normed_two = against(d_hidden, upward_weight)
    d_middle = outer.astype(jnp.float32) + norm_back(
        d_normed_two, standard_two, inverse_two, second_gain
    )
    d_branch = d_middle.astype(jnp.bfloat16)
    d_mixed = against(d_branch, output_weight).astype(jnp.bfloat16)
    d_mixed_heads = d_mixed.reshape(seqs_here, rows, heads, HD)
    delta = jnp.transpose(
        jnp.sum(d_mixed_heads.astype(jnp.float32) * mixed_full, axis=-1), (0, 2, 1)
    )
    key_all, value_all = (
        lax.all_gather(key_blocks, "blk", axis=1, tiled=True),
        lax.all_gather(value_blocks, "blk", axis=1, tiled=True),
    )
    key_heads_all = key_all.reshape(seqs_here, length_all, heads, HD)
    value_heads_all = value_all.reshape(seqs_here, length_all, heads, HD)
    allowed_all = visible(query_place, jnp.arange(length_all, dtype=jnp.int32))
    scores = (
        jnp.einsum(
            "sqhd,skhd->shqk", query_heads, key_heads_all, preferred_element_type=jnp.float32
        )
        * scale
    )
    probs = jnp.where(allowed_all, jnp.exp(scores - log_total[..., None]), 0.0)
    d_probs = jnp.einsum(
        "sqhd,skhd->shqk", d_mixed_heads, value_heads_all, preferred_element_type=jnp.float32
    )
    d_scores = (probs * (d_probs - delta[..., None])).astype(jnp.bfloat16)
    d_queries = (
        jnp.einsum("shqk,skhd->sqhd", d_scores, key_heads_all, preferred_element_type=jnp.float32)
        * scale
    )
    d_keys_all = (
        jnp.einsum("shqk,sqhd->kshd", d_scores, query_heads, preferred_element_type=jnp.float32)
        * scale
    )
    d_values_all = jnp.einsum(
        "shqk,sqhd->kshd",
        probs.astype(jnp.bfloat16),
        d_mixed_heads,
        preferred_element_type=jnp.float32,
    )
    stacked = jnp.stack(
        (
            d_keys_all.reshape(length_all, seqs_here, width),
            d_values_all.reshape(length_all, seqs_here, width),
        ),
        axis=2,
    )
    owned = lax.psum_scatter(
        stacked.astype(jnp.bfloat16), "blk", scatter_dimension=0, tiled=True
    ).astype(jnp.float32)
    d_keys = jnp.transpose(owned[:, :, 0], (1, 0, 2)).reshape(positions, width)
    d_values = jnp.transpose(owned[:, :, 1], (1, 0, 2)).reshape(positions, width)
    d_query_low = d_queries.reshape(positions, width).astype(jnp.bfloat16)
    d_key_low = d_keys.astype(jnp.bfloat16)
    d_value_low = d_values.astype(jnp.bfloat16)
    query_up_grad = adapter * transposed(query_low, d_query_low)
    value_up_grad = adapter * transposed(value_low, d_value_low)
    d_query_small = (adapter * against(d_query_low, query_up)).astype(jnp.bfloat16)
    d_value_small = (adapter * against(d_value_low, value_up)).astype(jnp.bfloat16)
    query_down_grad = transposed(normed, d_query_small)
    value_down_grad = transposed(normed, d_value_small)
    d_joint = jnp.concatenate((d_query_low, d_key_low, d_value_low), axis=1)
    d_normed = (
        against(d_joint, joint_weight)
        + against(d_query_small, query_down)
        + against(d_value_small, value_down)
    )
    token_grads = (d_middle + norm_back(d_normed, standard, inverse, norm_gain)).reshape(
        seqs_here, rows, width
    )
    sums = lax.psum(
        (query_down_grad, query_up_grad, value_down_grad, value_up_grad), ("batch", "blk")
    )
    return (block_output, token_grads, sums[0], sums[1], sums[2], sums[3])


def choose(tokens, *others):
    seqs, rows = tokens.shape[:2]
    ranks = lax.axis_size("blk")
    fits = seqs == ranks and ranks > 1 and not ranks & (ranks - 1)
    fits = fits and rows % LANES == 0 and (ranks // 2 * rows) % CHUNK == 0
    return (whole_slots if fits else body)(tokens, *others)


def solution(mesh):
    placed = (
        P("batch", "blk", None),
        P("batch"),
        P(),
        P(),
        P(),
        P(),
        P(),
        P(),
        P(),
        P(),
        P(),
        P(),
        P(),
        P(),
        P(),
        P(),
        P(),
        P(),
        P(),
        P("batch", "blk", None),
    )
    return jax.shard_map(
        choose,
        mesh=mesh,
        in_specs=placed,
        out_specs=(P("batch", "blk", None), P("batch", "blk", None), P(), P(), P(), P()),
        check_vma=False,
    )
```

```python
from functools import partial

import jax
import jax.numpy as jnp
from jax import lax
from jax.experimental import pallas as pl
from jax.experimental.pallas import tpu as pltpu
from jax.sharding import PartitionSpec as P

HD = 64
RANK = 4
LANES = 128
STEP = 256
FULL = 512
SAFE = 80.0
GROUP = 2
CHUNK = 512
TILE = 1024
VMEM = 62 << 20
GAIN = 0
SHIFT = 1
JOINT = 2
OUT = 5
GAIN_TWO = 6
SHIFT_TWO = 7
DOWN = 8
UP = 9
SMALL = 16
FIRST = 4
LAST = 5


epsilon = 1e-05
masked_value = -1e30


def normalize(values, gain, shift):
    centred = values - jnp.mean(values, axis=-1, keepdims=True)
    inverse = lax.rsqrt(jnp.mean(centred * centred, axis=-1, keepdims=True) + epsilon)
    standard = centred * inverse
    return (standard * gain.astype(jnp.float32) + shift.astype(jnp.float32), standard, inverse)


def norm_back(grad, standard, inverse, gain):
    scaled = grad * gain.astype(jnp.float32)
    centred = scaled - jnp.mean(scaled, axis=-1, keepdims=True)
    return inverse * (centred - standard * jnp.mean(scaled * standard, axis=-1, keepdims=True))


def transposed(left, right):
    return lax.dot_general(
        left, right, (((0,), (0,)), ((), ())), preferred_element_type=jnp.float32
    )


def against(left, right):
    return lax.dot_general(
        left, right, (((1,), (1,)), ((), ())), preferred_element_type=jnp.float32
    )


def nt(a, b):
    return lax.dot_general(a, b, (((1,), (1,)), ((), ())), preferred_element_type=jnp.float32)


def tn(a, b):
    return lax.dot_general(a, b, (((0,), (0,)), ((), ())), preferred_element_type=jnp.float32)


def nn(a, b):
    return jnp.dot(a, b, preferred_element_type=jnp.float32)


def thirds(x):
    first = x.astype(jnp.bfloat16)
    rest = x - first.astype(jnp.float32)
    second = rest.astype(jnp.bfloat16)
    third = (rest - second.astype(jnp.float32)).astype(jnp.bfloat16)
    return first, second, third


def in_first_head():
    return lax.broadcasted_iota(jnp.int32, (1, LANES), 1) < HD


def spare_lane():
    return lax.broadcasted_iota(jnp.int32, (1, LANES), 1) % HD


def key_extras(begin, rows, length):
    place = begin + lax.broadcasted_iota(jnp.int32, (rows, LANES), 0)
    bias = jnp.where(place < length, 0.0, masked_value).astype(jnp.bfloat16)
    spare = spare_lane()
    return jnp.where(spare == 0, bias, jnp.where(spare < 4, jnp.bfloat16(1), jnp.bfloat16(0)))


def attend_forward(base, group, calm, length, qkv, mixed_ref, aux_ref):
    q_ref, k_ref, v_ref = (qkv.at[part] for part in range(3))
    rows = q_ref.shape[1]
    one, zero = jnp.bfloat16(1), jnp.bfloat16(0)
    first, spare = in_first_head(), spare_lane()
    extras = key_extras(0, rows, length)
    lead = jnp.where(spare == 0, one, zero)
    causal = lax.broadcasted_iota(jnp.int32, (STEP, STEP), 1) <= lax.broadcasted_iota(jnp.int32, (STEP, STEP), 0)

    def widen(pair):
        q, k, v = q_ref[base + pair] * jnp.bfloat16(HD ** -0.5), k_ref[base + pair], v_ref[base + pair]
        q_aug = [jnp.where(first, q, lead), jnp.where(first, lead, q)]
        k_aug = [jnp.where(first, k, extras), jnp.where(first, extras, k)]
        v_aug = [jnp.where(first, v, one), jnp.where(first, one, v)]
        return q_aug, k_aug, v_aug

    def write(pair, start, sums, tops):
        total = jnp.where(first, sums[1], sums[0])
        mixed = jnp.where(first, sums[0], sums[1]) * pltpu.roll(1.0 / total, HD, 1)
        mixed_ref[base + pair, start:start + STEP] = mixed.astype(jnp.bfloat16)
        level = jnp.log(total)
        if tops is not None:
            level = level + jnp.where(first, tops[1], tops[0])
        aux = lead
        for index, part in enumerate(thirds(-level)):
            aux = jnp.where(spare == index + 1, part, aux)
        aux_ref[base + pair, start:start + STEP] = aux

    @pl.when(calm)
    def _():
        ready = widen(0)
        for pair in range(group):
            q_aug, k_aug, v_aug = ready
            sums = [[None] * (rows // STEP) for _ in range(2)]
            for start in range(0, rows, STEP):
                stop = start + STEP
                for h in range(2):
                    s = nt(q_aug[h][start:], k_aug[h][start:stop])
                    w = jnp.exp(jnp.where(causal, s[:STEP], masked_value)).astype(jnp.bfloat16)
                    if stop < rows:
                        w = jnp.concatenate([w, jnp.exp(s[STEP:]).astype(jnp.bfloat16)], axis=0)
                    o = nn(w, v_aug[h][start:stop])
                    for part in range(start // STEP, rows // STEP):
                        add = o[part * STEP - start:(part + 1) * STEP - start]
                        sums[h][part] = add if start == 0 else sums[h][part] + add
                if start == 0 and pair + 1 < group:
                    ready = widen(pair + 1)
                write(pair, start, [sums[0][start // STEP], sums[1][start // STEP]], None)

    @pl.when(jnp.logical_not(calm))
    def _():
        for pair in range(group):
            q_aug, k_aug, v_aug = widen(pair)
            for start in range(0, rows, STEP):
                stop = start + STEP
                sums, tops = [], []
                for h in range(2):
                    s = nt(q_aug[h][start:stop], k_aug[h][:stop])
                    edge = jnp.where(causal, s[:, start:], masked_value)
                    s = edge if start == 0 else jnp.concatenate([s[:, :start], edge], axis=1)
                    tops.append(jnp.max(s, axis=1, keepdims=True))
                    w = jnp.exp(s - tops[h]).astype(jnp.bfloat16)
                    sums.append(nn(w, v_aug[h][:stop]))
                write(pair, start, sums, tops)


def widen_backward(pair, extras, q_ref, k_ref, v_ref, mixed_ref, aux_ref, do_ref):
    one, zero = jnp.bfloat16(1), jnp.bfloat16(0)
    first, spare = in_first_head(), spare_lane()
    three = jnp.where(spare < 3, one, zero)
    row = lax.broadcasted_iota(jnp.int32, (LANES, LANES), 0) // HD
    column = lax.broadcasted_iota(jnp.int32, (LANES, LANES), 1) // HD
    cross = jnp.where(row != column, one, zero)
    q, k, v = q_ref[pair] * jnp.bfloat16(HD ** -0.5), k_ref[pair], v_ref[pair]
    do, aux = do_ref[pair], aux_ref[pair]
    k_aug = [jnp.where(first, k, extras), jnp.where(first, extras, k)]
    q_aug = [jnp.where(first, q, aux), jnp.where(first, aux, q)]
    v_aug = [jnp.where(first, v, three), jnp.where(first, three, v)]
    product = do.astype(jnp.float32) * mixed_ref[pair].astype(jnp.float32)
    high = product.astype(jnp.bfloat16)
    low = (product - high.astype(jnp.float32)).astype(jnp.bfloat16)
    delta = nn(high, cross) + nn(low, cross)
    extra = zero
    for index, part in enumerate(thirds(-delta)):
        extra = jnp.where(spare == index, part, extra)
    do_aug = [jnp.where(first, do, extra), jnp.where(first, extra, do)]
    return (q, do, *q_aug, *do_aug), (k, *k_aug, *v_aug)


def square_back(asking, asked, causal):
    q, do = asking[:2]
    k = asked[0]
    rows = q.shape[0]
    first = in_first_head()
    allowed = lax.broadcasted_iota(jnp.int32, (STEP, STEP), 0) <= lax.broadcasted_iota(jnp.int32, (STEP, STEP), 1)
    d_queries, d_keys, d_values = [None] * (rows // STEP), [], []
    size = STEP if causal else FULL
    for start in range(0, rows, size):
        stop = start + size
        begin = start if causal else 0
        dks, dvs, dqs = [], [], []
        for h in range(2):
            s = nt(asked[1 + h][start:stop], asking[2 + h][begin:])
            if causal:
                edge = jnp.where(allowed, s[:, :STEP], masked_value)
                s = edge if stop == rows else jnp.concatenate([edge, s[:, STEP:]], axis=1)
            p = jnp.exp(s)
            dp = nt(asked[3 + h][start:stop], asking[4 + h][begin:])
            ds = (p * dp).astype(jnp.bfloat16)
            dvs.append(nn(p.astype(jnp.bfloat16), do[begin:]))
            dks.append(nn(ds, q[begin:]))
            dqs.append(tn(ds, k[start:stop]))
        d_values.append(jnp.where(first, dvs[0], dvs[1]))
        d_keys.append(jnp.where(first, dks[0], dks[1]))
        dq = jnp.where(first, dqs[0], dqs[1])
        for part in range(begin // STEP, rows // STEP):
            add = dq[part * STEP - begin:(part + 1) * STEP - begin]
            d_queries[part] = add if d_queries[part] is None else d_queries[part] + add
    return [jnp.concatenate(parts, axis=0) for parts in (d_queries, d_keys, d_values)]


def attend_back_far(place, base, group, qkv, mixed, aux, d_mixed, d_buf, store):
    views = (qkv.at[0], qkv.at[1], qkv.at[2], mixed, aux, d_mixed)
    rows = mixed.shape[1]
    span = rows // 2
    low_far = place[1] == 0
    extras = key_extras(0, rows, place[3])
    ready = widen_backward(base, extras, *views)
    for pair in range(group):
        asking, asked = ready
        late = [x[span:] for x in asking]
        early = [x[:span] for x in asked]
        cross_q, cross_k, cross_v = square_back(late, early, False)
        if pair + 1 < group:
            ready = widen_backward(base + pair + 1, extras, *views)
        far_asking = [jnp.where(low_far, x[:span], x[span:]) for x in asking]
        far_asked = [jnp.where(low_far, x[:span], x[span:]) for x in asked]
        d_q, d_k, d_v = square_back(far_asking, far_asked, True)
        at = base + pair
        d_buf[0, at] = ((d_q + jnp.where(low_far, 0.0, cross_q)) * HD ** -0.5).astype(jnp.bfloat16)
        d_buf[1, at] = (d_k + jnp.where(low_far, cross_k, 0.0)).astype(jnp.bfloat16)
        d_buf[2, at] = (d_v + jnp.where(low_far, cross_v, 0.0)).astype(jnp.bfloat16)
        store(at, jnp.where(low_far, cross_q, cross_k), cross_v)


def attend_back_near(place, step, qkv_ref, mixed_ref, aux_ref, do_ref, d_buf, kept_ref, other_ref):
    q_ref, k_ref, v_ref = (qkv_ref.at[part] for part in range(3))
    group, span = q_ref.shape[:2]
    low_far = place[1] == 0
    extras = key_extras(place[2] * span, span, place[3])
    ready = widen_backward(0, extras, q_ref, k_ref, v_ref, mixed_ref, aux_ref, do_ref)
    for pair in range(group):
        asking, asked = ready
        d_q, d_k, d_v = square_back(asking, asked, True)
        if pair + 1 < group:
            ready = widen_backward(pair + 1, extras, q_ref, k_ref, v_ref, mixed_ref, aux_ref, do_ref)
        kept, other = (ref[:, pair * LANES:(pair + 1) * LANES] for ref in (kept_ref, other_ref))
        at = step * group + pair
        d_buf[0, at] = ((d_q + jnp.where(low_far, kept, 0.0)) * HD ** -0.5).astype(jnp.bfloat16)
        d_buf[1, at] = (d_k + jnp.where(low_far, 0.0, kept)).astype(jnp.bfloat16)
        d_buf[2, at] = (d_v + jnp.where(low_far, 0.0, other)).astype(jnp.bfloat16)


def finish_grads(vectors, factors, d_buf, weight_buf, token_buf, middle_buf, normed, grad_buf):
    gain = vectors[GAIN:GAIN + 1]
    smalls = []
    for part in pieces_of(grad_buf.shape[0], STEP):
        d_parts = [side_by_side(d_buf.at[t], part) for t in range(d_buf.shape[0])]
        small = nt(d_parts[0], factors[SMALL:2 * SMALL]) + nt(d_parts[2], factors[2 * SMALL:])
        small = small.astype(jnp.bfloat16)
        d_normed = nt(jnp.concatenate(d_parts, axis=1), weight_buf[...]) + nn(small, factors[:SMALL])
        standard, inverse = standardize(token_buf[part].astype(jnp.float32))
        normed[part] = (standard * gain + vectors[SHIFT:SHIFT + 1]).astype(jnp.bfloat16)
        grad_buf[part] = (middle_buf[part] + pull_norm(d_normed, standard, inverse, gain)).astype(grad_buf.dtype)
        smalls.append(small)
    return jnp.concatenate(smalls, axis=0)


def sum_factors(small, normed, low_buf, d_buf, former, summed):
    everything = slice(None)
    scale = 32.0 / RANK
    downs = tn(small, normed[...])[:2 * RANK]
    ups = scale * jnp.concatenate(
        (
            tn(low_buf[...], side_by_side(d_buf.at[0], everything))[:RANK],
            tn(low_buf[...], side_by_side(d_buf.at[2], everything))[RANK:2 * RANK],
        )
    )
    if former is not None:
        downs, ups = former[:2 * RANK] + downs, former[2 * RANK:] + ups
    summed[:2 * RANK] = downs
    summed[2 * RANK:] = ups


def near_kernel(count, place, vectors, factors, former, qkv, mixed, aux, d_mixed, kept, other, inner, d_middle, lows, weight, carried, summed, landed, *refs):
    blocks, refs = refs[:count], refs[count:]
    d_buf, weight_buf, token_buf, middle_buf, low_buf, normed, grad_buf, held_buf, semaphores = refs
    step = pl.program_id(0)
    span = grad_buf.shape[0]
    rows = span // count
    mine = pl.ds(pl.multiple_of(place[2] * span, span), span)
    sources = [weight, inner.at[mine], d_middle.at[mine], lows.at[mine], carried]
    targets = [weight_buf, token_buf, middle_buf, low_buf, held_buf]
    fetched = [pltpu.make_async_copy(a, b, semaphores.at[i]) for i, (a, b) in enumerate(zip(sources, targets))]
    used = len(fetched)

    @pl.when(step == 0)
    def _():
        for move in fetched:
            move.start()

    attend_back_near(place, step, qkv, mixed, aux, d_mixed, d_buf, kept, other)

    @pl.when(step == pl.num_programs(0) - 1)
    def _():
        for move in fetched:
            move.wait()
        sent = [pltpu.make_async_copy(held_buf, landed, semaphores.at[used])]
        sent[0].start()
        small = finish_grads(vectors, factors, d_buf, weight_buf, token_buf, middle_buf, normed, grad_buf)
        for index, block in enumerate(blocks):
            part = block_part(place, index, count, rows, 0)
            sent.append(pltpu.make_async_copy(grad_buf.at[part], block, semaphores.at[used + 1 + index]))
            sent[-1].start()
        sum_factors(small, normed, low_buf, d_buf, former, summed)
        for move in sent:
            move.wait()


def heads(rows, half=None):
    return pl.BlockSpec((GROUP, rows, LANES), lambda step, place: (step, 0 if half is None else place[half], 0))


def triple(rows, half=None):
    return pl.BlockSpec((3, GROUP, rows, LANES), lambda step, place: (0, step, 0 if half is None else place[half], 0))


def backward_near(place, count, qkv, mixed, aux, d_mixed, kept, other, inner, d_middle, lows, vectors, factors, weight, former, carried):
    pairs, rows = qkv.shape[1:3]
    span, width = rows // 2, inner.shape[1]
    summed = jax.ShapeDtypeStruct((4 * RANK, width), jnp.float32)
    partial_sums = pl.BlockSpec((span, GROUP * LANES), lambda step, place: (0, step))
    return pl.pallas_call(
        partial(near_kernel, count),
        grid_spec=pltpu.PrefetchScalarGridSpec(
            num_scalar_prefetch=1, grid=(pairs // GROUP,),
            in_specs=[held(vectors.shape), held(factors.shape), held(former.shape), triple(span, 2)] + [heads(span, 2)] * 3
            + [partial_sums] * 2 + anywhere(5),
            out_specs=[held(summed.shape)] + anywhere(1 + count),
            scratch_shapes=[
                pltpu.VMEM((3, pairs, span, LANES), jnp.bfloat16),
                pltpu.VMEM(weight.shape, jnp.bfloat16),
                pltpu.VMEM((span, width), jnp.bfloat16),
                pltpu.VMEM((span, width), jnp.float32),
                pltpu.VMEM((span, SMALL), jnp.bfloat16),
                pltpu.VMEM((span, width), jnp.bfloat16),
                pltpu.VMEM((span, width), jnp.bfloat16),
                pltpu.VMEM(carried.shape, carried.dtype),
                pltpu.SemaphoreType.DMA((6 + count,)),
            ]),
        out_shape=[summed, jax.ShapeDtypeStruct(carried.shape, carried.dtype)] + [jax.ShapeDtypeStruct((span // count, width), jnp.bfloat16)] * count,
        compiler_params=pltpu.CompilerParams(vmem_limit_bytes=VMEM),
        cost_estimate=pl.CostEstimate(flops=20 << 30, bytes_accessed=20 << 20, transcendentals=0),
        name="backward_near",
    )(place, vectors, factors, former, qkv, mixed, aux, d_mixed, kept, other, inner, d_middle, lows, weight, carried)


def standardize(values):
    centred = values - jnp.mean(values, axis=-1, keepdims=True)
    inverse = lax.rsqrt(jnp.mean(centred * centred, axis=-1, keepdims=True) + epsilon)
    return centred * inverse, inverse


def pull_norm(grad, standard, inverse, gain):
    scaled = grad * gain
    centred = scaled - jnp.mean(scaled, axis=-1, keepdims=True)
    return inverse * (centred - standard * jnp.mean(scaled * standard, axis=-1, keepdims=True))


def side_by_side(ref, part):
    return jnp.concatenate([ref[pair, part] for pair in range(ref.shape[0])], axis=1)


def spread(ref, part, values):
    for pair in range(ref.shape[0]):
        ref[pair, part] = values[:, pair * LANES:(pair + 1) * LANES].astype(ref.dtype)


def held(shape):
    return pl.BlockSpec(shape, lambda step, place: (0,) * len(shape), pipeline_mode=pl.Buffered(1))


def deal_kernel(tokens, *refs):
    count = tokens.shape[0]
    blocks, held, semaphores = refs[:count], refs[count], refs[count + 1]
    me = lax.axis_index("blk")
    order = list(range(count // 2, count)) + list(range(count // 2))
    pulled = [pltpu.make_async_copy(tokens.at[me ^ index], held.at[index], semaphores.at[index]) for index in order]
    pushed = [pltpu.make_async_copy(held.at[index], blocks[index], semaphores.at[count + index]) for index in order]
    for move in pulled:
        move.start()
    for pull, push in zip(pulled, pushed):
        pull.wait()
        push.start()
    for move in pushed:
        move.wait()


def deal(tokens):
    count = tokens.shape[0]
    return pl.pallas_call(
        deal_kernel,
        in_specs=anywhere(1),
        out_specs=anywhere(count),
        out_shape=[jax.ShapeDtypeStruct(tokens.shape[1:], tokens.dtype)] * count,
        scratch_shapes=[pltpu.VMEM(tokens.shape, tokens.dtype), pltpu.SemaphoreType.DMA((2 * count,))],
        compiler_params=pltpu.CompilerParams(vmem_limit_bytes=VMEM),
        name="deal",
    )(tokens)


def gather_kernel(place, far, *refs):
    count = len(refs) - 4
    near, out, arrived, made, semaphores = refs[:count], refs[count], *refs[count + 1:]
    copy = copier(semaphores)
    slots, moves, sent = [], [], []
    for index in range(count):
        slots.append(place[1] * count + index)
        moves.append(copy(far.at[slots[-1]], arrived.at[index]))
    for index, block in enumerate(near):
        slots.append(place[0] ^ index)
        moves.append(copy(block, arrived.at[count + index]))
    for index, slot in enumerate(slots):
        moves[index].wait()
        made[index] = arrived[index].astype(made.dtype)
        sent.append(copy(made.at[index], out.at[slot]))
    for move in sent:
        move.wait()


def gather(place, far, near, dtype):
    return pl.pallas_call(
        gather_kernel,
        in_specs=[pl.BlockSpec(memory_space=pltpu.SMEM)] + anywhere(1 + len(near)),
        out_specs=anywhere(1)[0],
        out_shape=jax.ShapeDtypeStruct(far.shape, dtype),
        scratch_shapes=[pltpu.VMEM(far.shape, far.dtype), pltpu.VMEM(far.shape, dtype), pltpu.SemaphoreType.DMA((2 * far.shape[0],))],
        compiler_params=pltpu.CompilerParams(vmem_limit_bytes=VMEM),
        cost_estimate=pl.CostEstimate(flops=0, bytes_accessed=8 << 20, transcendentals=0),
        name="gather",
    )(place, far, *near)


def copier(semaphores):
    started = []

    def copy(source, target):
        move = pltpu.make_async_copy(source, target, semaphores.at[len(started)])
        started.append(move)
        move.start()
        return move

    return copy


def pieces_of(rows, size):
    return [slice(start, start + size) for start in range(0, rows, size)]


def anywhere(count):
    return [pl.BlockSpec(memory_space=pl.ANY)] * count


def project_rows(parts, vectors, factors, token_buf, normed, low_buf, weight_of, qkv_buf, finished):
    width = token_buf.shape[1]
    lane = lax.broadcasted_iota(jnp.int32, (width, LANES), 0) // HD
    each = jnp.where(lane == lax.broadcasted_iota(jnp.int32, (width, LANES), 1), 1.0, 0.0).astype(jnp.bfloat16)
    peaks = []
    for t in range(3):
        weight = weight_of(t)
        peak = None
        for index, part in enumerate(parts):
            own = slice(index * STEP, (index + 1) * STEP)
            if t == 0:
                standard, _ = standardize(token_buf[part].astype(jnp.float32))
                normed[own] = (standard * vectors[GAIN:GAIN + 1] + vectors[SHIFT:SHIFT + 1]).astype(jnp.bfloat16)
                low_buf[own] = nt(normed[own], factors[:SMALL]).astype(jnp.bfloat16)
            values = nn(normed[own], weight) + vectors[JOINT + t:JOINT + t + 1]
            if t != 1:
                start = SMALL if t == 0 else 2 * SMALL
                values = values + nn(low_buf[own], factors[start:start + SMALL])
            values = values.astype(jnp.bfloat16)
            spread(qkv_buf.at[t], part, values)
            if t < 2:
                new = jnp.max(nn(values * values, each).reshape(-1, 8, LANES), axis=0)
                peak = new if index == 0 else jnp.maximum(peak, new)
        peaks.append(peak)
        finished(t)
    return peaks[:2]


def block_part(place, index, count, rows, base):
    return pl.ds(pl.multiple_of(base + (place[0] % count ^ index) * rows, rows), rows)


def project_kernel(side, count, place, vectors, factors, weight, *refs):
    blocks = refs[:count]
    qkv, lows, inner, peaks, token_buf, weight_buf, normed, qkv_buf, low_buf, semaphores = refs[-10:]
    copy = copier(semaphores)
    rows, width = blocks[0].shape
    span = rows * count
    mine = pl.ds(pl.multiple_of(place[side] * span, span), span)
    arrivals = [copy(block, token_buf.at[block_part(place, index, count, rows, 0)]) for index, block in enumerate(blocks)]
    weights = [copy(weight.at[:, part], weight_buf.at[t]) for t, part in enumerate(pieces_of(weight.shape[1], width))]
    for arrival in arrivals:
        arrival.wait()
    sent = [copy(token_buf, inner.at[mine])]

    def weight_of(t):
        weights[t].wait()
        return weight_buf[t]

    def finished(t):
        if t == 0:
            sent.append(copy(low_buf, lows.at[mine]))
        sent.append(copy(qkv_buf.at[t], qkv.at[t, :, mine]))

    found = project_rows(pieces_of(span, STEP), vectors, factors, token_buf, normed, low_buf, weight_of, qkv_buf, finished)
    for index, peak in enumerate(found):
        peaks[index] = peak
    for move in sent:
        move.wait()


def project(place, side, blocks, vectors, factors, weight, former=()):
    count = len(blocks)
    rows, width = blocks[0].shape
    parts = weight.shape[1] // width
    span, pairs = count * rows, width // LANES
    length = former[2].shape[0] if former else 2 * span
    return pl.pallas_call(
        partial(project_kernel, side, count),
        in_specs=[pl.BlockSpec(memory_space=pltpu.SMEM)] + [pl.BlockSpec(memory_space=pltpu.VMEM)] * 2 + anywhere(1 + count + len(former)),
        out_specs=anywhere(3) + [pl.BlockSpec(memory_space=pltpu.VMEM)],
        out_shape=[
            jax.ShapeDtypeStruct((parts, pairs, length, LANES), jnp.bfloat16),
            jax.ShapeDtypeStruct((length, SMALL), jnp.bfloat16),
            jax.ShapeDtypeStruct((length, width), jnp.bfloat16),
            jax.ShapeDtypeStruct((2, 8, LANES), jnp.float32),
        ],
        scratch_shapes=[
            pltpu.VMEM((span, width), jnp.bfloat16),
            pltpu.VMEM((parts, width, width), jnp.bfloat16),
            pltpu.VMEM((span, width), jnp.bfloat16),
            pltpu.VMEM((parts, pairs, span, LANES), jnp.bfloat16),
            pltpu.VMEM((span, SMALL), jnp.bfloat16),
            pltpu.SemaphoreType.DMA((count + 2 * parts + 2,)),
        ],
        input_output_aliases={4 + count + index: index for index in range(len(former))},
        compiler_params=pltpu.CompilerParams(vmem_limit_bytes=VMEM),
        cost_estimate=pl.CostEstimate(flops=2 * span * width * width * parts, bytes_accessed=6 * width * width * 2, transcendentals=0),
        name="project",
    )(place, vectors, factors, weight, *blocks, *former)


def gelu_and_slope(u):
    c = (2.0 / jnp.pi) ** 0.5
    square = u * u
    share = 0.5 + 0.5 * jnp.tanh(u * (c + (c * 0.044715) * square))
    value = u * share
    slope = share + value * (1.0 - share) * (2 * c + (6 * c * 0.044715) * square)
    return value, slope


def forward_kernel(count, place, vectors, factors, near_peaks, far_peaks, weight, out_weight, up, down, *refs):
    blocks, refs = refs[:count], refs[count:]
    former_qkv, _, former_inner = refs[:3]
    qkv, lows, inner, mixed, aux, result, middle, slopes = refs[3:11]
    token_buf, normed, low_buf, qkv_buf, mixed_buf, aux_buf, out_buf, up_buf, down_buf, middle_buf, slope_buf, active, semaphores = refs[11:]
    copy = copier(semaphores)
    rows, width = blocks[0].shape
    span = rows * count
    length = former_inner.shape[0]
    far_base = pl.multiple_of(place[LAST] * span, span)
    far, others = pl.ds(far_base, span), []
    for index in range(1, length // span):
        others.append(pl.ds(pl.multiple_of((place[LAST] ^ index) * span, span), span))
    joint = pieces_of(weight.shape[1], width)
    columns = pieces_of(up.shape[1], width)
    arrivals = [copy(block, token_buf.at[block_part(place, index, count, rows, far_base)]) for index, block in enumerate(blocks)]
    weights = [copy(weight.at[:, part], slope_buf.at[:, part]) for part in joint]
    before = [copy(former_qkv.at[:, :, part], qkv_buf.at[:, :, part]) for part in others]
    fetched = [copy(former_inner.at[part], token_buf.at[part]) for part in others] + [copy(out_weight, out_buf)]
    ups = [copy(up.at[:, column], up_buf.at[t]) for t, column in enumerate(columns)]
    downs = copy(down, down_buf)
    for arrival in arrivals:
        arrival.wait()
    early = [copy(token_buf.at[far], inner.at[far])]

    def weight_of(t):
        weights[t].wait()
        return slope_buf[:, joint[t]]

    def finished(t):
        if t == 0:
            early.append(copy(low_buf, lows.at[far]))
        early.append(copy(qkv_buf.at[t, :, far], qkv.at[t, :, far]))

    parts = [pl.ds(pl.multiple_of(far_base + start, STEP), STEP) for start in range(0, span, STEP)]
    found = project_rows(parts, vectors, factors, token_buf, normed, low_buf, weight_of, qkv_buf, finished)
    tops = [jnp.maximum(found[index], jnp.maximum(near_peaks[index], far_peaks[index])) for index in range(2)]
    calm = jnp.max(tops[0]) * jnp.max(tops[1]) < (SAFE / HD ** -0.5) ** 2
    for move in before:
        move.wait()

    @pl.loop(0, qkv_buf.shape[1] // GROUP)
    def _(step):
        attend_forward(step * GROUP, GROUP, calm, place[3], qkv_buf, mixed_buf, aux_buf)

    for move in early + fetched:
        move.wait()
    sent = [copy(mixed_buf, mixed), copy(aux_buf, aux)]
    pieces = pieces_of(length, STEP)
    products = [nn(side_by_side(mixed_buf, pieces[0]), out_buf[...])]
    for index, rows in enumerate(pieces):
        if index + 1 < len(pieces):
            products.append(nn(side_by_side(mixed_buf, pieces[index + 1]), out_buf[...]))
        m = token_buf[rows].astype(jnp.float32) + products[index] + vectors[OUT:OUT + 1]
        middle_buf[rows] = m
        standard, _ = standardize(m)
        token_buf[rows] = (standard * vectors[GAIN_TWO:GAIN_TWO + 1] + vectors[SHIFT_TWO:SHIFT_TWO + 1]).astype(jnp.bfloat16)
    sent.append(copy(middle_buf, middle))

    def close(index, rows, local):
        token_buf[rows] = (middle_buf[rows] + vectors[DOWN:DOWN + 1] + nn(active[index % 2, local], down_buf[...])).astype(jnp.bfloat16)
        sent.append(copy(token_buf.at[rows], result.at[rows]))

    parts = pieces_of(length, CHUNK)
    pending = []
    for index, part in enumerate(parts):
        for t, column in enumerate(columns):
            if index == 0:
                ups[t].wait()
            hidden = nn(token_buf[part], up_buf[t]) + vectors[UP + t:UP + t + 1]
            if pending:
                close(*pending.pop(0))
            value, slope = gelu_and_slope(hidden)
            slope_buf[part, column] = slope.astype(jnp.bfloat16)
            active[index % 2, :, column] = value.astype(jnp.bfloat16)
        sent.append(copy(slope_buf.at[part], slopes.at[part]))
        if index == 0:
            downs.wait()
        for local in pieces_of(CHUNK, STEP):
            pending.append((index, slice(part.start + local.start, part.start + local.stop), local))
    for last in pending:
        close(*last)
    for move in sent:
        move.wait()


def forward(place, blocks, former, near_peaks, far_peaks, vectors, factors, weight, out_weight, up, down):
    count = len(blocks)
    rows, width = blocks[0].shape
    span, wide = count * rows, up.shape[1]
    qkv, lows, inner = former
    length = inner.shape[0]
    pairs = qkv.shape[1]
    moves = count + 3 + 2 * (length // span) + wide // width + 1 + 5 + 3 + length // CHUNK + length // STEP
    shape = jax.ShapeDtypeStruct
    return pl.pallas_call(
        partial(forward_kernel, count),
        in_specs=[pl.BlockSpec(memory_space=pltpu.SMEM)] + [pl.BlockSpec(memory_space=pltpu.VMEM)] * 4 + anywhere(4 + count + 3),
        out_specs=anywhere(8),
        out_shape=[
            shape(qkv.shape, qkv.dtype),
            shape(lows.shape, lows.dtype),
            shape(inner.shape, inner.dtype),
            shape(qkv.shape[1:], jnp.bfloat16),
            shape(qkv.shape[1:], jnp.bfloat16),
            shape((length, width), jnp.bfloat16),
            shape((length, width), jnp.float32),
            shape((length, wide), jnp.bfloat16),
        ],
        scratch_shapes=[
            pltpu.VMEM((length, width), jnp.bfloat16),
            pltpu.VMEM((span, width), jnp.bfloat16),
            pltpu.VMEM((span, SMALL), jnp.bfloat16),
            pltpu.VMEM(qkv.shape, jnp.bfloat16),
            pltpu.VMEM((pairs, length, LANES), jnp.bfloat16),
            pltpu.VMEM((pairs, length, LANES), jnp.bfloat16),
            pltpu.VMEM((width, width), jnp.bfloat16),
            pltpu.VMEM((wide // width, width, width), jnp.bfloat16),
            pltpu.VMEM((wide, width), jnp.bfloat16),
            pltpu.VMEM((length, width), jnp.float32),
            pltpu.VMEM((length, wide), jnp.bfloat16),
            pltpu.VMEM((2, CHUNK, wide), jnp.bfloat16),
            pltpu.SemaphoreType.DMA((moves,)),
        ],
        input_output_aliases={9 + count + index: index for index in range(3)},
        compiler_params=pltpu.CompilerParams(vmem_limit_bytes=VMEM),
        cost_estimate=pl.CostEstimate(flops=60 << 30, bytes_accessed=60 << 20, transcendentals=0),
        name="forward",
    )(place, vectors, factors, near_peaks, far_peaks, weight, out_weight, up, down, *blocks, *former)


def far_kernel(place, vectors, factors, outer, slopes, up, down, middle, out_weight, qkv, mixed, aux, inner, lows, weight, *refs):
    summed, d_middle, d_mixed, kept, other, grads = refs[:6]
    outer_buf, slope_buf, up_buf, down_buf, middle_buf, out_buf, d_mixed_buf, qkv_buf, mixed_buf, aux_buf, d_buf, other_buf, low_buf, semaphores = refs[6:]
    copy = copier(semaphores)
    length, width = outer.shape
    span = length // 2
    far_base, near_base = (pl.multiple_of(place[side] * span, span) for side in (1, 2))
    far, near = pl.ds(far_base, span), pl.ds(near_base, span)
    parts = pieces_of(length, CHUNK)
    columns = pieces_of(up.shape[1], width)
    outers, downs, slants = [], [], []
    for t, column in enumerate(columns):
        downs.append(copy(down.at[column], down_buf.at[column]))
        for part in parts:
            if t == 0:
                outers.append(copy(outer.at[part], outer_buf.at[part]))
            slants.append(copy(slopes.at[part, column], slope_buf.at[part, column]))
    late = [copy(out_weight, out_buf), copy(up, up_buf), copy(middle, middle_buf)]
    attended = [copy(qkv, qkv_buf), copy(mixed, mixed_buf), copy(aux, aux_buf)]
    for t, column in enumerate(columns):
        downs[t].wait()
        for index, part in enumerate(parts):
            if t == 0:
                outers[index].wait()
            slants[t * len(parts) + index].wait()
            d_active = nt(outer_buf[part], down_buf[column])
            slope_buf[part, column] = (d_active * slope_buf[part, column].astype(jnp.float32)).astype(jnp.bfloat16)
    for ready in late:
        ready.wait()
    starts = [near_base + start for start in range(0, span, STEP)] + [far_base + start for start in range(0, span, STEP)]
    for index, start in enumerate(starts):
        rows = pl.ds(pl.multiple_of(start, STEP), STEP)
        grad = nt(slope_buf[rows], up_buf[...])
        standard, inverse = standardize(middle_buf[rows])
        d = outer_buf[rows].astype(jnp.float32) + pull_norm(grad, standard, inverse, vectors[GAIN_TWO:GAIN_TWO + 1])
        middle_buf[rows] = d
        spread(d_mixed_buf, rows, nt(d.astype(jnp.bfloat16), out_buf[...]))
        if index + 1 == span // STEP:
            passed = copy(middle_buf.at[near], d_middle.at[near])
    sent = [copy(d_mixed_buf, d_mixed)]
    weight_buf = slope_buf.at[:, :weight.shape[1]]
    ready = [copy(weight, weight_buf), copy(inner.at[far], outer_buf.at[:span]), copy(lows.at[far], low_buf)]
    passed.wait()
    for move in attended:
        move.wait()

    def store(at, first, second):
        lanes = pl.ds(pl.multiple_of(at * LANES, LANES), LANES)
        middle_buf[near, lanes] = first
        other_buf[:, lanes] = second

    @pl.loop(0, qkv_buf.shape[1] // GROUP)
    def _(step):
        attend_back_far(place, step * GROUP, GROUP, qkv_buf, mixed_buf, aux_buf, d_mixed_buf, d_buf, store)

    sent.append(copy(middle_buf.at[near], kept))
    sent.append(copy(other_buf, other))
    for move in ready:
        move.wait()
    normed, grad_buf = outer_buf.at[span:], slope_buf.at[:span, weight.shape[1]:]
    small = finish_grads(vectors, factors, d_buf, weight_buf, outer_buf.at[:span], middle_buf.at[far], normed, grad_buf)
    sent.append(copy(grad_buf, grads.at[far]))
    sum_factors(small, normed, low_buf, d_buf, None, summed)
    for move in sent:
        move.wait()


def backward_far(place, outer, slopes, up, down, middle, out_weight, qkv, mixed, aux, inner, lows, vectors, factors, weight):
    length, width = outer.shape
    span, wide, pairs = length // 2, up.shape[1], qkv.shape[1]
    shape = jax.ShapeDtypeStruct
    moves = length // CHUNK + (1 + length // CHUNK) * (wide // width) + 3 + 3 + 2 + 3 + 2 + 1
    return pl.pallas_call(
        far_kernel,
        in_specs=[pl.BlockSpec(memory_space=pltpu.SMEM)] + [pl.BlockSpec(memory_space=pltpu.VMEM)] * 2 + anywhere(12),
        out_specs=[pl.BlockSpec(memory_space=pltpu.VMEM)] + anywhere(5),
        out_shape=[
            shape((4 * RANK, width), jnp.float32),
            shape((length, width), jnp.float32),
            shape(mixed.shape, jnp.bfloat16),
            shape((span, width), jnp.float32),
            shape((span, width), jnp.float32),
            shape((length, width), jnp.bfloat16),
        ],
        scratch_shapes=[
            pltpu.VMEM((length, width), jnp.bfloat16),
            pltpu.VMEM((length, wide), jnp.bfloat16),
            pltpu.VMEM((width, wide), jnp.bfloat16),
            pltpu.VMEM((wide, width), jnp.bfloat16),
            pltpu.VMEM((length, width), jnp.float32),
            pltpu.VMEM((width, width), jnp.bfloat16),
            pltpu.VMEM(mixed.shape, jnp.bfloat16),
            pltpu.VMEM(qkv.shape, jnp.bfloat16),
            pltpu.VMEM(mixed.shape, jnp.bfloat16),
            pltpu.VMEM(mixed.shape, jnp.bfloat16),
            pltpu.VMEM((3, pairs, span, LANES), jnp.bfloat16),
            pltpu.VMEM((span, width), jnp.float32),
            pltpu.VMEM((span, SMALL), jnp.bfloat16),
            pltpu.SemaphoreType.DMA((moves,)),
        ],
        compiler_params=pltpu.CompilerParams(vmem_limit_bytes=VMEM),
        cost_estimate=pl.CostEstimate(flops=80 << 30, bytes_accessed=60 << 20, transcendentals=0),
        name="backward_far",
    )(place, vectors, factors, outer, slopes, up, down, middle, out_weight, qkv, mixed, aux, inner, lows, weight)


def sum_over(v, axis, steps):
    size = lax.axis_size(axis)
    if size & (size - 1):
        return lax.psum(v, axis) if 1 in steps else v
    others = [
        lax.ppermute(v, axis, [(i, i ^ step) for i in range(size)]) for step in steps if step < size
    ]
    return sum(others, v)


def whole_slots(
    tokens,
    lengths,
    norm_gain,
    norm_shift,
    joint_weight,
    query_bias,
    value_bias,
    output_weight,
    output_bias,
    second_gain,
    second_shift,
    upward_weight,
    upward_bias,
    down_weight,
    down_bias,
    query_down,
    query_up,
    value_down,
    value_up,
    cotangent,
):
    seqs_here, rows, width = tokens.shape
    ranks = lax.axis_size("blk")
    half = ranks // 2
    adapter = 32.0 / RANK

    def partner(index):
        return [(i, i ^ index) for i in range(ranks)]

    me = lax.axis_index("blk")
    side = me // half
    quarter = 2 * (1 - side) + (me % half) // (half // 2)
    place = jnp.stack((me, 1 - side, side, lengths[me], quarter, quarter ^ 1)).astype(jnp.int32)
    vectors = jnp.concatenate(
        (
            norm_gain,
            norm_shift,
            query_bias,
            jnp.zeros_like(query_bias),
            value_bias,
            output_bias,
            second_gain,
            second_shift,
            down_bias,
            upward_bias,
        )
    )
    vectors = vectors.astype(jnp.float32).reshape(-1, width)
    factors = jnp.concatenate(
        (
            jnp.pad(jnp.concatenate((query_down, value_down), axis=1).T, ((0, 2 * RANK), (0, 0))),
            jnp.pad(adapter * query_up, ((0, 3 * RANK), (0, 0))).astype(jnp.bfloat16),
            jnp.pad(adapter * value_up, ((RANK, 2 * RANK), (0, 0))).astype(jnp.bfloat16),
        )
    )
    own, *others = deal(tokens)
    far = [lax.ppermute(others[k - 1], "blk", partner(k)) for k in range(half, ranks)]
    near = [own] + [lax.ppermute(others[k - 1], "blk", partner(k)) for k in range(1, half)]
    *former, near_peaks = project(place, 2, near, vectors, factors, joint_weight)
    first, last = far[: half // 2], far[half // 2 :]
    *former, far_peaks = project(place, FIRST, first, vectors, factors, joint_weight, former)
    cotangent, _ = lax.optimization_barrier((cotangent, (near_peaks, far_peaks, last[:-1])))
    outer = lax.all_to_all(cotangent, "blk", 0, 0, tiled=True).reshape(-1, width)
    qkv, lows, inner, mixed, aux, result, middle, slopes = forward(
        place,
        last,
        former,
        near_peaks,
        far_peaks,
        vectors,
        factors,
        joint_weight,
        output_weight,
        upward_weight,
        down_weight,
    )
    result, middle, slopes, outer = lax.optimization_barrier((result, middle, slopes, outer))
    block_output = lax.all_to_all(
        result.reshape(ranks, rows, width), "blk", 0, 0, tiled=True
    )
    shared = (vectors, factors, joint_weight)
    far_factors, d_middle, d_mixed, kept, other, far_grads = backward_far(
        place,
        outer,
        slopes,
        upward_weight,
        down_weight,
        middle,
        output_weight,
        qkv,
        mixed,
        aux,
        inner,
        lows,
        *shared,
    )
    far_grads = lax.all_to_all(far_grads.reshape(ranks, rows, width), "blk", 0, 0, tiled=True)
    packed, block_output, *near_grads = backward_near(
        place,
        half,
        qkv,
        mixed,
        aux,
        d_mixed,
        kept,
        other,
        inner,
        d_middle,
        lows,
        *shared,
        far_factors,
        block_output,
    )
    near_grads = near_grads[:1] + [
        lax.ppermute(near_grads[k], "blk", partner(k)) for k in range(1, half)
    ]
    for step in (1, 2, 4, 8):
        packed = sum_over(packed, "batch", [step])
    packed = sum_over(packed, "blk", [1])
    packed, near_grads = lax.optimization_barrier((packed, near_grads))
    packed = sum_over(packed, "blk", range(2, ranks, 2))
    token_grads = gather(place, far_grads, near_grads, jnp.float32)
    query_down_grad, value_down_grad = packed[:RANK].T, packed[RANK : 2 * RANK].T
    query_up_grad, value_up_grad = packed[2 * RANK : 3 * RANK], packed[3 * RANK :]
    return (
        block_output,
        token_grads,
        query_down_grad,
        query_up_grad,
        value_down_grad,
        value_up_grad,
    )


def body(
    tokens,
    lengths,
    norm_gain,
    norm_shift,
    joint_weight,
    query_bias,
    value_bias,
    output_weight,
    output_bias,
    second_gain,
    second_shift,
    upward_weight,
    upward_bias,
    down_weight,
    down_bias,
    query_down,
    query_up,
    value_down,
    value_up,
    cotangent,
):
    seqs_here, rows, width = tokens.shape
    heads = width // HD
    positions = seqs_here * rows
    length_all = rows * lax.axis_size("blk")
    scale = HD ** (-0.5)
    adapter = 32.0 / RANK
    flat = tokens.reshape(positions, width).astype(jnp.float32)
    normed_full, standard, inverse = normalize(flat, norm_gain, norm_shift)
    normed = normed_full.astype(jnp.bfloat16)
    joint = jnp.dot(normed, joint_weight, preferred_element_type=jnp.float32)
    query_low = jnp.dot(normed, query_down, preferred_element_type=jnp.float32).astype(jnp.bfloat16)
    value_low = jnp.dot(normed, value_down, preferred_element_type=jnp.float32).astype(jnp.bfloat16)
    queries = (
        joint[:, :width]
        + query_bias.astype(jnp.float32)
        + adapter * jnp.dot(query_low, query_up, preferred_element_type=jnp.float32)
    ).astype(jnp.bfloat16)
    keys_here = joint[:, width : 2 * width].astype(jnp.bfloat16)
    values_here = (
        joint[:, 2 * width :]
        + value_bias.astype(jnp.float32)
        + adapter * jnp.dot(value_low, value_up, preferred_element_type=jnp.float32)
    ).astype(jnp.bfloat16)
    query_heads = queries.reshape(seqs_here, rows, heads, HD)
    key_blocks = keys_here.reshape(seqs_here, rows, width)
    value_blocks = values_here.reshape(seqs_here, rows, width)
    device = lax.axis_index("blk")
    query_place = device * rows + jnp.arange(rows, dtype=jnp.int32)
    limits = lengths[:, None, None, None]

    def visible(query_pos, key_pos):
        return (key_pos[None, None, None, :] <= query_pos[None, None, :, None]) & (
            key_pos[None, None, None, :] < limits
        )

    running = jnp.full((seqs_here, heads, rows), masked_value, jnp.float32)
    key_piece = lax.all_gather(key_blocks, "blk", axis=1, tiled=True)
    value_piece = lax.all_gather(value_blocks, "blk", axis=1, tiled=True)
    count = key_piece.shape[1]
    key_heads = key_piece.reshape(seqs_here, count, heads, HD)
    value_heads = value_piece.reshape(seqs_here, count, heads, HD)
    allowed = visible(query_place, jnp.arange(count, dtype=jnp.int32))
    scores = (
        jnp.einsum("sqhd,skhd->shqk", query_heads, key_heads, preferred_element_type=jnp.float32)
        * scale
    )
    masked = jnp.where(allowed, scores, masked_value)
    highest = jnp.maximum(running, jnp.max(masked, axis=-1))
    weights = jnp.where(allowed, jnp.exp(masked - highest[..., None]), 0.0)
    totals = jnp.sum(weights, axis=-1)
    update = jnp.einsum(
        "shqk,skhd->sqhd",
        weights.astype(jnp.bfloat16),
        value_heads,
        preferred_element_type=jnp.float32,
    )
    summed = update
    running, totals, summed = (highest, totals, summed)
    mixed_full = summed / jnp.transpose(totals, (0, 2, 1))[..., None]
    log_total = running + jnp.log(totals)
    mixed_low = mixed_full.reshape(positions, width).astype(jnp.bfloat16)
    middle = (
        flat
        + jnp.dot(mixed_low, output_weight, preferred_element_type=jnp.float32)
        + output_bias.astype(jnp.float32)
    )
    normed_two_full, standard_two, inverse_two = normalize(middle, second_gain, second_shift)
    normed_two = normed_two_full.astype(jnp.bfloat16)
    hidden = jnp.dot(
        normed_two, upward_weight, preferred_element_type=jnp.float32
    ) + upward_bias.astype(jnp.float32)
    active_full, gelu_pull = jax.vjp(partial(jax.nn.gelu, approximate=True), hidden)
    active = active_full.astype(jnp.bfloat16)
    block_output = (
        (
            middle
            + jnp.dot(active, down_weight, preferred_element_type=jnp.float32)
            + down_bias.astype(jnp.float32)
        )
        .astype(jnp.bfloat16)
        .reshape(seqs_here, rows, width)
    )
    outer = cotangent.reshape(positions, width)
    d_active = against(outer, down_weight)
    d_hidden = gelu_pull(d_active)[0].astype(jnp.bfloat16)
    d_normed_two = against(d_hidden, upward_weight)
    d_middle = outer.astype(jnp.float32) + norm_back(
        d_normed_two, standard_two, inverse_two, second_gain
    )
    d_branch = d_middle.astype(jnp.bfloat16)
    d_mixed = against(d_branch, output_weight).astype(jnp.bfloat16)
    d_mixed_heads = d_mixed.reshape(seqs_here, rows, heads, HD)
    delta = jnp.transpose(
        jnp.sum(d_mixed_heads.astype(jnp.float32) * mixed_full, axis=-1), (0, 2, 1)
    )
    key_all, value_all = (
        lax.all_gather(key_blocks, "blk", axis=1, tiled=True),
        lax.all_gather(value_blocks, "blk", axis=1, tiled=True),
    )
    key_heads_all = key_all.reshape(seqs_here, length_all, heads, HD)
    value_heads_all = value_all.reshape(seqs_here, length_all, heads, HD)
    allowed_all = visible(query_place, jnp.arange(length_all, dtype=jnp.int32))
    scores = (
        jnp.einsum(
            "sqhd,skhd->shqk", query_heads, key_heads_all, preferred_element_type=jnp.float32
        )
        * scale
    )
    probs = jnp.where(allowed_all, jnp.exp(scores - log_total[..., None]), 0.0)
    d_probs = jnp.einsum(
        "sqhd,skhd->shqk", d_mixed_heads, value_heads_all, preferred_element_type=jnp.float32
    )
    d_scores = (probs * (d_probs - delta[..., None])).astype(jnp.bfloat16)
    d_queries = (
        jnp.einsum("shqk,skhd->sqhd", d_scores, key_heads_all, preferred_element_type=jnp.float32)
        * scale
    )
    d_keys_all = (
        jnp.einsum("shqk,sqhd->kshd", d_scores, query_heads, preferred_element_type=jnp.float32)
        * scale
    )
    d_values_all = jnp.einsum(
        "shqk,sqhd->kshd",
        probs.astype(jnp.bfloat16),
        d_mixed_heads,
        preferred_element_type=jnp.float32,
    )
    stacked = jnp.stack(
        (
            d_keys_all.reshape(length_all, seqs_here, width),
            d_values_all.reshape(length_all, seqs_here, width),
        ),
        axis=2,
    )
    owned = lax.psum_scatter(
        stacked.astype(jnp.bfloat16), "blk", scatter_dimension=0, tiled=True
    ).astype(jnp.float32)
    d_keys = jnp.transpose(owned[:, :, 0], (1, 0, 2)).reshape(positions, width)
    d_values = jnp.transpose(owned[:, :, 1], (1, 0, 2)).reshape(positions, width)
    d_query_low = d_queries.reshape(positions, width).astype(jnp.bfloat16)
    d_key_low = d_keys.astype(jnp.bfloat16)
    d_value_low = d_values.astype(jnp.bfloat16)
    query_up_grad = adapter * transposed(query_low, d_query_low)
    value_up_grad = adapter * transposed(value_low, d_value_low)
    d_query_small = (adapter * against(d_query_low, query_up)).astype(jnp.bfloat16)
    d_value_small = (adapter * against(d_value_low, value_up)).astype(jnp.bfloat16)
    query_down_grad = transposed(normed, d_query_small)
    value_down_grad = transposed(normed, d_value_small)
    d_joint = jnp.concatenate((d_query_low, d_key_low, d_value_low), axis=1)
    d_normed = (
        against(d_joint, joint_weight)
        + against(d_query_small, query_down)
        + against(d_value_small, value_down)
    )
    token_grads = (d_middle + norm_back(d_normed, standard, inverse, norm_gain)).reshape(
        seqs_here, rows, width
    )
    sums = lax.psum(
        (query_down_grad, query_up_grad, value_down_grad, value_up_grad), ("batch", "blk")
    )
    return (block_output, token_grads, sums[0], sums[1], sums[2], sums[3])


def choose(tokens, *others):
    seqs, rows = tokens.shape[:2]
    ranks = lax.axis_size("blk")
    fits = seqs == ranks and ranks > 1 and not ranks & (ranks - 1)
    fits = fits and rows % LANES == 0 and (ranks // 2 * rows) % CHUNK == 0
    return (whole_slots if fits else body)(tokens, *others)


def solution(mesh):
    placed = (
        P("batch", "blk", None),
        P("batch"),
        P(),
        P(),
        P(),
        P(),
        P(),
        P(),
        P(),
        P(),
        P(),
        P(),
        P(),
        P(),
        P(),
        P(),
        P(),
        P(),
        P(),
        P("batch", "blk", None),
    )
    return jax.shard_map(
        choose,
        mesh=mesh,
        in_specs=placed,
        out_specs=(P("batch", "blk", None), P("batch", "blk", None), P(), P(), P(), P()),
        check_vma=False,
    )
```

```python
from functools import partial

import jax
import jax.numpy as jnp
from jax import lax
from jax.experimental import pallas as pl
from jax.experimental.pallas import tpu as pltpu
from jax.sharding import PartitionSpec as P

HD = 64
RANK = 4
LANES = 128
STEP = 256
FULL = 512
SAFE = 80.0
GROUP = 2
CHUNK = 512
TILE = 1024
VMEM = 62 << 20
GAIN = 0
SHIFT = 1
JOINT = 2
OUT = 5
GAIN_TWO = 6
SHIFT_TWO = 7
DOWN = 8
UP = 9
SMALL = 16
FIRST = 4
LAST = 5


epsilon = 1e-05
masked_value = -1e30


def normalize(values, gain, shift):
    centred = values - jnp.mean(values, axis=-1, keepdims=True)
    inverse = lax.rsqrt(jnp.mean(centred * centred, axis=-1, keepdims=True) + epsilon)
    standard = centred * inverse
    return (standard * gain.astype(jnp.float32) + shift.astype(jnp.float32), standard, inverse)


def norm_back(grad, standard, inverse, gain):
    scaled = grad * gain.astype(jnp.float32)
    centred = scaled - jnp.mean(scaled, axis=-1, keepdims=True)
    return inverse * (centred - standard * jnp.mean(scaled * standard, axis=-1, keepdims=True))


def transposed(left, right):
    return lax.dot_general(
        left, right, (((0,), (0,)), ((), ())), preferred_element_type=jnp.float32
    )


def against(left, right):
    return lax.dot_general(
        left, right, (((1,), (1,)), ((), ())), preferred_element_type=jnp.float32
    )


def nt(a, b):
    return lax.dot_general(a, b, (((1,), (1,)), ((), ())), preferred_element_type=jnp.float32)


def tn(a, b):
    return lax.dot_general(a, b, (((0,), (0,)), ((), ())), preferred_element_type=jnp.float32)


def nn(a, b):
    return jnp.dot(a, b, preferred_element_type=jnp.float32)


def thirds(x):
    first = x.astype(jnp.bfloat16)
    rest = x - first.astype(jnp.float32)
    second = rest.astype(jnp.bfloat16)
    third = (rest - second.astype(jnp.float32)).astype(jnp.bfloat16)
    return first, second, third


def in_first_head():
    return lax.broadcasted_iota(jnp.int32, (1, LANES), 1) < HD


def spare_lane():
    return lax.broadcasted_iota(jnp.int32, (1, LANES), 1) % HD


def key_extras(begin, rows, length):
    place = begin + lax.broadcasted_iota(jnp.int32, (rows, LANES), 0)
    bias = jnp.where(place < length, 0.0, masked_value).astype(jnp.bfloat16)
    spare = spare_lane()
    return jnp.where(spare == 0, bias, jnp.where(spare < 4, jnp.bfloat16(1), jnp.bfloat16(0)))


def attend_forward(base, group, calm, length, qkv, mixed_ref, aux_ref):
    q_ref, k_ref, v_ref = (qkv.at[part] for part in range(3))
    rows = q_ref.shape[1]
    one, zero = jnp.bfloat16(1), jnp.bfloat16(0)
    first, spare = in_first_head(), spare_lane()
    extras = key_extras(0, rows, length)
    lead = jnp.where(spare == 0, one, zero)
    causal = lax.broadcasted_iota(jnp.int32, (STEP, STEP), 1) <= lax.broadcasted_iota(jnp.int32, (STEP, STEP), 0)

    def widen(pair):
        q, k, v = q_ref[base + pair] * jnp.bfloat16(HD ** -0.5), k_ref[base + pair], v_ref[base + pair]
        q_aug = [jnp.where(first, q, lead), jnp.where(first, lead, q)]
        k_aug = [jnp.where(first, k, extras), jnp.where(first, extras, k)]
        v_aug = [jnp.where(first, v, one), jnp.where(first, one, v)]
        return q_aug, k_aug, v_aug

    def write(pair, start, sums, tops):
        total = jnp.where(first, sums[1], sums[0])
        mixed = jnp.where(first, sums[0], sums[1]) * pltpu.roll(1.0 / total, HD, 1)
        mixed_ref[base + pair, start:start + STEP] = mixed.astype(jnp.bfloat16)
        level = jnp.log(total)
        if tops is not None:
            level = level + jnp.where(first, tops[1], tops[0])
        aux = lead
        for index, part in enumerate(thirds(-level)):
            aux = jnp.where(spare == index + 1, part, aux)
        aux_ref[base + pair, start:start + STEP] = aux

    @pl.when(calm)
    def _():
        ready = widen(0)
        for pair in range(group):
            q_aug, k_aug, v_aug = ready
            sums = [[None] * (rows // STEP) for _ in range(2)]
            for start in range(0, rows, STEP):
                stop = start + STEP
                for h in range(2):
                    s = nt(q_aug[h][start:], k_aug[h][start:stop])
                    w = jnp.exp(jnp.where(causal, s[:STEP], masked_value)).astype(jnp.bfloat16)
                    if stop < rows:
                        w = jnp.concatenate([w, jnp.exp(s[STEP:]).astype(jnp.bfloat16)], axis=0)
                    o = nn(w, v_aug[h][start:stop])
                    for part in range(start // STEP, rows // STEP):
                        add = o[part * STEP - start:(part + 1) * STEP - start]
                        sums[h][part] = add if start == 0 else sums[h][part] + add
                if start == 0 and pair + 1 < group:
                    ready = widen(pair + 1)
                write(pair, start, [sums[0][start // STEP], sums[1][start // STEP]], None)

    @pl.when(jnp.logical_not(calm))
    def _():
        for pair in range(group):
            q_aug, k_aug, v_aug = widen(pair)
            for start in range(0, rows, STEP):
                stop = start + STEP
                sums, tops = [], []
                for h in range(2):
                    s = nt(q_aug[h][start:stop], k_aug[h][:stop])
                    edge = jnp.where(causal, s[:, start:], masked_value)
                    s = edge if start == 0 else jnp.concatenate([s[:, :start], edge], axis=1)
                    tops.append(jnp.max(s, axis=1, keepdims=True))
                    w = jnp.exp(s - tops[h]).astype(jnp.bfloat16)
                    sums.append(nn(w, v_aug[h][:stop]))
                write(pair, start, sums, tops)


def widen_backward(pair, extras, q_ref, k_ref, v_ref, mixed_ref, aux_ref, do_ref):
    one, zero = jnp.bfloat16(1), jnp.bfloat16(0)
    first, spare = in_first_head(), spare_lane()
    three = jnp.where(spare < 3, one, zero)
    row = lax.broadcasted_iota(jnp.int32, (LANES, LANES), 0) // HD
    column = lax.broadcasted_iota(jnp.int32, (LANES, LANES), 1) // HD
    cross = jnp.where(row != column, one, zero)
    q, k, v = q_ref[pair] * jnp.bfloat16(HD ** -0.5), k_ref[pair], v_ref[pair]
    do, aux = do_ref[pair], aux_ref[pair]
    k_aug = [jnp.where(first, k, extras), jnp.where(first, extras, k)]
    q_aug = [jnp.where(first, q, aux), jnp.where(first, aux, q)]
    v_aug = [jnp.where(first, v, three), jnp.where(first, three, v)]
    product = do.astype(jnp.float32) * mixed_ref[pair].astype(jnp.float32)
    high = product.astype(jnp.bfloat16)
    low = (product - high.astype(jnp.float32)).astype(jnp.bfloat16)
    delta = nn(high, cross) + nn(low, cross)
    extra = zero
    for index, part in enumerate(thirds(-delta)):
        extra = jnp.where(spare == index, part, extra)
    do_aug = [jnp.where(first, do, extra), jnp.where(first, extra, do)]
    return (q, do, *q_aug, *do_aug), (k, *k_aug, *v_aug)


def square_back(asking, asked, causal):
    q, do = asking[:2]
    k = asked[0]
    rows = q.shape[0]
    first = in_first_head()
    allowed = lax.broadcasted_iota(jnp.int32, (STEP, STEP), 0) <= lax.broadcasted_iota(jnp.int32, (STEP, STEP), 1)
    d_queries, d_keys, d_values = [None] * (rows // STEP), [], []
    size = STEP if causal else FULL
    for start in range(0, rows, size):
        stop = start + size
        begin = start if causal else 0
        dks, dvs, dqs = [], [], []
        for h in range(2):
            s = nt(asked[1 + h][start:stop], asking[2 + h][begin:])
            if causal:
                edge = jnp.where(allowed, s[:, :STEP], masked_value)
                s = edge if stop == rows else jnp.concatenate([edge, s[:, STEP:]], axis=1)
            p = jnp.exp(s)
            dp = nt(asked[3 + h][start:stop], asking[4 + h][begin:])
            ds = (p * dp).astype(jnp.bfloat16)
            dvs.append(nn(p.astype(jnp.bfloat16), do[begin:]))
            dks.append(nn(ds, q[begin:]))
            dqs.append(tn(ds, k[start:stop]))
        d_values.append(jnp.where(first, dvs[0], dvs[1]))
        d_keys.append(jnp.where(first, dks[0], dks[1]))
        dq = jnp.where(first, dqs[0], dqs[1])
        for part in range(begin // STEP, rows // STEP):
            add = dq[part * STEP - begin:(part + 1) * STEP - begin]
            d_queries[part] = add if d_queries[part] is None else d_queries[part] + add
    return [jnp.concatenate(parts, axis=0) for parts in (d_queries, d_keys, d_values)]


def attend_back_far(place, base, group, qkv, mixed, aux, d_mixed, d_buf, store):
    views = (qkv.at[0], qkv.at[1], qkv.at[2], mixed, aux, d_mixed)
    rows = mixed.shape[1]
    span = rows // 2
    low_far = place[1] == 0
    extras = key_extras(0, rows, place[3])
    ready = widen_backward(base, extras, *views)
    for pair in range(group):
        asking, asked = ready
        late = [x[span:] for x in asking]
        early = [x[:span] for x in asked]
        cross_q, cross_k, cross_v = square_back(late, early, False)
        if pair + 1 < group:
            ready = widen_backward(base + pair + 1, extras, *views)
        far_asking = [jnp.where(low_far, x[:span], x[span:]) for x in asking]
        far_asked = [jnp.where(low_far, x[:span], x[span:]) for x in asked]
        d_q, d_k, d_v = square_back(far_asking, far_asked, True)
        at = base + pair
        d_buf[0, at] = ((d_q + jnp.where(low_far, 0.0, cross_q)) * HD ** -0.5).astype(jnp.bfloat16)
        d_buf[1, at] = (d_k + jnp.where(low_far, cross_k, 0.0)).astype(jnp.bfloat16)
        d_buf[2, at] = (d_v + jnp.where(low_far, cross_v, 0.0)).astype(jnp.bfloat16)
        store(at, jnp.where(low_far, cross_q, cross_k), cross_v)


def attend_back_near(place, step, qkv_ref, mixed_ref, aux_ref, do_ref, d_buf, kept_ref, other_ref):
    q_ref, k_ref, v_ref = (qkv_ref.at[part] for part in range(3))
    group, span = q_ref.shape[:2]
    low_far = place[1] == 0
    extras = key_extras(place[2] * span, span, place[3])
    ready = widen_backward(0, extras, q_ref, k_ref, v_ref, mixed_ref, aux_ref, do_ref)
    for pair in range(group):
        asking, asked = ready
        d_q, d_k, d_v = square_back(asking, asked, True)
        if pair + 1 < group:
            ready = widen_backward(pair + 1, extras, q_ref, k_ref, v_ref, mixed_ref, aux_ref, do_ref)
        kept, other = (ref[:, pair * LANES:(pair + 1) * LANES] for ref in (kept_ref, other_ref))
        at = step * group + pair
        d_buf[0, at] = ((d_q + jnp.where(low_far, kept, 0.0)) * HD ** -0.5).astype(jnp.bfloat16)
        d_buf[1, at] = (d_k + jnp.where(low_far, 0.0, kept)).astype(jnp.bfloat16)
        d_buf[2, at] = (d_v + jnp.where(low_far, 0.0, other)).astype(jnp.bfloat16)


def finish_grads(vectors, factors, d_buf, weight_buf, token_buf, middle_buf, normed, grad_buf):
    gain = vectors[GAIN:GAIN + 1]
    smalls = []
    for part in pieces_of(grad_buf.shape[0], STEP):
        d_parts = [side_by_side(d_buf.at[t], part) for t in range(d_buf.shape[0])]
        small = nt(d_parts[0], factors[SMALL:2 * SMALL]) + nt(d_parts[2], factors[2 * SMALL:])
        small = small.astype(jnp.bfloat16)
        d_normed = nt(jnp.concatenate(d_parts, axis=1), weight_buf[...]) + nn(small, factors[:SMALL])
        standard, inverse = standardize(token_buf[part].astype(jnp.float32))
        normed[part] = (standard * gain + vectors[SHIFT:SHIFT + 1]).astype(jnp.bfloat16)
        grad_buf[part] = (middle_buf[part] + pull_norm(d_normed, standard, inverse, gain)).astype(grad_buf.dtype)
        smalls.append(small)
    return jnp.concatenate(smalls, axis=0)


def sum_factors(small, normed, low_buf, d_buf, former, summed):
    everything = slice(None)
    scale = 32.0 / RANK
    downs = tn(small, normed[...])[:2 * RANK]
    ups = scale * jnp.concatenate(
        (
            tn(low_buf[...], side_by_side(d_buf.at[0], everything))[:RANK],
            tn(low_buf[...], side_by_side(d_buf.at[2], everything))[RANK:2 * RANK],
        )
    )
    if former is not None:
        downs, ups = former[:2 * RANK] + downs, former[2 * RANK:] + ups
    summed[:2 * RANK] = downs
    summed[2 * RANK:] = ups


def near_kernel(count, place, vectors, factors, former, qkv, mixed, aux, d_mixed, kept, other, inner, d_middle, lows, weight, carried, summed, landed, *refs):
    blocks, refs = refs[:count], refs[count:]
    d_buf, weight_buf, token_buf, middle_buf, low_buf, normed, grad_buf, held_buf, semaphores = refs
    step = pl.program_id(0)
    span = grad_buf.shape[0]
    rows = span // count
    mine = pl.ds(pl.multiple_of(place[2] * span, span), span)
    sources = [weight, inner.at[mine], d_middle.at[mine], lows.at[mine], carried]
    targets = [weight_buf, token_buf, middle_buf, low_buf, held_buf]
    fetched = [pltpu.make_async_copy(a, b, semaphores.at[i]) for i, (a, b) in enumerate(zip(sources, targets))]
    used = len(fetched)

    @pl.when(step == 0)
    def _():
        for move in fetched:
            move.start()

    attend_back_near(place, step, qkv, mixed, aux, d_mixed, d_buf, kept, other)

    @pl.when(step == pl.num_programs(0) - 1)
    def _():
        for move in fetched:
            move.wait()
        sent = [pltpu.make_async_copy(held_buf, landed, semaphores.at[used])]
        sent[0].start()
        small = finish_grads(vectors, factors, d_buf, weight_buf, token_buf, middle_buf, normed, grad_buf)
        for index, block in enumerate(blocks):
            part = block_part(place, index, count, rows, 0)
            sent.append(pltpu.make_async_copy(grad_buf.at[part], block, semaphores.at[used + 1 + index]))
            sent[-1].start()
        sum_factors(small, normed, low_buf, d_buf, former, summed)
        for move in sent:
            move.wait()


def heads(rows, half=None):
    return pl.BlockSpec((GROUP, rows, LANES), lambda step, place: (step, 0 if half is None else place[half], 0))


def triple(rows, half=None):
    return pl.BlockSpec((3, GROUP, rows, LANES), lambda step, place: (0, step, 0 if half is None else place[half], 0))


def backward_near(place, count, qkv, mixed, aux, d_mixed, kept, other, inner, d_middle, lows, vectors, factors, weight, former, carried):
    pairs, rows = qkv.shape[1:3]
    span, width = rows // 2, inner.shape[1]
    summed = jax.ShapeDtypeStruct((4 * RANK, width), jnp.float32)
    partial_sums = pl.BlockSpec((span, GROUP * LANES), lambda step, place: (0, step))
    return pl.pallas_call(
        partial(near_kernel, count),
        grid_spec=pltpu.PrefetchScalarGridSpec(
            num_scalar_prefetch=1, grid=(pairs // GROUP,),
            in_specs=[held(vectors.shape), held(factors.shape), held(former.shape), triple(span, 2)] + [heads(span, 2)] * 3
            + [partial_sums] * 2 + anywhere(5),
            out_specs=[held(summed.shape)] + anywhere(1 + count),
            scratch_shapes=[
                pltpu.VMEM((3, pairs, span, LANES), jnp.bfloat16),
                pltpu.VMEM(weight.shape, jnp.bfloat16),
                pltpu.VMEM((span, width), jnp.bfloat16),
                pltpu.VMEM((span, width), jnp.float32),
                pltpu.VMEM((span, SMALL), jnp.bfloat16),
                pltpu.VMEM((span, width), jnp.bfloat16),
                pltpu.VMEM((span, width), jnp.bfloat16),
                pltpu.VMEM(carried.shape, carried.dtype),
                pltpu.SemaphoreType.DMA((6 + count,)),
            ]),
        out_shape=[summed, jax.ShapeDtypeStruct(carried.shape, carried.dtype)] + [jax.ShapeDtypeStruct((span // count, width), jnp.bfloat16)] * count,
        compiler_params=pltpu.CompilerParams(vmem_limit_bytes=VMEM),
        cost_estimate=pl.CostEstimate(flops=20 << 30, bytes_accessed=20 << 20, transcendentals=0),
        name="backward_near",
    )(place, vectors, factors, former, qkv, mixed, aux, d_mixed, kept, other, inner, d_middle, lows, weight, carried)


def standardize(values):
    centred = values - jnp.mean(values, axis=-1, keepdims=True)
    inverse = lax.rsqrt(jnp.mean(centred * centred, axis=-1, keepdims=True) + epsilon)
    return centred * inverse, inverse


def pull_norm(grad, standard, inverse, gain):
    scaled = grad * gain
    centred = scaled - jnp.mean(scaled, axis=-1, keepdims=True)
    return inverse * (centred - standard * jnp.mean(scaled * standard, axis=-1, keepdims=True))


def side_by_side(ref, part):
    return jnp.concatenate([ref[pair, part] for pair in range(ref.shape[0])], axis=1)


def spread(ref, part, values):
    for pair in range(ref.shape[0]):
        ref[pair, part] = values[:, pair * LANES:(pair + 1) * LANES].astype(ref.dtype)


def held(shape):
    return pl.BlockSpec(shape, lambda step, place: (0,) * len(shape), pipeline_mode=pl.Buffered(1))


def deal_kernel(tokens, *refs):
    count = tokens.shape[0]
    blocks, held, semaphores = refs[:count], refs[count], refs[count + 1]
    me = lax.axis_index("blk")
    order = list(range(count // 2, count)) + list(range(count // 2))
    pulled = [pltpu.make_async_copy(tokens.at[me ^ index], held.at[index], semaphores.at[index]) for index in order]
    pushed = [pltpu.make_async_copy(held.at[index], blocks[index], semaphores.at[count + index]) for index in order]
    for move in pulled:
        move.start()
    for pull, push in zip(pulled, pushed):
        pull.wait()
        push.start()
    for move in pushed:
        move.wait()


def deal(tokens):
    count = tokens.shape[0]
    return pl.pallas_call(
        deal_kernel,
        in_specs=anywhere(1),
        out_specs=anywhere(count),
        out_shape=[jax.ShapeDtypeStruct(tokens.shape[1:], tokens.dtype)] * count,
        scratch_shapes=[pltpu.VMEM(tokens.shape, tokens.dtype), pltpu.SemaphoreType.DMA((2 * count,))],
        compiler_params=pltpu.CompilerParams(vmem_limit_bytes=VMEM),
        name="deal",
    )(tokens)


def gather_kernel(far, *refs):
    count = len(refs) - 4
    near, out, arrived, made, semaphores = refs[:count], refs[count], *refs[count + 1:]
    copy = copier(semaphores)
    me = lax.axis_index("blk")
    far_base = (1 - me // count) * count
    slots, moves, sent = [], [], []
    for index in range(count):
        slots.append(far_base + index)
        moves.append(copy(far.at[slots[-1]], arrived.at[index]))
    for index, block in enumerate(near):
        slots.append(me ^ index)
        moves.append(copy(block, arrived.at[count + index]))
    for index, slot in enumerate(slots):
        moves[index].wait()
        made[index] = arrived[index].astype(made.dtype)
        sent.append(copy(made.at[index], out.at[slot]))
    for move in sent:
        move.wait()


def gather(far, near, dtype):
    return pl.pallas_call(
        gather_kernel,
        in_specs=anywhere(1 + len(near)),
        out_specs=anywhere(1)[0],
        out_shape=jax.ShapeDtypeStruct(far.shape, dtype),
        scratch_shapes=[pltpu.VMEM(far.shape, far.dtype), pltpu.VMEM(far.shape, dtype), pltpu.SemaphoreType.DMA((2 * far.shape[0],))],
        compiler_params=pltpu.CompilerParams(vmem_limit_bytes=VMEM),
        cost_estimate=pl.CostEstimate(flops=0, bytes_accessed=8 << 20, transcendentals=0),
        name="gather",
    )(far, *near)


def copier(semaphores):
    started = []

    def copy(source, target):
        move = pltpu.make_async_copy(source, target, semaphores.at[len(started)])
        started.append(move)
        move.start()
        return move

    return copy


def pieces_of(rows, size):
    return [slice(start, start + size) for start in range(0, rows, size)]


def anywhere(count):
    return [pl.BlockSpec(memory_space=pl.ANY)] * count


def project_rows(parts, vectors, factors, token_buf, normed, low_buf, weight_of, qkv_buf, finished):
    width = token_buf.shape[1]
    lane = lax.broadcasted_iota(jnp.int32, (width, LANES), 0) // HD
    each = jnp.where(lane == lax.broadcasted_iota(jnp.int32, (width, LANES), 1), 1.0, 0.0).astype(jnp.bfloat16)
    peaks = []
    for t in range(3):
        weight = weight_of(t)
        peak = None
        for index, part in enumerate(parts):
            own = slice(index * STEP, (index + 1) * STEP)
            if t == 0:
                standard, _ = standardize(token_buf[part].astype(jnp.float32))
                normed[own] = (standard * vectors[GAIN:GAIN + 1] + vectors[SHIFT:SHIFT + 1]).astype(jnp.bfloat16)
                low_buf[own] = nt(normed[own], factors[:SMALL]).astype(jnp.bfloat16)
            values = nn(normed[own], weight) + vectors[JOINT + t:JOINT + t + 1]
            if t != 1:
                start = SMALL if t == 0 else 2 * SMALL
                values = values + nn(low_buf[own], factors[start:start + SMALL])
            values = values.astype(jnp.bfloat16)
            spread(qkv_buf.at[t], part, values)
            if t < 2:
                new = jnp.max(nn(values * values, each).reshape(-1, 8, LANES), axis=0)
                peak = new if index == 0 else jnp.maximum(peak, new)
        peaks.append(peak)
        finished(t)
    return peaks[:2]


def block_part(place, index, count, rows, base):
    return pl.ds(pl.multiple_of(base + (place[0] % count ^ index) * rows, rows), rows)


def project_kernel(side, count, place, vectors, factors, weight, *refs):
    blocks = refs[:count]
    qkv, lows, inner, peaks, token_buf, weight_buf, normed, qkv_buf, low_buf, semaphores = refs[-10:]
    copy = copier(semaphores)
    rows, width = blocks[0].shape
    span = rows * count
    mine = pl.ds(pl.multiple_of(place[side] * span, span), span)
    arrivals = [copy(block, token_buf.at[block_part(place, index, count, rows, 0)]) for index, block in enumerate(blocks)]
    weights = [copy(weight.at[:, part], weight_buf.at[t]) for t, part in enumerate(pieces_of(weight.shape[1], width))]
    for arrival in arrivals:
        arrival.wait()
    sent = [copy(token_buf, inner.at[mine])]

    def weight_of(t):
        weights[t].wait()
        return weight_buf[t]

    def finished(t):
        if t == 0:
            sent.append(copy(low_buf, lows.at[mine]))
        sent.append(copy(qkv_buf.at[t], qkv.at[t, :, mine]))

    found = project_rows(pieces_of(span, STEP), vectors, factors, token_buf, normed, low_buf, weight_of, qkv_buf, finished)
    for index, peak in enumerate(found):
        peaks[index] = peak
    for move in sent:
        move.wait()


def project(place, side, blocks, vectors, factors, weight, former=()):
    count = len(blocks)
    rows, width = blocks[0].shape
    parts = weight.shape[1] // width
    span, pairs = count * rows, width // LANES
    length = former[2].shape[0] if former else 2 * span
    return pl.pallas_call(
        partial(project_kernel, side, count),
        in_specs=[pl.BlockSpec(memory_space=pltpu.SMEM)] + [pl.BlockSpec(memory_space=pltpu.VMEM)] * 2 + anywhere(1 + count + len(former)),
        out_specs=anywhere(3) + [pl.BlockSpec(memory_space=pltpu.VMEM)],
        out_shape=[
            jax.ShapeDtypeStruct((parts, pairs, length, LANES), jnp.bfloat16),
            jax.ShapeDtypeStruct((length, SMALL), jnp.bfloat16),
            jax.ShapeDtypeStruct((length, width), jnp.bfloat16),
            jax.ShapeDtypeStruct((2, 8, LANES), jnp.float32),
        ],
        scratch_shapes=[
            pltpu.VMEM((span, width), jnp.bfloat16),
            pltpu.VMEM((parts, width, width), jnp.bfloat16),
            pltpu.VMEM((span, width), jnp.bfloat16),
            pltpu.VMEM((parts, pairs, span, LANES), jnp.bfloat16),
            pltpu.VMEM((span, SMALL), jnp.bfloat16),
            pltpu.SemaphoreType.DMA((count + 2 * parts + 2,)),
        ],
        input_output_aliases={4 + count + index: index for index in range(len(former))},
        compiler_params=pltpu.CompilerParams(vmem_limit_bytes=VMEM),
        cost_estimate=pl.CostEstimate(flops=2 * span * width * width * parts, bytes_accessed=6 * width * width * 2, transcendentals=0),
        name="project",
    )(place, vectors, factors, weight, *blocks, *former)


def gelu_and_slope(u):
    c = (2.0 / jnp.pi) ** 0.5
    square = u * u
    share = 0.5 + 0.5 * jnp.tanh(u * (c + (c * 0.044715) * square))
    value = u * share
    slope = share + value * (1.0 - share) * (2 * c + (6 * c * 0.044715) * square)
    return value, slope


def forward_kernel(count, place, vectors, factors, near_peaks, far_peaks, weight, out_weight, up, down, *refs):
    blocks, refs = refs[:count], refs[count:]
    former_qkv, _, former_inner = refs[:3]
    qkv, lows, inner, mixed, aux, result, middle, slopes = refs[3:11]
    token_buf, normed, low_buf, qkv_buf, mixed_buf, aux_buf, out_buf, up_buf, down_buf, middle_buf, slope_buf, active, semaphores = refs[11:]
    copy = copier(semaphores)
    rows, width = blocks[0].shape
    span = rows * count
    length = former_inner.shape[0]
    far_base = pl.multiple_of(place[LAST] * span, span)
    far, others = pl.ds(far_base, span), []
    for index in range(1, length // span):
        others.append(pl.ds(pl.multiple_of((place[LAST] ^ index) * span, span), span))
    joint = pieces_of(weight.shape[1], width)
    columns = pieces_of(up.shape[1], width)
    arrivals = [copy(block, token_buf.at[block_part(place, index, count, rows, far_base)]) for index, block in enumerate(blocks)]
    weights = [copy(weight.at[:, part], slope_buf.at[:, part]) for part in joint]
    before = [copy(former_qkv.at[:, :, part], qkv_buf.at[:, :, part]) for part in others]
    fetched = [copy(former_inner.at[part], token_buf.at[part]) for part in others] + [copy(out_weight, out_buf)]
    ups = [copy(up.at[:, column], up_buf.at[t]) for t, column in enumerate(columns)]
    downs = copy(down, down_buf)
    for arrival in arrivals:
        arrival.wait()
    early = [copy(token_buf.at[far], inner.at[far])]

    def weight_of(t):
        weights[t].wait()
        return slope_buf[:, joint[t]]

    def finished(t):
        if t == 0:
            early.append(copy(low_buf, lows.at[far]))
        early.append(copy(qkv_buf.at[t, :, far], qkv.at[t, :, far]))

    parts = [pl.ds(pl.multiple_of(far_base + start, STEP), STEP) for start in range(0, span, STEP)]
    found = project_rows(parts, vectors, factors, token_buf, normed, low_buf, weight_of, qkv_buf, finished)
    tops = [jnp.maximum(found[index], jnp.maximum(near_peaks[index], far_peaks[index])) for index in range(2)]
    calm = jnp.max(tops[0]) * jnp.max(tops[1]) < (SAFE / HD ** -0.5) ** 2
    for move in before:
        move.wait()

    @pl.loop(0, qkv_buf.shape[1] // GROUP)
    def _(step):
        attend_forward(step * GROUP, GROUP, calm, place[3], qkv_buf, mixed_buf, aux_buf)

    for move in early + fetched:
        move.wait()
    sent = [copy(mixed_buf, mixed), copy(aux_buf, aux)]
    pieces = pieces_of(length, STEP)
    products = [nn(side_by_side(mixed_buf, pieces[0]), out_buf[...])]
    for index, rows in enumerate(pieces):
        if index + 1 < len(pieces):
            products.append(nn(side_by_side(mixed_buf, pieces[index + 1]), out_buf[...]))
        m = token_buf[rows].astype(jnp.float32) + products[index] + vectors[OUT:OUT + 1]
        middle_buf[rows] = m
        standard, _ = standardize(m)
        token_buf[rows] = (standard * vectors[GAIN_TWO:GAIN_TWO + 1] + vectors[SHIFT_TWO:SHIFT_TWO + 1]).astype(jnp.bfloat16)
    sent.append(copy(middle_buf, middle))

    def close(index, rows, local):
        token_buf[rows] = (middle_buf[rows] + vectors[DOWN:DOWN + 1] + nn(active[index % 2, local], down_buf[...])).astype(jnp.bfloat16)
        sent.append(copy(token_buf.at[rows], result.at[rows]))

    parts = pieces_of(length, CHUNK)
    pending = []
    for index, part in enumerate(parts):
        for t, column in enumerate(columns):
            if index == 0:
                ups[t].wait()
            hidden = nn(token_buf[part], up_buf[t]) + vectors[UP + t:UP + t + 1]
            if pending:
                close(*pending.pop(0))
            value, slope = gelu_and_slope(hidden)
            slope_buf[part, column] = slope.astype(jnp.bfloat16)
            active[index % 2, :, column] = value.astype(jnp.bfloat16)
        sent.append(copy(slope_buf.at[part], slopes.at[part]))
        if index == 0:
            downs.wait()
        for local in pieces_of(CHUNK, STEP):
            pending.append((index, slice(part.start + local.start, part.start + local.stop), local))
    for last in pending:
        close(*last)
    for move in sent:
        move.wait()


def forward(place, blocks, former, near_peaks, far_peaks, vectors, factors, weight, out_weight, up, down):
    count = len(blocks)
    rows, width = blocks[0].shape
    span, wide = count * rows, up.shape[1]
    qkv, lows, inner = former
    length = inner.shape[0]
    pairs = qkv.shape[1]
    moves = count + 3 + 2 * (length // span) + wide // width + 1 + 5 + 3 + length // CHUNK + length // STEP
    shape = jax.ShapeDtypeStruct
    return pl.pallas_call(
        partial(forward_kernel, count),
        in_specs=[pl.BlockSpec(memory_space=pltpu.SMEM)] + [pl.BlockSpec(memory_space=pltpu.VMEM)] * 4 + anywhere(4) + [pl.BlockSpec(memory_space=pltpu.VMEM)] * count + anywhere(3),
        out_specs=anywhere(8),
        out_shape=[
            shape(qkv.shape, qkv.dtype),
            shape(lows.shape, lows.dtype),
            shape(inner.shape, inner.dtype),
            shape(qkv.shape[1:], jnp.bfloat16),
            shape(qkv.shape[1:], jnp.bfloat16),
            shape((length, width), jnp.bfloat16),
            shape((length, width), jnp.float32),
            shape((length, wide), jnp.bfloat16),
        ],
        scratch_shapes=[
            pltpu.VMEM((length, width), jnp.bfloat16),
            pltpu.VMEM((span, width), jnp.bfloat16),
            pltpu.VMEM((span, SMALL), jnp.bfloat16),
            pltpu.VMEM(qkv.shape, jnp.bfloat16),
            pltpu.VMEM((pairs, length, LANES), jnp.bfloat16),
            pltpu.VMEM((pairs, length, LANES), jnp.bfloat16),
            pltpu.VMEM((width, width), jnp.bfloat16),
            pltpu.VMEM((wide // width, width, width), jnp.bfloat16),
            pltpu.VMEM((wide, width), jnp.bfloat16),
            pltpu.VMEM((length, width), jnp.float32),
            pltpu.VMEM((length, wide), jnp.bfloat16),
            pltpu.VMEM((2, CHUNK, wide), jnp.bfloat16),
            pltpu.SemaphoreType.DMA((moves,)),
        ],
        input_output_aliases={9 + count + index: index for index in range(3)},
        compiler_params=pltpu.CompilerParams(vmem_limit_bytes=VMEM),
        cost_estimate=pl.CostEstimate(flops=60 << 30, bytes_accessed=60 << 20, transcendentals=0),
        name="forward",
    )(place, vectors, factors, near_peaks, far_peaks, weight, out_weight, up, down, *blocks, *former)


def far_kernel(place, vectors, factors, outer, slopes, up, down, middle, out_weight, qkv, mixed, aux, inner, lows, weight, *refs):
    summed, d_middle, d_mixed, kept, other, grads = refs[:6]
    outer_buf, slope_buf, up_buf, down_buf, middle_buf, out_buf, d_mixed_buf, qkv_buf, mixed_buf, aux_buf, d_buf, other_buf, low_buf, semaphores = refs[6:]
    copy = copier(semaphores)
    length, width = outer.shape
    span = length // 2
    far_base, near_base = (pl.multiple_of(place[side] * span, span) for side in (1, 2))
    far, near = pl.ds(far_base, span), pl.ds(near_base, span)
    parts = pieces_of(length, CHUNK)
    columns = pieces_of(up.shape[1], width)
    outers, downs, slants = [], [], []
    for t, column in enumerate(columns):
        downs.append(copy(down.at[column], down_buf.at[column]))
        for part in parts:
            if t == 0:
                outers.append(copy(outer.at[part], outer_buf.at[part]))
            slants.append(copy(slopes.at[part, column], slope_buf.at[part, column]))
    late = [copy(out_weight, out_buf), copy(up, up_buf), copy(middle, middle_buf)]
    attended = [copy(qkv, qkv_buf), copy(mixed, mixed_buf), copy(aux, aux_buf)]
    for t, column in enumerate(columns):
        downs[t].wait()
        for index, part in enumerate(parts):
            if t == 0:
                outers[index].wait()
            slants[t * len(parts) + index].wait()
            d_active = nt(outer_buf[part], down_buf[column])
            slope_buf[part, column] = (d_active * slope_buf[part, column].astype(jnp.float32)).astype(jnp.bfloat16)
    for ready in late:
        ready.wait()
    starts = [near_base + start for start in range(0, span, STEP)] + [far_base + start for start in range(0, span, STEP)]
    for index, start in enumerate(starts):
        rows = pl.ds(pl.multiple_of(start, STEP), STEP)
        grad = nt(slope_buf[rows], up_buf[...])
        standard, inverse = standardize(middle_buf[rows])
        d = outer_buf[rows].astype(jnp.float32) + pull_norm(grad, standard, inverse, vectors[GAIN_TWO:GAIN_TWO + 1])
        middle_buf[rows] = d
        spread(d_mixed_buf, rows, nt(d.astype(jnp.bfloat16), out_buf[...]))
        if index + 1 == span // STEP:
            passed = copy(middle_buf.at[near], d_middle.at[near])
    sent = [copy(d_mixed_buf, d_mixed)]
    weight_buf = slope_buf.at[:, :weight.shape[1]]
    ready = [copy(weight, weight_buf), copy(inner.at[far], outer_buf.at[:span]), copy(lows.at[far], low_buf)]
    passed.wait()
    for move in attended:
        move.wait()

    def store(at, first, second):
        lanes = pl.ds(pl.multiple_of(at * LANES, LANES), LANES)
        middle_buf[near, lanes] = first
        other_buf[:, lanes] = second

    @pl.loop(0, qkv_buf.shape[1] // GROUP)
    def _(step):
        attend_back_far(place, step * GROUP, GROUP, qkv_buf, mixed_buf, aux_buf, d_mixed_buf, d_buf, store)

    sent.append(copy(middle_buf.at[near], kept))
    sent.append(copy(other_buf, other))
    for move in ready:
        move.wait()
    normed, grad_buf = outer_buf.at[span:], slope_buf.at[:span, weight.shape[1]:]
    small = finish_grads(vectors, factors, d_buf, weight_buf, outer_buf.at[:span], middle_buf.at[far], normed, grad_buf)
    sent.append(copy(grad_buf, grads.at[far]))
    sum_factors(small, normed, low_buf, d_buf, None, summed)
    for move in sent:
        move.wait()


def backward_far(place, outer, slopes, up, down, middle, out_weight, qkv, mixed, aux, inner, lows, vectors, factors, weight):
    length, width = outer.shape
    span, wide, pairs = length // 2, up.shape[1], qkv.shape[1]
    shape = jax.ShapeDtypeStruct
    moves = length // CHUNK + (1 + length // CHUNK) * (wide // width) + 3 + 3 + 2 + 3 + 2 + 1
    return pl.pallas_call(
        far_kernel,
        in_specs=[pl.BlockSpec(memory_space=pltpu.SMEM)] + [pl.BlockSpec(memory_space=pltpu.VMEM)] * 2 + anywhere(12),
        out_specs=[pl.BlockSpec(memory_space=pltpu.VMEM)] + anywhere(5),
        out_shape=[
            shape((4 * RANK, width), jnp.float32),
            shape((length, width), jnp.float32),
            shape(mixed.shape, jnp.bfloat16),
            shape((span, width), jnp.float32),
            shape((span, width), jnp.float32),
            shape((length, width), jnp.bfloat16),
        ],
        scratch_shapes=[
            pltpu.VMEM((length, width), jnp.bfloat16),
            pltpu.VMEM((length, wide), jnp.bfloat16),
            pltpu.VMEM((width, wide), jnp.bfloat16),
            pltpu.VMEM((wide, width), jnp.bfloat16),
            pltpu.VMEM((length, width), jnp.float32),
            pltpu.VMEM((width, width), jnp.bfloat16),
            pltpu.VMEM(mixed.shape, jnp.bfloat16),
            pltpu.VMEM(qkv.shape, jnp.bfloat16),
            pltpu.VMEM(mixed.shape, jnp.bfloat16),
            pltpu.VMEM(mixed.shape, jnp.bfloat16),
            pltpu.VMEM((3, pairs, span, LANES), jnp.bfloat16),
            pltpu.VMEM((span, width), jnp.float32),
            pltpu.VMEM((span, SMALL), jnp.bfloat16),
            pltpu.SemaphoreType.DMA((moves,)),
        ],
        compiler_params=pltpu.CompilerParams(vmem_limit_bytes=VMEM),
        cost_estimate=pl.CostEstimate(flops=80 << 30, bytes_accessed=60 << 20, transcendentals=0),
        name="backward_far",
    )(place, vectors, factors, outer, slopes, up, down, middle, out_weight, qkv, mixed, aux, inner, lows, weight)


def swap(v, axis, steps):
    size = lax.axis_size(axis)
    return [lax.ppermute(v, axis, [(i, i ^ step) for i in range(size)]) for step in steps]


def sum_batch(v):
    size = lax.axis_size("batch")
    if size & (size - 1):
        return lax.psum(v, "batch")
    step = 1
    while step < size:
        (other,) = swap(v, "batch", [step])
        v, step = v + other, 2 * step
    return v


def whole_slots(
    tokens,
    lengths,
    norm_gain,
    norm_shift,
    joint_weight,
    query_bias,
    value_bias,
    output_weight,
    output_bias,
    second_gain,
    second_shift,
    upward_weight,
    upward_bias,
    down_weight,
    down_bias,
    query_down,
    query_up,
    value_down,
    value_up,
    cotangent,
):
    seqs_here, rows, width = tokens.shape
    ranks = lax.axis_size("blk")
    half = ranks // 2
    adapter = 32.0 / RANK

    def partner(index):
        return [(i, i ^ index) for i in range(ranks)]

    me = lax.axis_index("blk")
    side = me // half
    quarter = 2 * (1 - side) + (me % half) // (half // 2)
    place = jnp.stack((me, 1 - side, side, lengths[me], quarter, quarter ^ 1)).astype(jnp.int32)
    vectors = jnp.concatenate(
        (
            norm_gain,
            norm_shift,
            query_bias,
            jnp.zeros_like(query_bias),
            value_bias,
            output_bias,
            second_gain,
            second_shift,
            down_bias,
            upward_bias,
        )
    )
    vectors = vectors.astype(jnp.float32).reshape(-1, width)
    factors = jnp.concatenate(
        (
            jnp.pad(jnp.concatenate((query_down, value_down), axis=1).T, ((0, 2 * RANK), (0, 0))),
            jnp.pad(adapter * query_up, ((0, 3 * RANK), (0, 0))).astype(jnp.bfloat16),
            jnp.pad(adapter * value_up, ((RANK, 2 * RANK), (0, 0))).astype(jnp.bfloat16),
        )
    )
    own, *others = deal(tokens)
    far = [lax.ppermute(others[k - 1], "blk", partner(k)) for k in range(half, ranks)]
    near = [own] + [lax.ppermute(others[k - 1], "blk", partner(k)) for k in range(1, half)]
    *former, near_peaks = project(place, 2, near, vectors, factors, joint_weight)
    first, last = far[: half // 2], far[half // 2 :]
    *former, far_peaks = project(place, FIRST, first, vectors, factors, joint_weight, former)
    cotangent, _ = lax.optimization_barrier((cotangent, (near_peaks, far_peaks, last[:-1])))
    outer = lax.all_to_all(cotangent, "blk", 0, 0, tiled=True).reshape(-1, width)
    qkv, lows, inner, mixed, aux, result, middle, slopes = forward(
        place,
        last,
        former,
        near_peaks,
        far_peaks,
        vectors,
        factors,
        joint_weight,
        output_weight,
        upward_weight,
        down_weight,
    )
    result, middle, slopes, outer = lax.optimization_barrier((result, middle, slopes, outer))
    block_output = lax.all_to_all(
        result.reshape(ranks, rows, width), "blk", 0, 0, tiled=True
    )
    shared = (vectors, factors, joint_weight)
    far_factors, d_middle, d_mixed, kept, other, far_grads = backward_far(
        place,
        outer,
        slopes,
        upward_weight,
        down_weight,
        middle,
        output_weight,
        qkv,
        mixed,
        aux,
        inner,
        lows,
        *shared,
    )
    far_grads = lax.all_to_all(far_grads.reshape(ranks, rows, width), "blk", 0, 0, tiled=True)
    packed, block_output, *near_grads = backward_near(
        place,
        half,
        qkv,
        mixed,
        aux,
        d_mixed,
        kept,
        other,
        inner,
        d_middle,
        lows,
        *shared,
        far_factors,
        block_output,
    )
    near_grads = near_grads[:1] + [
        lax.ppermute(near_grads[k], "blk", partner(k)) for k in range(1, half)
    ]
    packed = sum_batch(packed)
    step = 1
    while step < ranks:
        if step == half:
            packed, near_grads = lax.optimization_barrier((packed, near_grads))
        (other,) = swap(packed, "blk", [step])
        packed, step = packed + other, 2 * step
    token_grads = gather(far_grads, near_grads, jnp.float32)
    query_down_grad, value_down_grad = packed[:RANK].T, packed[RANK : 2 * RANK].T
    query_up_grad, value_up_grad = packed[2 * RANK : 3 * RANK], packed[3 * RANK :]
    return (
        block_output,
        token_grads,
        query_down_grad,
        query_up_grad,
        value_down_grad,
        value_up_grad,
    )


def body(
    tokens,
    lengths,
    norm_gain,
    norm_shift,
    joint_weight,
    query_bias,
    value_bias,
    output_weight,
    output_bias,
    second_gain,
    second_shift,
    upward_weight,
    upward_bias,
    down_weight,
    down_bias,
    query_down,
    query_up,
    value_down,
    value_up,
    cotangent,
):
    seqs_here, rows, width = tokens.shape
    heads = width // HD
    positions = seqs_here * rows
    length_all = rows * lax.axis_size("blk")
    scale = HD ** (-0.5)
    adapter = 32.0 / RANK
    flat = tokens.reshape(positions, width).astype(jnp.float32)
    normed_full, standard, inverse = normalize(flat, norm_gain, norm_shift)
    normed = normed_full.astype(jnp.bfloat16)
    joint = jnp.dot(normed, joint_weight, preferred_element_type=jnp.float32)
    query_low = jnp.dot(normed, query_down, preferred_element_type=jnp.float32).astype(jnp.bfloat16)
    value_low = jnp.dot(normed, value_down, preferred_element_type=jnp.float32).astype(jnp.bfloat16)
    queries = (
        joint[:, :width]
        + query_bias.astype(jnp.float32)
        + adapter * jnp.dot(query_low, query_up, preferred_element_type=jnp.float32)
    ).astype(jnp.bfloat16)
    keys_here = joint[:, width : 2 * width].astype(jnp.bfloat16)
    values_here = (
        joint[:, 2 * width :]
        + value_bias.astype(jnp.float32)
        + adapter * jnp.dot(value_low, value_up, preferred_element_type=jnp.float32)
    ).astype(jnp.bfloat16)
    query_heads = queries.reshape(seqs_here, rows, heads, HD)
    key_blocks = keys_here.reshape(seqs_here, rows, width)
    value_blocks = values_here.reshape(seqs_here, rows, width)
    device = lax.axis_index("blk")
    query_place = device * rows + jnp.arange(rows, dtype=jnp.int32)
    limits = lengths[:, None, None, None]

    def visible(query_pos, key_pos):
        return (key_pos[None, None, None, :] <= query_pos[None, None, :, None]) & (
            key_pos[None, None, None, :] < limits
        )

    running = jnp.full((seqs_here, heads, rows), masked_value, jnp.float32)
    key_piece = lax.all_gather(key_blocks, "blk", axis=1, tiled=True)
    value_piece = lax.all_gather(value_blocks, "blk", axis=1, tiled=True)
    count = key_piece.shape[1]
    key_heads = key_piece.reshape(seqs_here, count, heads, HD)
    value_heads = value_piece.reshape(seqs_here, count, heads, HD)
    allowed = visible(query_place, jnp.arange(count, dtype=jnp.int32))
    scores = (
        jnp.einsum("sqhd,skhd->shqk", query_heads, key_heads, preferred_element_type=jnp.float32)
        * scale
    )
    masked = jnp.where(allowed, scores, masked_value)
    highest = jnp.maximum(running, jnp.max(masked, axis=-1))
    weights = jnp.where(allowed, jnp.exp(masked - highest[..., None]), 0.0)
    totals = jnp.sum(weights, axis=-1)
    update = jnp.einsum(
        "shqk,skhd->sqhd",
        weights.astype(jnp.bfloat16),
        value_heads,
        preferred_element_type=jnp.float32,
    )
    summed = update
    running, totals, summed = (highest, totals, summed)
    mixed_full = summed / jnp.transpose(totals, (0, 2, 1))[..., None]
    log_total = running + jnp.log(totals)
    mixed_low = mixed_full.reshape(positions, width).astype(jnp.bfloat16)
    middle = (
        flat
        + jnp.dot(mixed_low, output_weight, preferred_element_type=jnp.float32)
        + output_bias.astype(jnp.float32)
    )
    normed_two_full, standard_two, inverse_two = normalize(middle, second_gain, second_shift)
    normed_two = normed_two_full.astype(jnp.bfloat16)
    hidden = jnp.dot(
        normed_two, upward_weight, preferred_element_type=jnp.float32
    ) + upward_bias.astype(jnp.float32)
    active_full, gelu_pull = jax.vjp(partial(jax.nn.gelu, approximate=True), hidden)
    active = active_full.astype(jnp.bfloat16)
    block_output = (
        (
            middle
            + jnp.dot(active, down_weight, preferred_element_type=jnp.float32)
            + down_bias.astype(jnp.float32)
        )
        .astype(jnp.bfloat16)
        .reshape(seqs_here, rows, width)
    )
    outer = cotangent.reshape(positions, width)
    d_active = against(outer, down_weight)
    d_hidden = gelu_pull(d_active)[0].astype(jnp.bfloat16)
    d_normed_two = against(d_hidden, upward_weight)
    d_middle = outer.astype(jnp.float32) + norm_back(
        d_normed_two, standard_two, inverse_two, second_gain
    )
    d_branch = d_middle.astype(jnp.bfloat16)
    d_mixed = against(d_branch, output_weight).astype(jnp.bfloat16)
    d_mixed_heads = d_mixed.reshape(seqs_here, rows, heads, HD)
    delta = jnp.transpose(
        jnp.sum(d_mixed_heads.astype(jnp.float32) * mixed_full, axis=-1), (0, 2, 1)
    )
    key_all, value_all = (
        lax.all_gather(key_blocks, "blk", axis=1, tiled=True),
        lax.all_gather(value_blocks, "blk", axis=1, tiled=True),
    )
    key_heads_all = key_all.reshape(seqs_here, length_all, heads, HD)
    value_heads_all = value_all.reshape(seqs_here, length_all, heads, HD)
    allowed_all = visible(query_place, jnp.arange(length_all, dtype=jnp.int32))
    scores = (
        jnp.einsum(
            "sqhd,skhd->shqk", query_heads, key_heads_all, preferred_element_type=jnp.float32
        )
        * scale
    )
    probs = jnp.where(allowed_all, jnp.exp(scores - log_total[..., None]), 0.0)
    d_probs = jnp.einsum(
        "sqhd,skhd->shqk", d_mixed_heads, value_heads_all, preferred_element_type=jnp.float32
    )
    d_scores = (probs * (d_probs - delta[..., None])).astype(jnp.bfloat16)
    d_queries = (
        jnp.einsum("shqk,skhd->sqhd", d_scores, key_heads_all, preferred_element_type=jnp.float32)
        * scale
    )
    d_keys_all = (
        jnp.einsum("shqk,sqhd->kshd", d_scores, query_heads, preferred_element_type=jnp.float32)
        * scale
    )
    d_values_all = jnp.einsum(
        "shqk,sqhd->kshd",
        probs.astype(jnp.bfloat16),
        d_mixed_heads,
        preferred_element_type=jnp.float32,
    )
    stacked = jnp.stack(
        (
            d_keys_all.reshape(length_all, seqs_here, width),
            d_values_all.reshape(length_all, seqs_here, width),
        ),
        axis=2,
    )
    owned = lax.psum_scatter(
        stacked.astype(jnp.bfloat16), "blk", scatter_dimension=0, tiled=True
    ).astype(jnp.float32)
    d_keys = jnp.transpose(owned[:, :, 0], (1, 0, 2)).reshape(positions, width)
    d_values = jnp.transpose(owned[:, :, 1], (1, 0, 2)).reshape(positions, width)
    d_query_low = d_queries.reshape(positions, width).astype(jnp.bfloat16)
    d_key_low = d_keys.astype(jnp.bfloat16)
    d_value_low = d_values.astype(jnp.bfloat16)
    query_up_grad = adapter * transposed(query_low, d_query_low)
    value_up_grad = adapter * transposed(value_low, d_value_low)
    d_query_small = (adapter * against(d_query_low, query_up)).astype(jnp.bfloat16)
    d_value_small = (adapter * against(d_value_low, value_up)).astype(jnp.bfloat16)
    query_down_grad = transposed(normed, d_query_small)
    value_down_grad = transposed(normed, d_value_small)
    d_joint = jnp.concatenate((d_query_low, d_key_low, d_value_low), axis=1)
    d_normed = (
        against(d_joint, joint_weight)
        + against(d_query_small, query_down)
        + against(d_value_small, value_down)
    )
    token_grads = (d_middle + norm_back(d_normed, standard, inverse, norm_gain)).reshape(
        seqs_here, rows, width
    )
    sums = lax.psum(
        (query_down_grad, query_up_grad, value_down_grad, value_up_grad), ("batch", "blk")
    )
    return (block_output, token_grads, sums[0], sums[1], sums[2], sums[3])


def choose(tokens, *others):
    seqs, rows = tokens.shape[:2]
    ranks = lax.axis_size("blk")
    fits = seqs == ranks and ranks > 1 and not ranks & (ranks - 1)
    fits = fits and rows % LANES == 0 and (ranks // 2 * rows) % CHUNK == 0
    return (whole_slots if fits else body)(tokens, *others)


def solution(mesh):
    placed = (
        P("batch", "blk", None),
        P("batch"),
        P(),
        P(),
        P(),
        P(),
        P(),
        P(),
        P(),
        P(),
        P(),
        P(),
        P(),
        P(),
        P(),
        P(),
        P(),
        P(),
        P(),
        P("batch", "blk", None),
    )
    return jax.shard_map(
        choose,
        mesh=mesh,
        in_specs=placed,
        out_specs=(P("batch", "blk", None), P("batch", "blk", None), P(), P(), P(), P()),
        check_vma=False,
    )
```

```python
from functools import partial

import jax
import jax.numpy as jnp
from jax import lax
from jax.experimental import pallas as pl
from jax.experimental.pallas import tpu as pltpu
from jax.sharding import PartitionSpec as P

HD = 64
RANK = 4
LANES = 128
STEP = 256
FULL = 512
SAFE = 80.0
GROUP = 2
CHUNK = 512
TILE = 1024
VMEM = 62 << 20
GAIN = 0
SHIFT = 1
JOINT = 2
OUT = 5
GAIN_TWO = 6
SHIFT_TWO = 7
DOWN = 8
UP = 9
SMALL = 16
FIRST = 4
LAST = 5


epsilon = 1e-05
masked_value = -1e30


def normalize(values, gain, shift):
    centred = values - jnp.mean(values, axis=-1, keepdims=True)
    inverse = lax.rsqrt(jnp.mean(centred * centred, axis=-1, keepdims=True) + epsilon)
    standard = centred * inverse
    return (standard * gain.astype(jnp.float32) + shift.astype(jnp.float32), standard, inverse)


def norm_back(grad, standard, inverse, gain):
    scaled = grad * gain.astype(jnp.float32)
    centred = scaled - jnp.mean(scaled, axis=-1, keepdims=True)
    return inverse * (centred - standard * jnp.mean(scaled * standard, axis=-1, keepdims=True))


def transposed(left, right):
    return lax.dot_general(
        left, right, (((0,), (0,)), ((), ())), preferred_element_type=jnp.float32
    )


def against(left, right):
    return lax.dot_general(
        left, right, (((1,), (1,)), ((), ())), preferred_element_type=jnp.float32
    )


def nt(a, b):
    return lax.dot_general(a, b, (((1,), (1,)), ((), ())), preferred_element_type=jnp.float32)


def tn(a, b):
    return lax.dot_general(a, b, (((0,), (0,)), ((), ())), preferred_element_type=jnp.float32)


def nn(a, b):
    return jnp.dot(a, b, preferred_element_type=jnp.float32)


def thirds(x):
    first = x.astype(jnp.bfloat16)
    rest = x - first.astype(jnp.float32)
    second = rest.astype(jnp.bfloat16)
    third = (rest - second.astype(jnp.float32)).astype(jnp.bfloat16)
    return first, second, third


def in_first_head():
    return lax.broadcasted_iota(jnp.int32, (1, LANES), 1) < HD


def spare_lane():
    return lax.broadcasted_iota(jnp.int32, (1, LANES), 1) % HD


def key_extras(begin, rows, length):
    place = begin + lax.broadcasted_iota(jnp.int32, (rows, LANES), 0)
    bias = jnp.where(place < length, 0.0, masked_value).astype(jnp.bfloat16)
    spare = spare_lane()
    return jnp.where(spare == 0, bias, jnp.where(spare < 4, jnp.bfloat16(1), jnp.bfloat16(0)))


def attend_forward(base, group, calm, length, qkv, mixed_ref, aux_ref):
    q_ref, k_ref, v_ref = (qkv.at[part] for part in range(3))
    rows = q_ref.shape[1]
    one, zero = jnp.bfloat16(1), jnp.bfloat16(0)
    first, spare = in_first_head(), spare_lane()
    extras = key_extras(0, rows, length)
    lead = jnp.where(spare == 0, one, zero)
    causal = lax.broadcasted_iota(jnp.int32, (STEP, STEP), 1) <= lax.broadcasted_iota(jnp.int32, (STEP, STEP), 0)

    def widen(pair):
        q, k, v = q_ref[base + pair] * jnp.bfloat16(HD ** -0.5), k_ref[base + pair], v_ref[base + pair]
        q_aug = [jnp.where(first, q, lead), jnp.where(first, lead, q)]
        k_aug = [jnp.where(first, k, extras), jnp.where(first, extras, k)]
        v_aug = [jnp.where(first, v, one), jnp.where(first, one, v)]
        return q_aug, k_aug, v_aug

    def write(pair, start, sums, tops):
        total = jnp.where(first, sums[1], sums[0])
        mixed = jnp.where(first, sums[0], sums[1]) * pltpu.roll(1.0 / total, HD, 1)
        mixed_ref[base + pair, start:start + STEP] = mixed.astype(jnp.bfloat16)
        level = jnp.log(total)
        if tops is not None:
            level = level + jnp.where(first, tops[1], tops[0])
        aux = lead
        for index, part in enumerate(thirds(-level)):
            aux = jnp.where(spare == index + 1, part, aux)
        aux_ref[base + pair, start:start + STEP] = aux

    @pl.when(calm)
    def _():
        ready = widen(0)
        for pair in range(group):
            q_aug, k_aug, v_aug = ready
            sums = [[None] * (rows // STEP) for _ in range(2)]
            for start in range(0, rows, STEP):
                stop = start + STEP
                for h in range(2):
                    s = nt(q_aug[h][start:], k_aug[h][start:stop])
                    w = jnp.exp(jnp.where(causal, s[:STEP], masked_value)).astype(jnp.bfloat16)
                    if stop < rows:
                        w = jnp.concatenate([w, jnp.exp(s[STEP:]).astype(jnp.bfloat16)], axis=0)
                    o = nn(w, v_aug[h][start:stop])
                    for part in range(start // STEP, rows // STEP):
                        add = o[part * STEP - start:(part + 1) * STEP - start]
                        sums[h][part] = add if start == 0 else sums[h][part] + add
                if start == 0 and pair + 1 < group:
                    ready = widen(pair + 1)
                write(pair, start, [sums[0][start // STEP], sums[1][start // STEP]], None)

    @pl.when(jnp.logical_not(calm))
    def _():
        for pair in range(group):
            q_aug, k_aug, v_aug = widen(pair)
            for start in range(0, rows, STEP):
                stop = start + STEP
                sums, tops = [], []
                for h in range(2):
                    s = nt(q_aug[h][start:stop], k_aug[h][:stop])
                    edge = jnp.where(causal, s[:, start:], masked_value)
                    s = edge if start == 0 else jnp.concatenate([s[:, :start], edge], axis=1)
                    tops.append(jnp.max(s, axis=1, keepdims=True))
                    w = jnp.exp(s - tops[h]).astype(jnp.bfloat16)
                    sums.append(nn(w, v_aug[h][:stop]))
                write(pair, start, sums, tops)


def widen_backward(pair, extras, q_ref, k_ref, v_ref, mixed_ref, aux_ref, do_ref):
    one, zero = jnp.bfloat16(1), jnp.bfloat16(0)
    first, spare = in_first_head(), spare_lane()
    three = jnp.where(spare < 3, one, zero)
    row = lax.broadcasted_iota(jnp.int32, (LANES, LANES), 0) // HD
    column = lax.broadcasted_iota(jnp.int32, (LANES, LANES), 1) // HD
    cross = jnp.where(row != column, one, zero)
    q, k, v = q_ref[pair] * jnp.bfloat16(HD ** -0.5), k_ref[pair], v_ref[pair]
    do, aux = do_ref[pair], aux_ref[pair]
    k_aug = [jnp.where(first, k, extras), jnp.where(first, extras, k)]
    q_aug = [jnp.where(first, q, aux), jnp.where(first, aux, q)]
    v_aug = [jnp.where(first, v, three), jnp.where(first, three, v)]
    product = do.astype(jnp.float32) * mixed_ref[pair].astype(jnp.float32)
    high = product.astype(jnp.bfloat16)
    low = (product - high.astype(jnp.float32)).astype(jnp.bfloat16)
    delta = nn(high, cross) + nn(low, cross)
    extra = zero
    for index, part in enumerate(thirds(-delta)):
        extra = jnp.where(spare == index, part, extra)
    do_aug = [jnp.where(first, do, extra), jnp.where(first, extra, do)]
    return (q, do, *q_aug, *do_aug), (k, *k_aug, *v_aug)


def square_back(asking, asked, causal):
    q, do = asking[:2]
    k = asked[0]
    rows = q.shape[0]
    first = in_first_head()
    allowed = lax.broadcasted_iota(jnp.int32, (STEP, STEP), 0) <= lax.broadcasted_iota(jnp.int32, (STEP, STEP), 1)
    d_queries, d_keys, d_values = [None] * (rows // STEP), [], []
    size = STEP if causal else FULL
    for start in range(0, rows, size):
        stop = start + size
        begin = start if causal else 0
        dks, dvs, dqs = [], [], []
        for h in range(2):
            s = nt(asked[1 + h][start:stop], asking[2 + h][begin:])
            if causal:
                edge = jnp.where(allowed, s[:, :STEP], masked_value)
                s = edge if stop == rows else jnp.concatenate([edge, s[:, STEP:]], axis=1)
            p = jnp.exp(s)
            dp = nt(asked[3 + h][start:stop], asking[4 + h][begin:])
            ds = (p * dp).astype(jnp.bfloat16)
            dvs.append(nn(p.astype(jnp.bfloat16), do[begin:]))
            dks.append(nn(ds, q[begin:]))
            dqs.append(tn(ds, k[start:stop]))
        d_values.append(jnp.where(first, dvs[0], dvs[1]))
        d_keys.append(jnp.where(first, dks[0], dks[1]))
        dq = jnp.where(first, dqs[0], dqs[1])
        for part in range(begin // STEP, rows // STEP):
            add = dq[part * STEP - begin:(part + 1) * STEP - begin]
            d_queries[part] = add if d_queries[part] is None else d_queries[part] + add
    return [jnp.concatenate(parts, axis=0) for parts in (d_queries, d_keys, d_values)]


def attend_back_far(place, base, group, qkv, mixed, aux, d_mixed, d_buf, store):
    views = (qkv.at[0], qkv.at[1], qkv.at[2], mixed, aux, d_mixed)
    rows = mixed.shape[1]
    span = rows // 2
    low_far = place[1] == 0
    extras = key_extras(0, rows, place[3])
    ready = widen_backward(base, extras, *views)
    for pair in range(group):
        asking, asked = ready
        late = [x[span:] for x in asking]
        early = [x[:span] for x in asked]
        cross_q, cross_k, cross_v = square_back(late, early, False)
        if pair + 1 < group:
            ready = widen_backward(base + pair + 1, extras, *views)
        far_asking = [jnp.where(low_far, x[:span], x[span:]) for x in asking]
        far_asked = [jnp.where(low_far, x[:span], x[span:]) for x in asked]
        d_q, d_k, d_v = square_back(far_asking, far_asked, True)
        at = base + pair
        d_buf[0, at] = ((d_q + jnp.where(low_far, 0.0, cross_q)) * HD ** -0.5).astype(jnp.bfloat16)
        d_buf[1, at] = (d_k + jnp.where(low_far, cross_k, 0.0)).astype(jnp.bfloat16)
        d_buf[2, at] = (d_v + jnp.where(low_far, cross_v, 0.0)).astype(jnp.bfloat16)
        store(at, jnp.where(low_far, cross_q, cross_k), cross_v)


def attend_back_near(place, step, qkv_ref, mixed_ref, aux_ref, do_ref, d_buf, kept_ref, other_ref):
    q_ref, k_ref, v_ref = (qkv_ref.at[part] for part in range(3))
    group, span = q_ref.shape[:2]
    low_far = place[1] == 0
    extras = key_extras(place[2] * span, span, place[3])
    ready = widen_backward(0, extras, q_ref, k_ref, v_ref, mixed_ref, aux_ref, do_ref)
    for pair in range(group):
        asking, asked = ready
        d_q, d_k, d_v = square_back(asking, asked, True)
        if pair + 1 < group:
            ready = widen_backward(pair + 1, extras, q_ref, k_ref, v_ref, mixed_ref, aux_ref, do_ref)
        kept, other = (ref[:, pair * LANES:(pair + 1) * LANES] for ref in (kept_ref, other_ref))
        at = step * group + pair
        d_buf[0, at] = ((d_q + jnp.where(low_far, kept, 0.0)) * HD ** -0.5).astype(jnp.bfloat16)
        d_buf[1, at] = (d_k + jnp.where(low_far, 0.0, kept)).astype(jnp.bfloat16)
        d_buf[2, at] = (d_v + jnp.where(low_far, 0.0, other)).astype(jnp.bfloat16)


def finish_grads(vectors, factors, d_buf, weight_buf, token_buf, middle_buf, normed, grad_buf):
    gain = vectors[GAIN:GAIN + 1]
    smalls = []
    for part in pieces_of(grad_buf.shape[0], STEP):
        d_parts = [side_by_side(d_buf.at[t], part) for t in range(d_buf.shape[0])]
        small = nt(d_parts[0], factors[SMALL:2 * SMALL]) + nt(d_parts[2], factors[2 * SMALL:])
        small = small.astype(jnp.bfloat16)
        d_normed = nt(jnp.concatenate(d_parts, axis=1), weight_buf[...]) + nn(small, factors[:SMALL])
        standard, inverse = standardize(token_buf[part].astype(jnp.float32))
        normed[part] = (standard * gain + vectors[SHIFT:SHIFT + 1]).astype(jnp.bfloat16)
        grad_buf[part] = (middle_buf[part] + pull_norm(d_normed, standard, inverse, gain)).astype(grad_buf.dtype)
        smalls.append(small)
    return jnp.concatenate(smalls, axis=0)


def sum_factors(small, normed, low_buf, d_buf, former, summed):
    everything = slice(None)
    scale = 32.0 / RANK
    downs = tn(small, normed[...])[:2 * RANK]
    ups = scale * jnp.concatenate(
        (
            tn(low_buf[...], side_by_side(d_buf.at[0], everything))[:RANK],
            tn(low_buf[...], side_by_side(d_buf.at[2], everything))[RANK:2 * RANK],
        )
    )
    if former is not None:
        downs, ups = former[:2 * RANK] + downs, former[2 * RANK:] + ups
    summed[:2 * RANK] = downs
    summed[2 * RANK:] = ups


def near_kernel(count, place, vectors, factors, former, qkv, mixed, aux, d_mixed, kept, other, inner, d_middle, lows, weight, carried, summed, landed, *refs):
    blocks, refs = refs[:count], refs[count:]
    d_buf, weight_buf, token_buf, middle_buf, low_buf, normed, grad_buf, held_buf, semaphores = refs
    step = pl.program_id(0)
    span = grad_buf.shape[0]
    rows = span // count
    mine = pl.ds(pl.multiple_of(place[2] * span, span), span)
    sources = [weight, inner.at[mine], d_middle.at[mine], lows.at[mine], carried]
    targets = [weight_buf, token_buf, middle_buf, low_buf, held_buf]
    fetched = [pltpu.make_async_copy(a, b, semaphores.at[i]) for i, (a, b) in enumerate(zip(sources, targets))]
    used = len(fetched)

    @pl.when(step == 0)
    def _():
        for move in fetched:
            move.start()

    attend_back_near(place, step, qkv, mixed, aux, d_mixed, d_buf, kept, other)

    @pl.when(step == pl.num_programs(0) - 1)
    def _():
        for move in fetched:
            move.wait()
        sent = [pltpu.make_async_copy(held_buf, landed, semaphores.at[used])]
        sent[0].start()
        small = finish_grads(vectors, factors, d_buf, weight_buf, token_buf, middle_buf, normed, grad_buf)
        for index, block in enumerate(blocks):
            part = block_part(place, index, count, rows, 0)
            sent.append(pltpu.make_async_copy(grad_buf.at[part], block, semaphores.at[used + 1 + index]))
            sent[-1].start()
        sum_factors(small, normed, low_buf, d_buf, former, summed)
        for move in sent:
            move.wait()


def heads(rows, half=None):
    return pl.BlockSpec((GROUP, rows, LANES), lambda step, place: (step, 0 if half is None else place[half], 0))


def triple(rows, half=None):
    return pl.BlockSpec((3, GROUP, rows, LANES), lambda step, place: (0, step, 0 if half is None else place[half], 0))


def backward_near(place, count, qkv, mixed, aux, d_mixed, kept, other, inner, d_middle, lows, vectors, factors, weight, former, carried):
    pairs, rows = qkv.shape[1:3]
    span, width = rows // 2, inner.shape[1]
    summed = jax.ShapeDtypeStruct((4 * RANK, width), jnp.float32)
    partial_sums = pl.BlockSpec((span, GROUP * LANES), lambda step, place: (0, step))
    return pl.pallas_call(
        partial(near_kernel, count),
        grid_spec=pltpu.PrefetchScalarGridSpec(
            num_scalar_prefetch=1, grid=(pairs // GROUP,),
            in_specs=[held(vectors.shape), held(factors.shape), held(former.shape), triple(span, 2)] + [heads(span, 2)] * 3
            + [partial_sums] * 2 + anywhere(5),
            out_specs=[held(summed.shape)] + anywhere(1 + count),
            scratch_shapes=[
                pltpu.VMEM((3, pairs, span, LANES), jnp.bfloat16),
                pltpu.VMEM(weight.shape, jnp.bfloat16),
                pltpu.VMEM((span, width), jnp.bfloat16),
                pltpu.VMEM((span, width), jnp.float32),
                pltpu.VMEM((span, SMALL), jnp.bfloat16),
                pltpu.VMEM((span, width), jnp.bfloat16),
                pltpu.VMEM((span, width), jnp.bfloat16),
                pltpu.VMEM(carried.shape, carried.dtype),
                pltpu.SemaphoreType.DMA((6 + count,)),
            ]),
        out_shape=[summed, jax.ShapeDtypeStruct(carried.shape, carried.dtype)] + [jax.ShapeDtypeStruct((span // count, width), jnp.bfloat16)] * count,
        compiler_params=pltpu.CompilerParams(vmem_limit_bytes=VMEM),
        cost_estimate=pl.CostEstimate(flops=20 << 30, bytes_accessed=20 << 20, transcendentals=0),
        name="backward_near",
    )(place, vectors, factors, former, qkv, mixed, aux, d_mixed, kept, other, inner, d_middle, lows, weight, carried)


def standardize(values):
    centred = values - jnp.mean(values, axis=-1, keepdims=True)
    inverse = lax.rsqrt(jnp.mean(centred * centred, axis=-1, keepdims=True) + epsilon)
    return centred * inverse, inverse


def pull_norm(grad, standard, inverse, gain):
    scaled = grad * gain
    centred = scaled - jnp.mean(scaled, axis=-1, keepdims=True)
    return inverse * (centred - standard * jnp.mean(scaled * standard, axis=-1, keepdims=True))


def side_by_side(ref, part):
    return jnp.concatenate([ref[pair, part] for pair in range(ref.shape[0])], axis=1)


def spread(ref, part, values):
    for pair in range(ref.shape[0]):
        ref[pair, part] = values[:, pair * LANES:(pair + 1) * LANES].astype(ref.dtype)


def held(shape):
    return pl.BlockSpec(shape, lambda step, place: (0,) * len(shape), pipeline_mode=pl.Buffered(1))


def deal_kernel(tokens, *refs):
    count = tokens.shape[0]
    blocks, held, semaphores = refs[:count], refs[count], refs[count + 1]
    me = lax.axis_index("blk")
    order = list(range(count // 2, count)) + list(range(count // 2))
    pulled = [pltpu.make_async_copy(tokens.at[me ^ index], held.at[index], semaphores.at[index]) for index in order]
    pushed = [pltpu.make_async_copy(held.at[index], blocks[index], semaphores.at[count + index]) for index in order]
    for move in pulled:
        move.start()
    for pull, push in zip(pulled, pushed):
        pull.wait()
        push.start()
    for move in pushed:
        move.wait()


def deal(tokens):
    count = tokens.shape[0]
    return pl.pallas_call(
        deal_kernel,
        in_specs=anywhere(1),
        out_specs=anywhere(count),
        out_shape=[jax.ShapeDtypeStruct(tokens.shape[1:], tokens.dtype)] * count,
        scratch_shapes=[pltpu.VMEM(tokens.shape, tokens.dtype), pltpu.SemaphoreType.DMA((2 * count,))],
        compiler_params=pltpu.CompilerParams(vmem_limit_bytes=VMEM),
        name="deal",
    )(tokens)


def gather_kernel(far, *refs):
    count = len(refs) - 4
    near, out, arrived, made, semaphores = refs[:count], refs[count], *refs[count + 1:]
    copy = copier(semaphores)
    me = lax.axis_index("blk")
    far_base = (1 - me // count) * count
    slots, moves, sent = [], [], []
    for index in range(count):
        slots.append(far_base + index)
        moves.append(copy(far.at[slots[-1]], arrived.at[index]))
    for index, block in enumerate(near):
        slots.append(me ^ index)
        moves.append(copy(block, arrived.at[count + index]))
    for index, slot in enumerate(slots):
        moves[index].wait()
        made[index] = arrived[index].astype(made.dtype)
        sent.append(copy(made.at[index], out.at[slot]))
    for move in sent:
        move.wait()


def gather(far, near, dtype):
    return pl.pallas_call(
        gather_kernel,
        in_specs=anywhere(1 + len(near)),
        out_specs=anywhere(1)[0],
        out_shape=jax.ShapeDtypeStruct(far.shape, dtype),
        scratch_shapes=[pltpu.VMEM(far.shape, far.dtype), pltpu.VMEM(far.shape, dtype), pltpu.SemaphoreType.DMA((2 * far.shape[0],))],
        compiler_params=pltpu.CompilerParams(vmem_limit_bytes=VMEM),
        cost_estimate=pl.CostEstimate(flops=0, bytes_accessed=8 << 20, transcendentals=0),
        name="gather",
    )(far, *near)


def copier(semaphores):
    started = []

    def copy(source, target):
        move = pltpu.make_async_copy(source, target, semaphores.at[len(started)])
        started.append(move)
        move.start()
        return move

    return copy


def pieces_of(rows, size):
    return [slice(start, start + size) for start in range(0, rows, size)]


def anywhere(count):
    return [pl.BlockSpec(memory_space=pl.ANY)] * count


def project_rows(parts, vectors, factors, token_buf, normed, low_buf, weight_of, qkv_buf, finished):
    width = token_buf.shape[1]
    lane = lax.broadcasted_iota(jnp.int32, (width, LANES), 0) // HD
    each = jnp.where(lane == lax.broadcasted_iota(jnp.int32, (width, LANES), 1), 1.0, 0.0).astype(jnp.bfloat16)
    peaks = []
    for t in range(3):
        weight = weight_of(t)
        peak = None
        for index, part in enumerate(parts):
            own = slice(index * STEP, (index + 1) * STEP)
            if t == 0:
                standard, _ = standardize(token_buf[part].astype(jnp.float32))
                normed[own] = (standard * vectors[GAIN:GAIN + 1] + vectors[SHIFT:SHIFT + 1]).astype(jnp.bfloat16)
                low_buf[own] = nt(normed[own], factors[:SMALL]).astype(jnp.bfloat16)
            values = nn(normed[own], weight) + vectors[JOINT + t:JOINT + t + 1]
            if t != 1:
                start = SMALL if t == 0 else 2 * SMALL
                values = values + nn(low_buf[own], factors[start:start + SMALL])
            values = values.astype(jnp.bfloat16)
            spread(qkv_buf.at[t], part, values)
            if t < 2:
                new = jnp.max(nn(values * values, each).reshape(-1, 8, LANES), axis=0)
                peak = new if index == 0 else jnp.maximum(peak, new)
        peaks.append(peak)
        finished(t)
    return peaks[:2]


def block_part(place, index, count, rows, base):
    return pl.ds(pl.multiple_of(base + (place[0] % count ^ index) * rows, rows), rows)


def project_kernel(side, count, place, vectors, factors, weight, *refs):
    blocks = refs[:count]
    qkv, lows, inner, peaks, token_buf, weight_buf, normed, qkv_buf, low_buf, semaphores = refs[-10:]
    copy = copier(semaphores)
    rows, width = blocks[0].shape
    span = rows * count
    mine = pl.ds(pl.multiple_of(place[side] * span, span), span)
    arrivals = [copy(block, token_buf.at[block_part(place, index, count, rows, 0)]) for index, block in enumerate(blocks)]
    weights = [copy(weight.at[:, part], weight_buf.at[t]) for t, part in enumerate(pieces_of(weight.shape[1], width))]
    for arrival in arrivals:
        arrival.wait()
    sent = [copy(token_buf, inner.at[mine])]

    def weight_of(t):
        weights[t].wait()
        return weight_buf[t]

    def finished(t):
        if t == 0:
            sent.append(copy(low_buf, lows.at[mine]))
        sent.append(copy(qkv_buf.at[t], qkv.at[t, :, mine]))

    found = project_rows(pieces_of(span, STEP), vectors, factors, token_buf, normed, low_buf, weight_of, qkv_buf, finished)
    for index, peak in enumerate(found):
        peaks[index] = peak
    for move in sent:
        move.wait()


def project(place, side, blocks, vectors, factors, weight, former=()):
    count = len(blocks)
    rows, width = blocks[0].shape
    parts = weight.shape[1] // width
    span, pairs = count * rows, width // LANES
    length = former[2].shape[0] if former else 2 * span
    return pl.pallas_call(
        partial(project_kernel, side, count),
        in_specs=[pl.BlockSpec(memory_space=pltpu.SMEM)] + [pl.BlockSpec(memory_space=pltpu.VMEM)] * 2 + anywhere(1 + count + len(former)),
        out_specs=anywhere(3) + [pl.BlockSpec(memory_space=pltpu.VMEM)],
        out_shape=[
            jax.ShapeDtypeStruct((parts, pairs, length, LANES), jnp.bfloat16),
            jax.ShapeDtypeStruct((length, SMALL), jnp.bfloat16),
            jax.ShapeDtypeStruct((length, width), jnp.bfloat16),
            jax.ShapeDtypeStruct((2, 8, LANES), jnp.float32),
        ],
        scratch_shapes=[
            pltpu.VMEM((span, width), jnp.bfloat16),
            pltpu.VMEM((parts, width, width), jnp.bfloat16),
            pltpu.VMEM((span, width), jnp.bfloat16),
            pltpu.VMEM((parts, pairs, span, LANES), jnp.bfloat16),
            pltpu.VMEM((span, SMALL), jnp.bfloat16),
            pltpu.SemaphoreType.DMA((count + 2 * parts + 2,)),
        ],
        input_output_aliases={4 + count + index: index for index in range(len(former))},
        compiler_params=pltpu.CompilerParams(vmem_limit_bytes=VMEM),
        cost_estimate=pl.CostEstimate(flops=2 * span * width * width * parts, bytes_accessed=6 * width * width * 2, transcendentals=0),
        name="project",
    )(place, vectors, factors, weight, *blocks, *former)


def gelu_and_slope(u):
    c = (2.0 / jnp.pi) ** 0.5
    square = u * u
    share = 0.5 + 0.5 * jnp.tanh(u * (c + (c * 0.044715) * square))
    value = u * share
    near, part = share.astype(jnp.bfloat16), value.astype(jnp.bfloat16)
    bend = jnp.bfloat16(2 * c) + jnp.bfloat16(6 * c * 0.044715) * square.astype(jnp.bfloat16)
    slope = near + part * (jnp.bfloat16(1) - near) * bend
    return value, slope


def forward_kernel(count, place, vectors, factors, near_peaks, far_peaks, weight, out_weight, up, down, *refs):
    blocks, refs = refs[:count], refs[count:]
    former_qkv, _, former_inner = refs[:3]
    qkv, lows, inner, mixed, aux, result, middle, slopes = refs[3:11]
    token_buf, normed, low_buf, qkv_buf, mixed_buf, aux_buf, out_buf, up_buf, down_buf, middle_buf, slope_buf, active, semaphores = refs[11:]
    copy = copier(semaphores)
    rows, width = blocks[0].shape
    span = rows * count
    length = former_inner.shape[0]
    far_base = pl.multiple_of(place[LAST] * span, span)
    far, others = pl.ds(far_base, span), []
    for index in range(1, length // span):
        others.append(pl.ds(pl.multiple_of((place[LAST] ^ index) * span, span), span))
    joint = pieces_of(weight.shape[1], width)
    columns = pieces_of(up.shape[1], width)
    arrivals = [copy(block, token_buf.at[block_part(place, index, count, rows, far_base)]) for index, block in enumerate(blocks)]
    weights = [copy(weight.at[:, part], slope_buf.at[:, part]) for part in joint]
    before = [copy(former_qkv.at[:, :, part], qkv_buf.at[:, :, part]) for part in others]
    fetched = [copy(former_inner.at[part], token_buf.at[part]) for part in others] + [copy(out_weight, out_buf)]
    ups = [copy(up.at[:, column], up_buf.at[t]) for t, column in enumerate(columns)]
    downs = copy(down, down_buf)
    for arrival in arrivals:
        arrival.wait()
    early = [copy(token_buf.at[far], inner.at[far])]

    def weight_of(t):
        weights[t].wait()
        return slope_buf[:, joint[t]]

    def finished(t):
        if t == 0:
            early.append(copy(low_buf, lows.at[far]))
        early.append(copy(qkv_buf.at[t, :, far], qkv.at[t, :, far]))

    parts = [pl.ds(pl.multiple_of(far_base + start, STEP), STEP) for start in range(0, span, STEP)]
    found = project_rows(parts, vectors, factors, token_buf, normed, low_buf, weight_of, qkv_buf, finished)
    tops = [jnp.maximum(found[index], jnp.maximum(near_peaks[index], far_peaks[index])) for index in range(2)]
    calm = jnp.max(tops[0]) * jnp.max(tops[1]) < (SAFE / HD ** -0.5) ** 2
    for move in before:
        move.wait()

    @pl.loop(0, qkv_buf.shape[1] // GROUP)
    def _(step):
        attend_forward(step * GROUP, GROUP, calm, place[3], qkv_buf, mixed_buf, aux_buf)

    for move in early + fetched + ups + [downs]:
        move.wait()
    sent = [copy(mixed_buf, mixed), copy(aux_buf, aux)]
    pieces = pieces_of(length, STEP)
    products = [nn(side_by_side(mixed_buf, pieces[0]), out_buf[...])]
    for index, rows in enumerate(pieces):
        if index + 1 < len(pieces):
            products.append(nn(side_by_side(mixed_buf, pieces[index + 1]), out_buf[...]))
        m = token_buf[rows].astype(jnp.float32) + products[index] + vectors[OUT:OUT + 1]
        middle_buf[rows] = m
        standard, _ = standardize(m)
        token_buf[rows] = (standard * vectors[GAIN_TWO:GAIN_TWO + 1] + vectors[SHIFT_TWO:SHIFT_TWO + 1]).astype(jnp.bfloat16)
    sent.append(copy(middle_buf, middle))

    def close(index, rows, local):
        token_buf[rows] = (middle_buf[rows] + vectors[DOWN:DOWN + 1] + nn(active[index % 2, local], down_buf[...])).astype(jnp.bfloat16)
        sent.append(copy(token_buf.at[rows], result.at[rows]))

    parts = pieces_of(length, CHUNK)
    pending = []
    for index, part in enumerate(parts):
        for t, column in enumerate(columns):
            hidden = nn(token_buf[part], up_buf[t]) + vectors[UP + t:UP + t + 1]
            if pending:
                close(*pending.pop(0))
            value, slope = gelu_and_slope(hidden)
            slope_buf[part, column] = slope.astype(jnp.bfloat16)
            active[index % 2, :, column] = value.astype(jnp.bfloat16)
        sent.append(copy(slope_buf.at[part], slopes.at[part]))
        for local in pieces_of(CHUNK, STEP):
            pending.append((index, slice(part.start + local.start, part.start + local.stop), local))
    for last in pending:
        close(*last)
    for move in sent:
        move.wait()


def forward(place, blocks, former, near_peaks, far_peaks, vectors, factors, weight, out_weight, up, down):
    count = len(blocks)
    rows, width = blocks[0].shape
    span, wide = count * rows, up.shape[1]
    qkv, lows, inner = former
    length = inner.shape[0]
    pairs = qkv.shape[1]
    moves = count + 3 + 2 * (length // span) + wide // width + 1 + 5 + 3 + length // CHUNK + length // STEP
    shape = jax.ShapeDtypeStruct
    return pl.pallas_call(
        partial(forward_kernel, count),
        in_specs=[pl.BlockSpec(memory_space=pltpu.SMEM)] + [pl.BlockSpec(memory_space=pltpu.VMEM)] * 4 + anywhere(4) + [pl.BlockSpec(memory_space=pltpu.VMEM)] * count + anywhere(3),
        out_specs=anywhere(8),
        out_shape=[
            shape(qkv.shape, qkv.dtype),
            shape(lows.shape, lows.dtype),
            shape(inner.shape, inner.dtype),
            shape(qkv.shape[1:], jnp.bfloat16),
            shape(qkv.shape[1:], jnp.bfloat16),
            shape((length, width), jnp.bfloat16),
            shape((length, width), jnp.float32),
            shape((length, wide), jnp.bfloat16),
        ],
        scratch_shapes=[
            pltpu.VMEM((length, width), jnp.bfloat16),
            pltpu.VMEM((span, width), jnp.bfloat16),
            pltpu.VMEM((span, SMALL), jnp.bfloat16),
            pltpu.VMEM(qkv.shape, jnp.bfloat16),
            pltpu.VMEM((pairs, length, LANES), jnp.bfloat16),
            pltpu.VMEM((pairs, length, LANES), jnp.bfloat16),
            pltpu.VMEM((width, width), jnp.bfloat16),
            pltpu.VMEM((wide // width, width, width), jnp.bfloat16),
            pltpu.VMEM((wide, width), jnp.bfloat16),
            pltpu.VMEM((length, width), jnp.float32),
            pltpu.VMEM((length, wide), jnp.bfloat16),
            pltpu.VMEM((2, CHUNK, wide), jnp.bfloat16),
            pltpu.SemaphoreType.DMA((moves,)),
        ],
        input_output_aliases={9 + count + index: index for index in range(3)},
        compiler_params=pltpu.CompilerParams(vmem_limit_bytes=VMEM),
        cost_estimate=pl.CostEstimate(flops=60 << 30, bytes_accessed=60 << 20, transcendentals=0),
        name="forward",
    )(place, vectors, factors, near_peaks, far_peaks, weight, out_weight, up, down, *blocks, *former)


def far_kernel(place, vectors, factors, outer, slopes, up, down, middle, out_weight, qkv, mixed, aux, inner, lows, weight, *refs):
    summed, d_middle, d_mixed, kept, other, grads = refs[:6]
    outer_buf, slope_buf, up_buf, down_buf, middle_buf, out_buf, d_mixed_buf, qkv_buf, mixed_buf, aux_buf, d_buf, other_buf, low_buf, semaphores = refs[6:]
    copy = copier(semaphores)
    length, width = outer.shape
    span = length // 2
    far_base, near_base = (pl.multiple_of(place[side] * span, span) for side in (1, 2))
    far, near = pl.ds(far_base, span), pl.ds(near_base, span)
    parts = pieces_of(length, CHUNK)
    columns = pieces_of(up.shape[1], width)
    outers, downs, slants = [], [], []
    for t, column in enumerate(columns):
        downs.append(copy(down.at[column], down_buf.at[column]))
        for part in parts:
            if t == 0:
                outers.append(copy(outer.at[part], outer_buf.at[part]))
            slants.append(copy(slopes.at[part, column], slope_buf.at[part, column]))
    late = [copy(out_weight, out_buf), copy(up, up_buf), copy(middle, middle_buf)]
    attended = [copy(qkv, qkv_buf), copy(mixed, mixed_buf), copy(aux, aux_buf)]
    for t, column in enumerate(columns):
        downs[t].wait()
        for index, part in enumerate(parts):
            if t == 0:
                outers[index].wait()
            slants[t * len(parts) + index].wait()
            d_active = nt(outer_buf[part], down_buf[column])
            slope_buf[part, column] = (d_active * slope_buf[part, column].astype(jnp.float32)).astype(jnp.bfloat16)
    for ready in late:
        ready.wait()
    starts = [near_base + start for start in range(0, span, STEP)] + [far_base + start for start in range(0, span, STEP)]
    for index, start in enumerate(starts):
        rows = pl.ds(pl.multiple_of(start, STEP), STEP)
        grad = nt(slope_buf[rows], up_buf[...])
        standard, inverse = standardize(middle_buf[rows])
        d = outer_buf[rows].astype(jnp.float32) + pull_norm(grad, standard, inverse, vectors[GAIN_TWO:GAIN_TWO + 1])
        middle_buf[rows] = d
        spread(d_mixed_buf, rows, nt(d.astype(jnp.bfloat16), out_buf[...]))
        if index + 1 == span // STEP:
            passed = copy(middle_buf.at[near], d_middle.at[near])
    sent = [copy(d_mixed_buf.at[:, near], d_mixed.at[:, near])]
    weight_buf = slope_buf.at[:, :weight.shape[1]]
    ready = [copy(weight, weight_buf), copy(inner.at[far], outer_buf.at[:span]), copy(lows.at[far], low_buf)]
    passed.wait()
    for move in attended:
        move.wait()

    def store(at, first, second):
        lanes = pl.ds(pl.multiple_of(at * LANES, LANES), LANES)
        middle_buf[near, lanes] = first
        other_buf[:, lanes] = second

    @pl.loop(0, qkv_buf.shape[1] // GROUP)
    def _(step):
        attend_back_far(place, step * GROUP, GROUP, qkv_buf, mixed_buf, aux_buf, d_mixed_buf, d_buf, store)

    sent.append(copy(middle_buf.at[near], kept))
    sent.append(copy(other_buf, other))
    for move in ready:
        move.wait()
    normed, grad_buf = outer_buf.at[span:], slope_buf.at[:span, weight.shape[1]:]
    small = finish_grads(vectors, factors, d_buf, weight_buf, outer_buf.at[:span], middle_buf.at[far], normed, grad_buf)
    sent.append(copy(grad_buf, grads.at[far]))
    sum_factors(small, normed, low_buf, d_buf, None, summed)
    for move in sent:
        move.wait()


def backward_far(place, outer, slopes, up, down, middle, out_weight, qkv, mixed, aux, inner, lows, vectors, factors, weight):
    length, width = outer.shape
    span, wide, pairs = length // 2, up.shape[1], qkv.shape[1]
    shape = jax.ShapeDtypeStruct
    moves = length // CHUNK + (1 + length // CHUNK) * (wide // width) + 3 + 3 + 2 + 3 + 2 + 1
    return pl.pallas_call(
        far_kernel,
        in_specs=[pl.BlockSpec(memory_space=pltpu.SMEM)] + [pl.BlockSpec(memory_space=pltpu.VMEM)] * 2 + anywhere(12),
        out_specs=[pl.BlockSpec(memory_space=pltpu.VMEM)] + anywhere(5),
        out_shape=[
            shape((4 * RANK, width), jnp.float32),
            shape((length, width), jnp.float32),
            shape(mixed.shape, jnp.bfloat16),
            shape((span, width), jnp.float32),
            shape((span, width), jnp.float32),
            shape((length, width), jnp.bfloat16),
        ],
        scratch_shapes=[
            pltpu.VMEM((length, width), jnp.bfloat16),
            pltpu.VMEM((length, wide), jnp.bfloat16),
            pltpu.VMEM((width, wide), jnp.bfloat16),
            pltpu.VMEM((wide, width), jnp.bfloat16),
            pltpu.VMEM((length, width), jnp.float32),
            pltpu.VMEM((width, width), jnp.bfloat16),
            pltpu.VMEM(mixed.shape, jnp.bfloat16),
            pltpu.VMEM(qkv.shape, jnp.bfloat16),
            pltpu.VMEM(mixed.shape, jnp.bfloat16),
            pltpu.VMEM(mixed.shape, jnp.bfloat16),
            pltpu.VMEM((3, pairs, span, LANES), jnp.bfloat16),
            pltpu.VMEM((span, width), jnp.float32),
            pltpu.VMEM((span, SMALL), jnp.bfloat16),
            pltpu.SemaphoreType.DMA((moves,)),
        ],
        compiler_params=pltpu.CompilerParams(vmem_limit_bytes=VMEM),
        cost_estimate=pl.CostEstimate(flops=80 << 30, bytes_accessed=60 << 20, transcendentals=0),
        name="backward_far",
    )(place, vectors, factors, outer, slopes, up, down, middle, out_weight, qkv, mixed, aux, inner, lows, weight)


def swap(v, axis, steps):
    size = lax.axis_size(axis)
    return [lax.ppermute(v, axis, [(i, i ^ step) for i in range(size)]) for step in steps]


def sum_batch(v):
    size = lax.axis_size("batch")
    if size & (size - 1):
        return lax.psum(v, "batch")
    step = 1
    while step < size:
        (other,) = swap(v, "batch", [step])
        v, step = v + other, 2 * step
    return v


def whole_slots(
    tokens,
    lengths,
    norm_gain,
    norm_shift,
    joint_weight,
    query_bias,
    value_bias,
    output_weight,
    output_bias,
    second_gain,
    second_shift,
    upward_weight,
    upward_bias,
    down_weight,
    down_bias,
    query_down,
    query_up,
    value_down,
    value_up,
    cotangent,
):
    seqs_here, rows, width = tokens.shape
    ranks = lax.axis_size("blk")
    half = ranks // 2
    adapter = 32.0 / RANK

    def partner(index):
        return [(i, i ^ index) for i in range(ranks)]

    me = lax.axis_index("blk")
    side = me // half
    quarter = 2 * (1 - side) + (me % half) // (half // 2)
    place = jnp.stack((me, 1 - side, side, lengths[me], quarter, quarter ^ 1)).astype(jnp.int32)
    vectors = jnp.concatenate(
        (
            norm_gain,
            norm_shift,
            query_bias,
            jnp.zeros_like(query_bias),
            value_bias,
            output_bias,
            second_gain,
            second_shift,
            down_bias,
            upward_bias,
        )
    )
    vectors = vectors.astype(jnp.float32).reshape(-1, width)
    factors = jnp.concatenate(
        (
            jnp.pad(jnp.concatenate((query_down, value_down), axis=1).T, ((0, 2 * RANK), (0, 0))),
            jnp.pad(adapter * query_up, ((0, 3 * RANK), (0, 0))).astype(jnp.bfloat16),
            jnp.pad(adapter * value_up, ((RANK, 2 * RANK), (0, 0))).astype(jnp.bfloat16),
        )
    )
    own, *others = deal(tokens)
    far = [lax.ppermute(others[k - 1], "blk", partner(k)) for k in range(half, ranks)]
    near = [own] + [lax.ppermute(others[k - 1], "blk", partner(k)) for k in range(1, half)]
    *former, near_peaks = project(place, 2, near, vectors, factors, joint_weight)
    first, last = far[: half // 2], far[half // 2 :]
    *former, far_peaks = project(place, FIRST, first, vectors, factors, joint_weight, former)
    cotangent, _ = lax.optimization_barrier((cotangent, (near_peaks, far_peaks, last[:-1])))
    outer = lax.all_to_all(cotangent, "blk", 0, 0, tiled=True).reshape(-1, width)
    qkv, lows, inner, mixed, aux, result, middle, slopes = forward(
        place,
        last,
        former,
        near_peaks,
        far_peaks,
        vectors,
        factors,
        joint_weight,
        output_weight,
        upward_weight,
        down_weight,
    )
    result, middle, slopes, outer = lax.optimization_barrier((result, middle, slopes, outer))
    block_output = lax.all_to_all(
        result.reshape(ranks, rows, width), "blk", 0, 0, tiled=True
    )
    shared = (vectors, factors, joint_weight)
    far_factors, d_middle, d_mixed, kept, other, far_grads = backward_far(
        place,
        outer,
        slopes,
        upward_weight,
        down_weight,
        middle,
        output_weight,
        qkv,
        mixed,
        aux,
        inner,
        lows,
        *shared,
    )
    far_grads = lax.all_to_all(far_grads.reshape(ranks, rows, width), "blk", 0, 0, tiled=True)
    packed, block_output, *near_grads = backward_near(
        place,
        half,
        qkv,
        mixed,
        aux,
        d_mixed,
        kept,
        other,
        inner,
        d_middle,
        lows,
        *shared,
        far_factors,
        block_output,
    )
    near_grads = near_grads[:1] + [
        lax.ppermute(near_grads[k], "blk", partner(k)) for k in range(1, half)
    ]
    packed = sum_batch(packed)
    step = 1
    while step < ranks:
        if step == half:
            packed, near_grads = lax.optimization_barrier((packed, near_grads))
        (other,) = swap(packed, "blk", [step])
        packed, step = packed + other, 2 * step
    token_grads = gather(far_grads, near_grads, jnp.float32)
    query_down_grad, value_down_grad = packed[:RANK].T, packed[RANK : 2 * RANK].T
    query_up_grad, value_up_grad = packed[2 * RANK : 3 * RANK], packed[3 * RANK :]
    return (
        block_output,
        token_grads,
        query_down_grad,
        query_up_grad,
        value_down_grad,
        value_up_grad,
    )


def body(
    tokens,
    lengths,
    norm_gain,
    norm_shift,
    joint_weight,
    query_bias,
    value_bias,
    output_weight,
    output_bias,
    second_gain,
    second_shift,
    upward_weight,
    upward_bias,
    down_weight,
    down_bias,
    query_down,
    query_up,
    value_down,
    value_up,
    cotangent,
):
    seqs_here, rows, width = tokens.shape
    heads = width // HD
    positions = seqs_here * rows
    length_all = rows * lax.axis_size("blk")
    scale = HD ** (-0.5)
    adapter = 32.0 / RANK
    flat = tokens.reshape(positions, width).astype(jnp.float32)
    normed_full, standard, inverse = normalize(flat, norm_gain, norm_shift)
    normed = normed_full.astype(jnp.bfloat16)
    joint = jnp.dot(normed, joint_weight, preferred_element_type=jnp.float32)
    query_low = jnp.dot(normed, query_down, preferred_element_type=jnp.float32).astype(jnp.bfloat16)
    value_low = jnp.dot(normed, value_down, preferred_element_type=jnp.float32).astype(jnp.bfloat16)
    queries = (
        joint[:, :width]
        + query_bias.astype(jnp.float32)
        + adapter * jnp.dot(query_low, query_up, preferred_element_type=jnp.float32)
    ).astype(jnp.bfloat16)
    keys_here = joint[:, width : 2 * width].astype(jnp.bfloat16)
    values_here = (
        joint[:, 2 * width :]
        + value_bias.astype(jnp.float32)
        + adapter * jnp.dot(value_low, value_up, preferred_element_type=jnp.float32)
    ).astype(jnp.bfloat16)
    query_heads = queries.reshape(seqs_here, rows, heads, HD)
    key_blocks = keys_here.reshape(seqs_here, rows, width)
    value_blocks = values_here.reshape(seqs_here, rows, width)
    device = lax.axis_index("blk")
    query_place = device * rows + jnp.arange(rows, dtype=jnp.int32)
    limits = lengths[:, None, None, None]

    def visible(query_pos, key_pos):
        return (key_pos[None, None, None, :] <= query_pos[None, None, :, None]) & (
            key_pos[None, None, None, :] < limits
        )

    running = jnp.full((seqs_here, heads, rows), masked_value, jnp.float32)
    key_piece = lax.all_gather(key_blocks, "blk", axis=1, tiled=True)
    value_piece = lax.all_gather(value_blocks, "blk", axis=1, tiled=True)
    count = key_piece.shape[1]
    key_heads = key_piece.reshape(seqs_here, count, heads, HD)
    value_heads = value_piece.reshape(seqs_here, count, heads, HD)
    allowed = visible(query_place, jnp.arange(count, dtype=jnp.int32))
    scores = (
        jnp.einsum("sqhd,skhd->shqk", query_heads, key_heads, preferred_element_type=jnp.float32)
        * scale
    )
    masked = jnp.where(allowed, scores, masked_value)
    highest = jnp.maximum(running, jnp.max(masked, axis=-1))
    weights = jnp.where(allowed, jnp.exp(masked - highest[..., None]), 0.0)
    totals = jnp.sum(weights, axis=-1)
    update = jnp.einsum(
        "shqk,skhd->sqhd",
        weights.astype(jnp.bfloat16),
        value_heads,
        preferred_element_type=jnp.float32,
    )
    summed = update
    running, totals, summed = (highest, totals, summed)
    mixed_full = summed / jnp.transpose(totals, (0, 2, 1))[..., None]
    log_total = running + jnp.log(totals)
    mixed_low = mixed_full.reshape(positions, width).astype(jnp.bfloat16)
    middle = (
        flat
        + jnp.dot(mixed_low, output_weight, preferred_element_type=jnp.float32)
        + output_bias.astype(jnp.float32)
    )
    normed_two_full, standard_two, inverse_two = normalize(middle, second_gain, second_shift)
    normed_two = normed_two_full.astype(jnp.bfloat16)
    hidden = jnp.dot(
        normed_two, upward_weight, preferred_element_type=jnp.float32
    ) + upward_bias.astype(jnp.float32)
    active_full, gelu_pull = jax.vjp(partial(jax.nn.gelu, approximate=True), hidden)
    active = active_full.astype(jnp.bfloat16)
    block_output = (
        (
            middle
            + jnp.dot(active, down_weight, preferred_element_type=jnp.float32)
            + down_bias.astype(jnp.float32)
        )
        .astype(jnp.bfloat16)
        .reshape(seqs_here, rows, width)
    )
    outer = cotangent.reshape(positions, width)
    d_active = against(outer, down_weight)
    d_hidden = gelu_pull(d_active)[0].astype(jnp.bfloat16)
    d_normed_two = against(d_hidden, upward_weight)
    d_middle = outer.astype(jnp.float32) + norm_back(
        d_normed_two, standard_two, inverse_two, second_gain
    )
    d_branch = d_middle.astype(jnp.bfloat16)
    d_mixed = against(d_branch, output_weight).astype(jnp.bfloat16)
    d_mixed_heads = d_mixed.reshape(seqs_here, rows, heads, HD)
    delta = jnp.transpose(
        jnp.sum(d_mixed_heads.astype(jnp.float32) * mixed_full, axis=-1), (0, 2, 1)
    )
    key_all, value_all = (
        lax.all_gather(key_blocks, "blk", axis=1, tiled=True),
        lax.all_gather(value_blocks, "blk", axis=1, tiled=True),
    )
    key_heads_all = key_all.reshape(seqs_here, length_all, heads, HD)
    value_heads_all = value_all.reshape(seqs_here, length_all, heads, HD)
    allowed_all = visible(query_place, jnp.arange(length_all, dtype=jnp.int32))
    scores = (
        jnp.einsum(
            "sqhd,skhd->shqk", query_heads, key_heads_all, preferred_element_type=jnp.float32
        )
        * scale
    )
    probs = jnp.where(allowed_all, jnp.exp(scores - log_total[..., None]), 0.0)
    d_probs = jnp.einsum(
        "sqhd,skhd->shqk", d_mixed_heads, value_heads_all, preferred_element_type=jnp.float32
    )
    d_scores = (probs * (d_probs - delta[..., None])).astype(jnp.bfloat16)
    d_queries = (
        jnp.einsum("shqk,skhd->sqhd", d_scores, key_heads_all, preferred_element_type=jnp.float32)
        * scale
    )
    d_keys_all = (
        jnp.einsum("shqk,sqhd->kshd", d_scores, query_heads, preferred_element_type=jnp.float32)
        * scale
    )
    d_values_all = jnp.einsum(
        "shqk,sqhd->kshd",
        probs.astype(jnp.bfloat16),
        d_mixed_heads,
        preferred_element_type=jnp.float32,
    )
    stacked = jnp.stack(
        (
            d_keys_all.reshape(length_all, seqs_here, width),
            d_values_all.reshape(length_all, seqs_here, width),
        ),
        axis=2,
    )
    owned = lax.psum_scatter(
        stacked.astype(jnp.bfloat16), "blk", scatter_dimension=0, tiled=True
    ).astype(jnp.float32)
    d_keys = jnp.transpose(owned[:, :, 0], (1, 0, 2)).reshape(positions, width)
    d_values = jnp.transpose(owned[:, :, 1], (1, 0, 2)).reshape(positions, width)
    d_query_low = d_queries.reshape(positions, width).astype(jnp.bfloat16)
    d_key_low = d_keys.astype(jnp.bfloat16)
    d_value_low = d_values.astype(jnp.bfloat16)
    query_up_grad = adapter * transposed(query_low, d_query_low)
    value_up_grad = adapter * transposed(value_low, d_value_low)
    d_query_small = (adapter * against(d_query_low, query_up)).astype(jnp.bfloat16)
    d_value_small = (adapter * against(d_value_low, value_up)).astype(jnp.bfloat16)
    query_down_grad = transposed(normed, d_query_small)
    value_down_grad = transposed(normed, d_value_small)
    d_joint = jnp.concatenate((d_query_low, d_key_low, d_value_low), axis=1)
    d_normed = (
        against(d_joint, joint_weight)
        + against(d_query_small, query_down)
        + against(d_value_small, value_down)
    )
    token_grads = (d_middle + norm_back(d_normed, standard, inverse, norm_gain)).reshape(
        seqs_here, rows, width
    )
    sums = lax.psum(
        (query_down_grad, query_up_grad, value_down_grad, value_up_grad), ("batch", "blk")
    )
    return (block_output, token_grads, sums[0], sums[1], sums[2], sums[3])


def choose(tokens, *others):
    seqs, rows = tokens.shape[:2]
    ranks = lax.axis_size("blk")
    fits = seqs == ranks and ranks > 1 and not ranks & (ranks - 1)
    fits = fits and rows % LANES == 0 and (ranks // 2 * rows) % CHUNK == 0
    return (whole_slots if fits else body)(tokens, *others)


def solution(mesh):
    placed = (
        P("batch", "blk", None),
        P("batch"),
        P(),
        P(),
        P(),
        P(),
        P(),
        P(),
        P(),
        P(),
        P(),
        P(),
        P(),
        P(),
        P(),
        P(),
        P(),
        P(),
        P(),
        P("batch", "blk", None),
    )
    return jax.shard_map(
        choose,
        mesh=mesh,
        in_specs=placed,
        out_specs=(P("batch", "blk", None), P("batch", "blk", None), P(), P(), P(), P()),
        check_vma=False,
    )
```
